32 devices in a mesh: ctx: 16 (over z, y, x), head: 2 (over core).
Axes of the slice: x: 2, y: 2, z: 4, core: 2. Of those that a mesh axis runs over, the one named last changes fastest.
Arguments:
- queries: bfloat16 [512, 8192], P('ctx', 'head'), may hold values from -128 to 128
- fresh_span_keys: bfloat16 [512, 1024], P('ctx', 'head'), may hold values from -10 to 10
- fresh_span_values: bfloat16 [512, 1024], P('ctx', 'head'), may hold values from -6 to 6
- context_keys: bfloat16 [65536, 1024], P('ctx', 'head'), may hold values from -6 to 6
- context_values: bfloat16 [65536, 1024], P('ctx', 'head'), may hold values from -12 to 12
- selected: int32 [4, 12], replicated, may hold values from 0 to 15, as said below
- out_weight: bfloat16 [8192, 8192], P('head', 'ctx'), may hold values from -0.0625 to 0.0625
Outputs:
- attended: bfloat16 [512, 8192], P('head', 'ctx')
The draws below stay inside these ranges and needn't reach their ends.
Inputs may be any that keep to these rules, and one draw needn't show every extreme that they name: `selected`: each row lists 12 different cache blocks, and every row lists the newest block, 15.
All inputs are finite; a program needn't handle non-finite values.
Results may differ from the reference program's by a relative error of at most 0.01345.
Values may be sent and summed in bfloat16 or wider, within the bound.
No kernel may reach another device: no remote copies, remote signals or barrier semaphores. Data moves between devices by JAX's collectives and lax.ppermute only.
A program may use at most 192 MiB of HBM per device.

```python
import jax
import jax.numpy as jnp
from jax import lax

D = 8192
QUERY_HEADS = 64
KEY_VALUE_HEADS = 8
HEAD_SIZE = 128
GROUP_QUERIES = 8
BLOCK_TOKENS = 4096
QUERY_BLOCK_SIZE = 128
PICKED_BLOCKS = 12
SPAN_TOKENS = 512
QUERY_BLOCKS = 4
CACHE_BLOCKS = 16
CACHED_TOKENS = 65536


def span_pair(key):
    base = jax.random.fold_in(key, 7301)
    query_seed, span_seed = jax.random.split(base, 2)
    key_matrix = 1.6 * jnp.clip(jax.random.normal(span_seed, (SPAN_TOKENS, KEY_VALUE_HEADS, HEAD_SIZE), jnp.float32), -6.0, 6.0)
    query_matrix = 2.0 * jnp.clip(jax.random.normal(query_seed, (SPAN_TOKENS, KEY_VALUE_HEADS, GROUP_QUERIES, HEAD_SIZE), jnp.float32), -6.0, 6.0)
    return (query_matrix.reshape(SPAN_TOKENS, QUERY_HEADS * HEAD_SIZE), key_matrix.reshape(SPAN_TOKENS, KEY_VALUE_HEADS * HEAD_SIZE))


def draw_queries(key, part):
    return span_pair(key)[0].astype(jnp.bfloat16)


def draw_fresh_span_keys(key, part):
    return span_pair(key)[1].astype(jnp.bfloat16)


def draw_context_values(key, part):
    base = jax.random.fold_in(key, 4409)
    average_key, random_seed_key = jax.random.split(base, 2)
    block_averages = jnp.clip(jax.random.normal(average_key, (CACHE_BLOCKS, 1, KEY_VALUE_HEADS * HEAD_SIZE), jnp.float32), -4.0, 4.0)
    random_draws = jnp.clip(jax.random.normal(random_seed_key, (CACHE_BLOCKS, BLOCK_TOKENS, KEY_VALUE_HEADS * HEAD_SIZE), jnp.float32), -6.0, 6.0)
    return (block_averages + random_draws).reshape(CACHE_BLOCKS * BLOCK_TOKENS, KEY_VALUE_HEADS * HEAD_SIZE).astype(jnp.bfloat16)


def draw_selected(key, part):
    score_key = jax.random.fold_in(key, 9127)
    base = jax.random.randint(score_key, (QUERY_BLOCKS, CACHE_BLOCKS), 0, 1 << 20, dtype=jnp.int32)
    block_ids = jnp.arange(CACHE_BLOCKS, dtype=jnp.int32)
    ranked = base * CACHE_BLOCKS + block_ids[None, :]
    ranked = jnp.where(block_ids[None, :] == CACHE_BLOCKS - 1, jnp.int32(1 << 30), ranked)
    return lax.top_k(ranked, PICKED_BLOCKS)[1].astype(jnp.int32)


def block_levels(own_key, dims, cuts, low, largest):
    factor_of, own = 1.0, jax.random.fold_in(own_key, 6)
    for axis_at, blocks in cuts:
        draws = jnp.exp(jax.random.uniform(jax.random.fold_in(own, axis_at), (blocks,), jnp.float32, low / len(cuts), largest / len(cuts)))
        factor_of = factor_of * jnp.repeat(draws, dims[axis_at] // blocks).reshape([-1 if axis == axis_at else 1 for axis in range(len(dims))])
    return factor_of


def noise(rng, shape, spread, reach, pieces=(), held_as=jnp.bfloat16):
    level = block_levels(rng, shape, pieces, -0.22, 0.18) if pieces else 1.0
    result = jax.random.normal(rng, shape, jnp.float32) * spread * level
    return jnp.minimum(jnp.maximum(result, -reach), reach).astype(held_as)


def setup_inputs(seed: int = 0) -> dict:
    seeds = jax.random.split(jax.random.key(seed), 8)
    queries = draw_queries(jax.random.fold_in(seeds[7], 71), 0)
    fresh_span_keys = draw_fresh_span_keys(jax.random.fold_in(seeds[7], 71), 0)
    fresh_span_values = noise(seeds[2], (SPAN_TOKENS, KEY_VALUE_HEADS * HEAD_SIZE), 1.0, 6.0, ((0, 16), (1, 2)))
    context_keys = noise(seeds[3], (CACHED_TOKENS, KEY_VALUE_HEADS * HEAD_SIZE), 1.0, 6.0, ((0, 16), (1, 2)))
    context_values = draw_context_values(jax.random.fold_in(seeds[7], 71), 0)
    selected = draw_selected(jax.random.fold_in(seeds[7], 71), 0)
    out_weight = noise(seeds[6], (QUERY_HEADS * HEAD_SIZE, D), (QUERY_HEADS * HEAD_SIZE) ** -0.5, 0.0625, ((0, 2), (1, 16)))
    return {"queries": queries, "fresh_span_keys": fresh_span_keys, "fresh_span_values": fresh_span_values, "context_keys": context_keys, "context_values": context_values, "selected": selected, "out_weight": out_weight}


def reference(queries, fresh_span_keys, fresh_span_values, context_keys, context_values, selected, out_weight):
    score_scale = HEAD_SIZE ** -0.5
    keys_by_block = context_keys.reshape(CACHE_BLOCKS, BLOCK_TOKENS, KEY_VALUE_HEADS, HEAD_SIZE)
    values_by_block = context_values.reshape(CACHE_BLOCKS, BLOCK_TOKENS, KEY_VALUE_HEADS, HEAD_SIZE)
    keys_of_span = fresh_span_keys.reshape(SPAN_TOKENS, KEY_VALUE_HEADS, HEAD_SIZE)
    values_of_span = fresh_span_values.reshape(SPAN_TOKENS, KEY_VALUE_HEADS, HEAD_SIZE)
    query_groups = queries.reshape(QUERY_BLOCKS, QUERY_BLOCK_SIZE, KEY_VALUE_HEADS, GROUP_QUERIES, HEAD_SIZE)
    key_pos = jnp.arange(SPAN_TOKENS, dtype=jnp.int32)

    def one_block(block_index):
        picked_blocks = lax.dynamic_index_in_dim(selected, block_index, 0, keepdims=False)
        joined_keys = jnp.concatenate([jnp.take(keys_by_block, picked_blocks, axis=0).reshape(PICKED_BLOCKS * BLOCK_TOKENS, KEY_VALUE_HEADS, HEAD_SIZE), keys_of_span], axis=0)
        joined_values = jnp.concatenate([jnp.take(values_by_block, picked_blocks, axis=0).reshape(PICKED_BLOCKS * BLOCK_TOKENS, KEY_VALUE_HEADS, HEAD_SIZE), values_of_span], axis=0)
        row_pos = block_index * QUERY_BLOCK_SIZE + jnp.arange(QUERY_BLOCK_SIZE, dtype=jnp.int32)
        causal = key_pos[None, :] <= row_pos[:, None]
        valid_mask = jnp.concatenate([jnp.ones((QUERY_BLOCK_SIZE, PICKED_BLOCKS * BLOCK_TOKENS), jnp.bool_), causal], axis=1)
        block_queries = lax.dynamic_index_in_dim(query_groups, block_index, 0, keepdims=False)

        def single_head(head_index):
            query_matrix = lax.dynamic_index_in_dim(block_queries, head_index, 1, keepdims=False).reshape(QUERY_BLOCK_SIZE * GROUP_QUERIES, HEAD_SIZE)
            head_keys = lax.dynamic_index_in_dim(joined_keys, head_index, 1, keepdims=False)
            head_values = lax.dynamic_index_in_dim(joined_values, head_index, 1, keepdims=False)
            scores = lax.dot_general(query_matrix, head_keys, (((1,), (1,)), ((), ())), preferred_element_type=jnp.float32) * score_scale
            scores = scores.reshape(QUERY_BLOCK_SIZE, GROUP_QUERIES, -1)
            scores = jnp.where(valid_mask[:, None, :], scores, -jnp.inf)
            weights = jnp.exp(scores - jnp.max(scores, axis=-1, keepdims=True))
            denominator = jnp.sum(weights, axis=-1)
            summed = jnp.dot(weights.astype(jnp.bfloat16).reshape(QUERY_BLOCK_SIZE * GROUP_QUERIES, -1), head_values, preferred_element_type=jnp.float32)
            return summed.reshape(QUERY_BLOCK_SIZE, GROUP_QUERIES, HEAD_SIZE) / denominator[..., None]

        output_per_head = lax.map(single_head, jnp.arange(KEY_VALUE_HEADS, dtype=jnp.int32))
        return jnp.transpose(output_per_head, (1, 0, 2, 3)).reshape(QUERY_BLOCK_SIZE, QUERY_HEADS * HEAD_SIZE)

    attention = lax.map(one_block, jnp.arange(QUERY_BLOCKS, dtype=jnp.int32)).reshape(SPAN_TOKENS, QUERY_HEADS * HEAD_SIZE).astype(jnp.bfloat16)
    return jnp.dot(attention, out_weight, preferred_element_type=jnp.float32).astype(jnp.bfloat16)
```

```python
import functools

import jax
import jax.numpy as jnp
import numpy as np
from jax import lax
from jax.experimental import pallas as pl
from jax.experimental.pallas import tpu as pltpu
from jax.sharding import PartitionSpec as P

HEAD_SIZE = 128
GROUP_QUERIES = 8
LANES = 128
LOG2_SCALE = float(HEAD_SIZE**-0.5 * np.log2(np.e))
MASKED = -1e30
LOWEST = -1e20
VMEM_LIMIT = 56 * 1024 * 1024

BF16, F32 = jnp.bfloat16, jnp.float32


def fold_lanes(op, x):
    parts = [x[:, i : i + LANES] for i in range(0, x.shape[1], LANES)]
    while len(parts) > 1:
        parts = [op(*parts[i : i + 2]) if i + 1 < len(parts) else parts[i] for i in range(0, len(parts), 2)]
    return parts[0]


def attend_kernel(
    info, *refs, plane, blocks, rows, group_step, key_chunk, waits
):
    q_refs, refs = refs[:plane], refs[plane:]
    k_ref, v_ref, ks_ref, vs_ref = refs[:4]
    refs = refs[4 + waits :]
    o_refs, refs = refs[:plane], refs[plane:]
    score_ref, peak_ref, aux_ref, pos_ref, ks_pad, vs_pad = refs
    me, my_plane, wanted = info[0], info[1], info[2]
    keys = k_ref.shape[0]
    block_rows = plane * rows
    tile_rows = group_step * block_rows
    steps = GROUP_QUERIES // group_step
    chunks = keys // key_chunk

    ks_pad[...] = jnp.zeros_like(ks_pad)
    vs_pad[...] = jnp.zeros_like(vs_pad)
    ks_pad[0:rows, :] = ks_ref[...]
    vs_pad[0:rows, :] = vs_ref[...]
    row = lax.broadcasted_iota(jnp.int32, (tile_rows, LANES), 0)
    col = lax.broadcasted_iota(jnp.int32, (tile_rows, LANES), 1)
    piece = lax.rem(lax.div(row, rows), plane)
    pos_ref[...] = jnp.where(
        col < rows, (piece ^ my_plane) * rows + lax.rem(row, rows) - me * rows - col, -(1 << 30)
    )
    lane = lax.broadcasted_iota(jnp.int32, (block_rows, LANES), 1)

    def place(tile):
        return info[3 + lax.div(tile, steps)], lax.rem(tile, steps) * group_step

    def load_queries(tile):
        slot, group = place(tile)
        parts = []
        for i in range(group_step):
            cols = pl.ds(pl.multiple_of((group + i) * HEAD_SIZE, HEAD_SIZE), HEAD_SIZE)
            parts += [q[slot, :, cols] for q in q_refs]
        return jnp.concatenate(parts, axis=0)

    def dot_keys(q, k):
        return lax.dot_general(q, k, (((1,), (1,)), ((), ())), preferred_element_type=F32)

    def span_scores(q, tile):
        slot, _ = place(tile)
        start = info[3 + blocks + slot] * block_rows
        return jnp.where(pos_ref[...] + start >= 0, dot_keys(q, ks_pad[...]), MASKED)

    def shift_of(peak):
        top = jnp.max(peak, axis=1, keepdims=True) * LOG2_SCALE
        return jnp.maximum(top, LOWEST).astype(BF16).astype(F32)

    def finish(tile, shift, total, acc):
        slot, group = place(tile)
        total = jnp.sum(total, axis=1, keepdims=True)
        high = total.astype(BF16).astype(F32)
        low = total - high
        aux = jnp.where(group == 0, 0.0, aux_ref[...])
        for i in range(group_step):
            cols = pl.ds(pl.multiple_of((group + i) * HEAD_SIZE, HEAD_SIZE), HEAD_SIZE)
            part = slice(i * block_rows, (i + 1) * block_rows)
            aux = jnp.where(lane == group + i, shift[part], aux)
            aux = jnp.where(lane == group + i + GROUP_QUERIES, high[part], aux)
            aux = jnp.where(lane == group + i + 2 * GROUP_QUERIES, low[part], aux)
            for b, o in enumerate(o_refs):
                start = i * block_rows + b * rows
                o[slot, :, cols] = acc[start : start + rows].astype(BF16)
        aux_ref[...] = aux
        for b, o in enumerate(o_refs):
            o[slot, :, GROUP_QUERIES * HEAD_SIZE :] = aux[b * rows : (b + 1) * rows].astype(BF16)

    def step(now, later):
        if now is not None:
            here = lax.rem(now, 2)
            shift = peak_ref[here][:, 0:1]
            wide_shift = jnp.broadcast_to(shift, (tile_rows, LANES))
            weights = jnp.exp2(score_ref[here, :, keys:] * LOG2_SCALE - wide_shift)
            total = weights
            acc = jnp.dot(weights.astype(BF16), vs_pad[...], preferred_element_type=F32)
        if later is not None:
            there = lax.rem(later, 2)
            q = load_queries(later)
            scores = span_scores(q, later)
            score_ref[there, :, keys:] = scores
            peak = scores
        for j in range(chunks):
            part = slice(j * key_chunk, (j + 1) * key_chunk)
            if later is not None:
                scores = dot_keys(q, k_ref[part])
                score_ref[there, :, part] = scores
                peak = jnp.maximum(peak, fold_lanes(jnp.maximum, scores))
            if now is not None:
                weights = jnp.exp2(score_ref[here, :, part] * LOG2_SCALE - shift)
                total = total + fold_lanes(jnp.add, weights)
                acc = acc + jnp.dot(weights.astype(BF16), v_ref[part], preferred_element_type=F32)
        if later is not None:
            peak_ref[there] = jnp.broadcast_to(shift_of(peak), (tile_rows, LANES))
        if now is not None:
            finish(now, shift, total, acc)

    count = wanted * steps

    @pl.when(count > 0)
    def _():
        step(None, jnp.int32(0))

        def body(t, _):
            step(t, t + 1)
            return 0

        lax.fori_loop(0, count - 1, body, 0)
        step(count - 1, None)

    def span_only(t, _):
        scores = span_scores(load_queries(t), t)
        shift = shift_of(scores)
        weights = jnp.exp2(scores * LOG2_SCALE - shift)
        acc = jnp.dot(weights.astype(BF16), vs_pad[...], preferred_element_type=F32)
        finish(t, shift, weights, acc)
        return 0

    lax.fori_loop(count, blocks * steps, span_only, 0)


def attend_head(info, q_pieces, keys, values, span_keys, span_values, head, after):
    plane = len(q_pieces)
    blocks, rows, cols = q_pieces[0].shape
    key_count = keys.shape[0]
    group_step = 2
    tile_rows = group_step * plane * rows
    out_cols = cols + LANES
    vmem = pltpu.MemorySpace.VMEM
    whole = pl.BlockSpec((blocks, rows, cols), lambda i, s: (0, 0, 0))
    whole_out = pl.BlockSpec((blocks, rows, out_cols), lambda i, s: (0, 0, 0))
    head_block = pl.BlockSpec((key_count, HEAD_SIZE), lambda i, s: (0, head))
    span_block = pl.BlockSpec((rows, HEAD_SIZE), lambda i, s: (0, head))
    scored = blocks * plane * rows * GROUP_QUERIES * key_count
    return pl.pallas_call(
        functools.partial(
            attend_kernel,
            plane=plane,
            blocks=blocks,
            rows=rows,
            group_step=group_step,
            key_chunk=min(key_count, 512),
            waits=len(after),
        ),
        grid_spec=pltpu.PrefetchScalarGridSpec(
            num_scalar_prefetch=1,
            grid=(1,),
            in_specs=[whole] * plane
            + [head_block, head_block, span_block, span_block]
            + [pl.BlockSpec(memory_space=pl.ANY)] * len(after),
            out_specs=[whole_out] * plane,
            scratch_shapes=[
                vmem((2, tile_rows, key_count + LANES), F32),
                vmem((2, tile_rows, LANES), F32),
                vmem((plane * rows, LANES), F32),
                vmem((tile_rows, LANES), jnp.int32),
                vmem((LANES, HEAD_SIZE), BF16),
                vmem((LANES, HEAD_SIZE), BF16),
            ],
        ),
        out_shape=[jax.ShapeDtypeStruct((blocks, rows, out_cols), BF16)] * plane,
        compiler_params=pltpu.CompilerParams(vmem_limit_bytes=VMEM_LIMIT),
        cost_estimate=pl.CostEstimate(
            flops=8 * scored * HEAD_SIZE,
            bytes_accessed=4 * key_count * HEAD_SIZE + 4 * blocks * plane * rows * cols,
            transcendentals=scored,
        ),
        name="attend",
    )(info, *q_pieces, keys, values, span_keys, span_values, *after)


def combine(parts):
    width = GROUP_QUERIES * HEAD_SIZE
    aux = [p[:, width:].astype(F32) for p in parts]
    top = functools.reduce(jnp.maximum, aux)
    factors = [jnp.exp2(jnp.minimum(a - top, 0.0)) for a in aux]
    sums = [
        pltpu.roll(a, LANES - GROUP_QUERIES, 1) + pltpu.roll(a, LANES - 2 * GROUP_QUERIES, 1) for a in aux
    ]
    total = sum(f * s for f, s in zip(factors, sums))
    heads = []
    for g in range(GROUP_QUERIES):
        cols = slice(g * HEAD_SIZE, (g + 1) * HEAD_SIZE)
        heads.append(sum(f[:, g : g + 1] * p[:, cols].astype(F32) for f, p in zip(factors, parts)))
    return heads, top, total


def merge_kernel(*refs, count, waits):
    ins, outs = refs[:count], refs[count + waits :]
    for a, out in enumerate(outs):
        heads, top, total = combine([p[a] for p in ins])
        for g, x in enumerate(heads):
            out[:, g * HEAD_SIZE : (g + 1) * HEAD_SIZE] = x.astype(BF16)
        lane = lax.broadcasted_iota(jnp.int32, top.shape, 1)
        high = total.astype(BF16).astype(F32)
        aux = jnp.where(
            lane < GROUP_QUERIES,
            top,
            jnp.where(
                lane < 2 * GROUP_QUERIES,
                pltpu.roll(high, GROUP_QUERIES, 1),
                pltpu.roll(total - high, 2 * GROUP_QUERIES, 1),
            ),
        )
        aux = jnp.where(lane < 3 * GROUP_QUERIES, aux, 0.0)
        out[:, GROUP_QUERIES * HEAD_SIZE :] = aux.astype(BF16)


def normalize_kernel(*refs, count):
    ins, out = refs[:count], refs[-1]
    heads, _, total = combine([p[...] for p in ins])
    for g, x in enumerate(heads):
        out[:, g * HEAD_SIZE : (g + 1) * HEAD_SIZE] = (x / total[:, g : g + 1]).astype(BF16)


def waiting_specs(pieces, after):
    whole = pl.BlockSpec(memory_space=pltpu.MemorySpace.VMEM)
    return [whole] * len(pieces) + [pl.BlockSpec(memory_space=pl.ANY)] * len(after)


def merge_pieces(pieces, after):
    blocks, rows, cols = pieces[0].shape
    size = blocks * rows * cols
    return pl.pallas_call(
        functools.partial(merge_kernel, count=len(pieces), waits=len(after)),
        in_specs=waiting_specs(pieces, after),
        out_shape=[jax.ShapeDtypeStruct((rows, cols), BF16)] * blocks,
        compiler_params=pltpu.CompilerParams(vmem_limit_bytes=VMEM_LIMIT),
        cost_estimate=pl.CostEstimate(
            flops=2 * size * len(pieces), bytes_accessed=2 * size * (len(pieces) + 1), transcendentals=0
        ),
        name="merge",
    )(*pieces, *after)


def normalize_pieces(pieces, after):
    rows, cols = pieces[0].shape
    size = rows * cols
    return pl.pallas_call(
        functools.partial(normalize_kernel, count=len(pieces)),
        in_specs=waiting_specs(pieces, after),
        out_shape=jax.ShapeDtypeStruct((rows, cols - LANES), BF16),
        compiler_params=pltpu.CompilerParams(vmem_limit_bytes=VMEM_LIMIT),
        cost_estimate=pl.CostEstimate(
            flops=2 * size * len(pieces), bytes_accessed=2 * size * (len(pieces) + 1), transcendentals=0
        ),
        name="normalize",
    )(*pieces, *after)


def project_kernel(info, *refs, plane, blocks, rows, heads):
    ins, w_ref, out = refs[: plane * heads], refs[-2], refs[-1]
    width = GROUP_QUERIES * HEAD_SIZE
    for b in range(plane):
        acc = None
        for h in range(heads):
            x = ins[h * plane + b][...].reshape(blocks * rows, width)
            y = jnp.dot(x, w_ref[h * width : (h + 1) * width], preferred_element_type=F32)
            acc = y if acc is None else acc + y
        for a in range(blocks):
            out[info[3 + blocks + a], b ^ info[1]] = acc[a * rows : (a + 1) * rows].astype(BF16)


def project(info, gathered, weight):
    heads, plane = len(gathered), len(gathered[0])
    blocks, rows, _ = gathered[0][0].shape
    vmem = pltpu.MemorySpace.VMEM
    span = plane * blocks * rows
    return pl.pallas_call(
        functools.partial(project_kernel, plane=plane, blocks=blocks, rows=rows, heads=heads),
        in_specs=[pl.BlockSpec(memory_space=pltpu.MemorySpace.SMEM)]
        + [pl.BlockSpec(memory_space=vmem)] * (heads * plane + 1),
        out_shape=jax.ShapeDtypeStruct((blocks, plane, rows, weight.shape[1]), BF16),
        compiler_params=pltpu.CompilerParams(vmem_limit_bytes=VMEM_LIMIT),
        cost_estimate=pl.CostEstimate(
            flops=2 * span * weight.size, bytes_accessed=2 * (weight.size + span * weight.shape[0]), transcendentals=0
        ),
        name="project",
    )(info, *[x for per_head in gathered for x in per_head], weight)


def exchange(x, axis, distance):
    count = lax.axis_size(axis)
    return lax.ppermute(x, axis, [(i, i ^ distance) for i in range(count)])


def local(queries, span_keys, span_values, context_keys, context_values, selected, out_weight):
    ctx_count, me = lax.axis_size("ctx"), lax.axis_index("ctx")
    head_count, my_head = lax.axis_size("head"), lax.axis_index("head")
    blocks = selected.shape[0]
    plane = ctx_count // blocks
    rows = queries.shape[0]
    heads = context_keys.shape[1] // HEAD_SIZE
    width = GROUP_QUERIES * HEAD_SIZE

    slot_block = lax.div(me, plane) ^ jnp.arange(blocks, dtype=jnp.int32)
    wanted = jnp.any(selected == me, axis=1)[slot_block]
    order = jnp.argsort(jnp.logical_not(wanted), stable=True).astype(jnp.int32)
    info = jnp.concatenate(
        [
            jnp.stack([me, lax.rem(me, plane), jnp.sum(wanted)]).astype(jnp.int32),
            order,
            slot_block.astype(jnp.int32),
        ]
    )

    def stack_blocks(x):
        return jnp.stack([x] + [exchange(x, "ctx", a * plane) for a in range(1, blocks)])

    def gather_plane(stack):
        return [stack] + [exchange(stack, "ctx", b) for b in range(1, plane)]

    def head_queries(h):
        return queries[:, h * width : (h + 1) * width]

    first = stack_blocks(head_queries(0))
    stacks, pieces = [first], [gather_plane(first)]
    for h in range(1, heads):
        held, _ = lax.optimization_barrier((head_queries(h), stacks[h - 1]))
        stacks.append(stack_blocks(held))
    for h in range(1, heads):
        pieces.append(gather_plane(stacks[h]))

    attended, merged, rows_of = [], [], []

    def merge(h, after):
        own = attended[h]
        parts = [own[0]] + [exchange(own[b], "ctx", b) for b in range(1, plane)]
        merged.append(merge_pieces(parts, after))

    def normalize(h, after):
        own = merged[h]
        parts = [own[0]] + [exchange(own[a], "ctx", a * plane) for a in range(1, blocks)]
        rows_of.append(normalize_pieces(parts, after))

    for h in range(heads):
        after = stacks[1:] if h == 0 else []
        if h >= 3:
            normalize(h - 3, [attended[h - 1][0]])
            after.append(rows_of[h - 3])
        if h >= 2:
            merge(h - 2, [attended[h - 1][0]])
            after.append(merged[h - 2][0])
        attended.append(
            attend_head(info, pieces[h], context_keys, context_values, span_keys, span_values, h, after)
        )
    last = [attended[-1][0]]
    for h in range(heads):
        if h >= len(merged):
            merge(h, last)
        if h >= len(rows_of):
            normalize(h, last)
    gathered = [gather_plane(stack_blocks(r)) for r in rows_of]

    partial_out = project(info, gathered, out_weight).reshape(ctx_count * rows, -1)
    share = partial_out.shape[0] // head_count
    total = lax.dynamic_slice_in_dim(partial_out, my_head * share, share, 0).astype(F32)
    for d in range(1, head_count):
        other = lax.dynamic_slice_in_dim(partial_out, (my_head ^ d) * share, share, 0)
        total = total + exchange(other, "head", d).astype(F32)
    return total.astype(BF16)


def solution(mesh):
    return jax.shard_map(
        local,
        mesh=mesh,
        in_specs=(
            P("ctx", "head"),
            P("ctx", "head"),
            P("ctx", "head"),
            P("ctx", "head"),
            P("ctx", "head"),
            P(),
            P("head", "ctx"),
        ),
        out_specs=P("head", "ctx"),
        check_vma=False,
    )
```

```python
import functools

import jax
import jax.numpy as jnp
import numpy as np
from jax import lax
from jax.experimental import pallas as pl
from jax.experimental.pallas import tpu as pltpu
from jax.sharding import PartitionSpec as P

HEAD_SIZE = 128
GROUP_QUERIES = 8
LANES = 128
LOG2_SCALE = float(HEAD_SIZE**-0.5 * np.log2(np.e))
MASKED = -1e30
LOWEST = -1e20
VMEM_LIMIT = 56 * 1024 * 1024

BF16, F32 = jnp.bfloat16, jnp.float32


def fold_lanes(op, x):
    parts = [x[:, i : i + LANES] for i in range(0, x.shape[1], LANES)]
    while len(parts) > 1:
        parts = [op(*parts[i : i + 2]) if i + 1 < len(parts) else parts[i] for i in range(0, len(parts), 2)]
    return parts[0]


def attend_kernel(info, *refs, plane, blocks, rows, group_step, key_chunk, pieces, waits):
    q_refs, refs = refs[:pieces], refs[pieces:]
    kt_ref, v_ref, ks_ref, vs_ref = refs[:4]
    refs = refs[4 + waits :]
    o_refs, refs = refs[:plane], refs[plane:]
    score_refs, refs = refs[:2], refs[2:]
    weight_refs, refs = refs[:2], refs[2:]
    shift_refs, refs = refs[:2], refs[2:]
    aux_ref, pos_ref, ks_pad, vs_pad = refs
    me, my_plane, wanted = info[0], info[1], info[2]
    keys = v_ref.shape[0]
    block_rows = plane * rows
    tile_rows = group_step * block_rows
    steps = GROUP_QUERIES // group_step
    chunks = keys // key_chunk
    strip = min(tile_rows, 64)

    ks_pad[...] = jnp.zeros_like(ks_pad)
    vs_pad[...] = jnp.zeros_like(vs_pad)
    ks_pad[0:rows, :] = ks_ref[...]
    vs_pad[0:rows, :] = vs_ref[...]
    row = lax.broadcasted_iota(jnp.int32, (tile_rows, LANES), 0)
    col = lax.broadcasted_iota(jnp.int32, (tile_rows, LANES), 1)
    piece = lax.rem(lax.div(row, rows), plane)
    pos_ref[...] = jnp.where(
        col < rows, (piece ^ my_plane) * rows + lax.rem(row, rows) - me * rows - col, -(1 << 30)
    )
    lane = lax.broadcasted_iota(jnp.int32, (block_rows, LANES), 1)

    def place(tile):
        return info[3 + lax.div(tile, steps)], lax.rem(tile, steps) * group_step

    def load_queries(tile):
        slot, group = place(tile)
        block = info[3 + blocks + slot]
        parts = []
        for i in range(group_step):
            cols = pl.ds(pl.multiple_of((group + i) * HEAD_SIZE, HEAD_SIZE), HEAD_SIZE)
            for b in range(plane):
                parts.append(q_refs[b][slot, :, cols] if pieces > 1 else q_refs[0][block, b ^ my_plane, :, cols])
        return jnp.concatenate(parts, axis=0)

    def span_scores(q, tile):
        slot, _ = place(tile)
        start = info[3 + blocks + slot] * block_rows
        scores = lax.dot_general(q, ks_pad[...], (((1,), (1,)), ((), ())), preferred_element_type=F32)
        return jnp.where(pos_ref[...] + start >= 0, scores, MASKED)

    def shift_of(peak):
        top = jnp.max(peak, axis=1, keepdims=True) * LOG2_SCALE
        return jnp.broadcast_to(jnp.maximum(top, LOWEST).astype(BF16).astype(F32), (tile_rows, LANES))

    def finish(tile, shift, total, acc):
        slot, group = place(tile)
        total = jnp.sum(total, axis=1, keepdims=True)
        high = total.astype(BF16).astype(F32)
        low = total - high
        aux = jnp.where(group == 0, 0.0, aux_ref[...])
        for i in range(group_step):
            cols = pl.ds(pl.multiple_of((group + i) * HEAD_SIZE, HEAD_SIZE), HEAD_SIZE)
            part = slice(i * block_rows, (i + 1) * block_rows)
            aux = jnp.where(lane == group + i, shift[part], aux)
            aux = jnp.where(lane == group + i + GROUP_QUERIES, high[part], aux)
            aux = jnp.where(lane == group + i + 2 * GROUP_QUERIES, low[part], aux)
            for b, o in enumerate(o_refs):
                start = i * block_rows + b * rows
                o[slot, :, cols] = acc[start : start + rows].astype(BF16)
        aux_ref[...] = aux
        for b, o in enumerate(o_refs):
            o[slot, :, GROUP_QUERIES * HEAD_SIZE :] = aux[b * rows : (b + 1) * rows].astype(BF16)

    def score_span(tile, side):
        q = load_queries(tile)
        scores = span_scores(q, tile)
        score_refs[side][:, keys:] = scores
        return q, scores

    def score_chunk(q, peak, j, side):
        part = slice(j * key_chunk, (j + 1) * key_chunk)
        scores = jnp.dot(q, kt_ref[:, part], preferred_element_type=F32)
        score_refs[side][:, part] = scores
        return jnp.maximum(peak, fold_lanes(jnp.maximum, scores))

    def weigh_chunk(totals, j, side):
        score_ref, shift_ref, weight_ref = score_refs[side], shift_refs[side], weight_refs[j % 2]
        for n, r in enumerate(range(0, tile_rows, strip)):
            part = slice(r, r + strip)
            shift = shift_ref[part]
            for c in range(0, key_chunk, LANES):
                start = j * key_chunk + c
                weights = jnp.exp2(score_ref[part, start : start + LANES] * LOG2_SCALE - shift)
                totals[n] = totals[n] + weights
                weight_ref[part, c : c + LANES] = weights.astype(BF16)

    def apply_chunk(acc, j):
        values = v_ref[j * key_chunk : (j + 1) * key_chunk]
        return acc + jnp.dot(weight_refs[j % 2][...], values, preferred_element_type=F32)

    def step(now, later, side):
        q, peak = score_span(later, 1 - side)
        weights = jnp.exp2(score_refs[side][:, keys:] * LOG2_SCALE - shift_refs[side][...])
        acc = jnp.dot(weights.astype(BF16), vs_pad[...], preferred_element_type=F32)
        totals = [weights[r : r + strip] for r in range(0, tile_rows, strip)]
        for j in range(chunks):
            peak = score_chunk(q, peak, j, 1 - side)
            weigh_chunk(totals, j, side)
            if j > 0:
                acc = apply_chunk(acc, j - 1)
        acc = apply_chunk(acc, chunks - 1)
        shift_refs[1 - side][...] = shift_of(peak)
        finish(now, shift_refs[side][...], jnp.concatenate(totals, axis=0), acc)

    count = wanted * steps

    @pl.when(count > 0)
    def _():
        q, peak = score_span(jnp.int32(0), 0)
        for j in range(chunks):
            peak = score_chunk(q, peak, j, 0)
        shift_refs[0][...] = shift_of(peak)

        def body(i, _):
            step(2 * i, 2 * i + 1, 0)
            step(2 * i + 1, jnp.minimum(2 * i + 2, count - 1), 1)
            return 0

        lax.fori_loop(0, lax.div(count, 2), body, 0)

    def span_only(t, _):
        scores = span_scores(load_queries(t), t)
        shift = shift_of(scores)
        weights = jnp.exp2(scores * LOG2_SCALE - shift)
        acc = jnp.dot(weights.astype(BF16), vs_pad[...], preferred_element_type=F32)
        finish(t, shift, weights, acc)
        return 0

    lax.fori_loop(count, blocks * steps, span_only, 0)


def attend_head(info, q_arrays, q_head, keys_t, values, span_keys, span_values, head, after):
    shape = q_arrays[0].shape
    blocks, rows = shape[0], shape[-2]
    plane = len(q_arrays) if len(q_arrays) > 1 else shape[1]
    cols = GROUP_QUERIES * HEAD_SIZE
    key_count = values.shape[0]
    group_step = 2
    tile_rows = group_step * plane * rows
    key_chunk = min(key_count, 512)
    out_cols = cols + LANES
    vmem = pltpu.MemorySpace.VMEM
    lead = (0,) * (len(shape) - 1)
    whole = pl.BlockSpec((*shape[:-1], cols), lambda i, s: (*lead, q_head))
    whole_out = pl.BlockSpec((blocks, rows, out_cols), lambda i, s: (0, 0, 0))
    span_block = pl.BlockSpec((rows, HEAD_SIZE), lambda i, s: (0, head))
    scored = blocks * plane * rows * GROUP_QUERIES * key_count
    return pl.pallas_call(
        functools.partial(
            attend_kernel,
            plane=plane,
            blocks=blocks,
            rows=rows,
            group_step=group_step,
            key_chunk=key_chunk,
            pieces=len(q_arrays),
            waits=len(after),
        ),
        grid_spec=pltpu.PrefetchScalarGridSpec(
            num_scalar_prefetch=1,
            grid=(1,),
            in_specs=[whole] * len(q_arrays)
            + [
                pl.BlockSpec((HEAD_SIZE, key_count), lambda i, s: (head, 0)),
                pl.BlockSpec((key_count, HEAD_SIZE), lambda i, s: (0, head)),
                span_block,
                span_block,
            ]
            + [pl.BlockSpec(memory_space=pl.ANY)] * len(after),
            out_specs=[whole_out] * plane,
            scratch_shapes=[vmem((tile_rows, key_count + LANES), F32)] * 2
            + [vmem((tile_rows, key_chunk), BF16)] * 2
            + [vmem((tile_rows, LANES), F32)] * 2
            + [
                vmem((plane * rows, LANES), F32),
                vmem((tile_rows, LANES), jnp.int32),
                vmem((LANES, HEAD_SIZE), BF16),
                vmem((LANES, HEAD_SIZE), BF16),
            ],
        ),
        out_shape=[jax.ShapeDtypeStruct((blocks, rows, out_cols), BF16)] * plane,
        compiler_params=pltpu.CompilerParams(vmem_limit_bytes=VMEM_LIMIT),
        cost_estimate=pl.CostEstimate(
            flops=8 * scored * HEAD_SIZE,
            bytes_accessed=4 * key_count * HEAD_SIZE + 4 * blocks * plane * rows * cols,
            transcendentals=scored,
        ),
        name="attend",
    )(info, *q_arrays, keys_t, values, span_keys, span_values, *after)


def combine(parts):
    width = GROUP_QUERIES * HEAD_SIZE
    aux = [p[:, width:].astype(F32) for p in parts]
    top = functools.reduce(jnp.maximum, aux)
    factors = [jnp.exp2(jnp.minimum(a - top, 0.0)) for a in aux]
    sums = [
        pltpu.roll(a, LANES - GROUP_QUERIES, 1) + pltpu.roll(a, LANES - 2 * GROUP_QUERIES, 1) for a in aux
    ]
    total = sum(f * s for f, s in zip(factors, sums))
    heads = []
    for g in range(GROUP_QUERIES):
        cols = slice(g * HEAD_SIZE, (g + 1) * HEAD_SIZE)
        heads.append(sum(f[:, g : g + 1] * p[:, cols].astype(F32) for f, p in zip(factors, parts)))
    return heads, top, total


def merge_kernel(*refs, count, waits):
    ins, outs = refs[:count], refs[count + waits :]
    for a, out in enumerate(outs):
        heads, top, total = combine([p[a] for p in ins])
        for g, x in enumerate(heads):
            out[:, g * HEAD_SIZE : (g + 1) * HEAD_SIZE] = x.astype(BF16)
        lane = lax.broadcasted_iota(jnp.int32, top.shape, 1)
        high = total.astype(BF16).astype(F32)
        aux = jnp.where(
            lane < GROUP_QUERIES,
            top,
            jnp.where(
                lane < 2 * GROUP_QUERIES,
                pltpu.roll(high, GROUP_QUERIES, 1),
                pltpu.roll(total - high, 2 * GROUP_QUERIES, 1),
            ),
        )
        aux = jnp.where(lane < 3 * GROUP_QUERIES, aux, 0.0)
        out[:, GROUP_QUERIES * HEAD_SIZE :] = aux.astype(BF16)


def normalize_kernel(*refs, count):
    ins, out = refs[:count], refs[-1]
    heads, _, total = combine([p[...] for p in ins])
    for g, x in enumerate(heads):
        out[:, g * HEAD_SIZE : (g + 1) * HEAD_SIZE] = (x / total[:, g : g + 1]).astype(BF16)


def waiting_specs(pieces, after):
    whole = pl.BlockSpec(memory_space=pltpu.MemorySpace.VMEM)
    return [whole] * len(pieces) + [pl.BlockSpec(memory_space=pl.ANY)] * len(after)


def merge_pieces(pieces, after):
    blocks, rows, cols = pieces[0].shape
    size = blocks * rows * cols
    return pl.pallas_call(
        functools.partial(merge_kernel, count=len(pieces), waits=len(after)),
        in_specs=waiting_specs(pieces, after),
        out_shape=[jax.ShapeDtypeStruct((rows, cols), BF16)] * blocks,
        compiler_params=pltpu.CompilerParams(vmem_limit_bytes=VMEM_LIMIT),
        cost_estimate=pl.CostEstimate(
            flops=2 * size * len(pieces), bytes_accessed=2 * size * (len(pieces) + 1), transcendentals=0
        ),
        name="merge",
    )(*pieces, *after)


def normalize_pieces(pieces, after):
    rows, cols = pieces[0].shape
    size = rows * cols
    return pl.pallas_call(
        functools.partial(normalize_kernel, count=len(pieces)),
        in_specs=waiting_specs(pieces, after),
        out_shape=jax.ShapeDtypeStruct((rows, cols - LANES), BF16),
        compiler_params=pltpu.CompilerParams(vmem_limit_bytes=VMEM_LIMIT),
        cost_estimate=pl.CostEstimate(
            flops=2 * size * len(pieces), bytes_accessed=2 * size * (len(pieces) + 1), transcendentals=0
        ),
        name="normalize",
    )(*pieces, *after)


def project_kernel(info, *refs, plane, blocks, rows, width):
    ins, (w_ref, *base_ref, out) = refs[:plane], refs[plane:]
    for b in range(plane):
        x = ins[b][...].reshape(blocks * rows, width)
        y = jnp.dot(x, w_ref[...], preferred_element_type=F32)
        for a in range(blocks):
            at = (info[3 + blocks + a], b ^ info[1])
            part = y[a * rows : (a + 1) * rows]
            out[at] = ((base_ref[0][at] + part) if base_ref else part).astype(BF16)


def project_late(info, pieces, weight, base):
    plane = len(pieces)
    blocks, rows, width = pieces[0].shape
    out_cols = weight.shape[1]
    span = plane * blocks * rows
    whole = pl.BlockSpec((blocks, rows, width), lambda i, s: (0, 0, 0))
    out_block = pl.BlockSpec((blocks, plane, rows, out_cols), lambda i, s: (0, 0, 0, 0))
    return pl.pallas_call(
        functools.partial(project_kernel, plane=plane, blocks=blocks, rows=rows, width=width),
        grid_spec=pltpu.PrefetchScalarGridSpec(
            num_scalar_prefetch=1,
            grid=(1,),
            in_specs=[whole] * plane
            + [pl.BlockSpec((width, out_cols), lambda i, s: (weight.shape[0] // width - 1, 0))]
            + [out_block] * len(base),
            out_specs=out_block,
        ),
        out_shape=jax.ShapeDtypeStruct((blocks, plane, rows, out_cols), BF16),
        compiler_params=pltpu.CompilerParams(vmem_limit_bytes=VMEM_LIMIT),
        cost_estimate=pl.CostEstimate(
            flops=2 * span * width * out_cols,
            bytes_accessed=2 * (width * out_cols + span * width),
            transcendentals=0,
        ),
        name="project",
    )(info, *pieces, weight, *[x.reshape(blocks, plane, rows, out_cols) for x in base])


def exchange(x, axis, distance):
    count = lax.axis_size(axis)
    return lax.ppermute(x, axis, [(i, i ^ distance) for i in range(count)])


def local(queries, span_keys, span_values, context_keys, context_values, selected, out_weight):
    ctx_count, me = lax.axis_size("ctx"), lax.axis_index("ctx")
    head_count, my_head = lax.axis_size("head"), lax.axis_index("head")
    blocks = selected.shape[0]
    plane = ctx_count // blocks
    rows = queries.shape[0]
    heads = context_keys.shape[1] // HEAD_SIZE
    width = GROUP_QUERIES * HEAD_SIZE

    slot_block = lax.div(me, plane) ^ jnp.arange(blocks, dtype=jnp.int32)
    wanted = jnp.any(selected == me, axis=1)[slot_block]
    order = jnp.argsort(jnp.logical_not(wanted), stable=True).astype(jnp.int32)
    info = jnp.concatenate(
        [
            jnp.stack([me, lax.rem(me, plane), jnp.sum(wanted)]).astype(jnp.int32),
            order,
            slot_block.astype(jnp.int32),
        ]
    )

    def stack_blocks(x):
        return jnp.stack([x] + [exchange(x, "ctx", a * plane) for a in range(1, blocks)])

    def gather_plane(stack):
        return [stack] + [exchange(stack, "ctx", b) for b in range(1, plane)]

    def in_span_order(x):
        return x.reshape(blocks, plane, rows, x.shape[1])

    first = stack_blocks(queries[:, :width])
    sources = [(gather_plane(first), 0)]
    for group in [range(1, 2), range(2, heads)]:
        if len(group) and group[0] < heads:
            held, _ = lax.optimization_barrier((queries[:, group[0] * width : (group[-1] + 1) * width], first))
            whole = in_span_order(lax.all_gather(held, "ctx", axis=0, tiled=True))
            sources += [([whole], i) for i in range(len(group))]

    keys_t = context_keys.T
    attended, merged, rows_of = [], [], []

    def merge(h, after):
        own = attended[h]
        parts = [own[0]] + [exchange(own[b], "ctx", b) for b in range(1, plane)]
        merged.append(merge_pieces(parts, after))

    def normalize(h, after):
        own = merged[h]
        parts = [own[0]] + [exchange(own[a], "ctx", a * plane) for a in range(1, blocks)]
        rows_of.append(normalize_pieces(parts, after))

    for h in range(heads):
        after = []
        if h >= 3:
            normalize(h - 3, [attended[h - 1][0]])
            after.append(rows_of[h - 3])
        if h >= 2:
            merge(h - 2, [attended[h - 1][0]])
            after.append(merged[h - 2][0])
        attended.append(
            attend_head(info, *sources[h], keys_t, context_values, span_keys, span_values, h, after)
        )
    early = max(heads - 2, 0)
    spread_rows = {}

    def spread(h):
        spread_rows[h] = lax.all_gather(rows_of[h], "ctx", axis=0, tiled=True)
        return spread_rows[h]

    last = [attended[-1][0]] + [spread(h) for h in range(min(early, len(rows_of)))]
    for h in range(heads):
        if h >= len(merged):
            merge(h, last)
        if h >= len(rows_of):
            normalize(h, last)
    base = [
        jnp.dot(
            spread_rows[h] if h in spread_rows else spread(h),
            out_weight[h * width : (h + 1) * width],
            preferred_element_type=F32,
        )
        for h in range(early)
    ]
    base = [functools.reduce(jnp.add, base)] if base else []
    late = gather_plane(stack_blocks(jnp.concatenate(rows_of[early:], axis=1)))
    partial_out = project_late(info, late, out_weight, base).reshape(ctx_count * rows, -1)
    share = partial_out.shape[0] // head_count
    total = lax.dynamic_slice_in_dim(partial_out, my_head * share, share, 0).astype(F32)
    for d in range(1, head_count):
        other = lax.dynamic_slice_in_dim(partial_out, (my_head ^ d) * share, share, 0)
        total = total + exchange(other, "head", d).astype(F32)
    return total.astype(BF16)


def solution(mesh):
    return jax.shard_map(
        local,
        mesh=mesh,
        in_specs=(
            P("ctx", "head"),
            P("ctx", "head"),
            P("ctx", "head"),
            P("ctx", "head"),
            P("ctx", "head"),
            P(),
            P("head", "ctx"),
        ),
        out_specs=P("head", "ctx"),
        check_vma=False,
    )
```

```python
import functools

import jax
import jax.numpy as jnp
import numpy as np
from jax import lax
from jax.experimental import pallas as pl
from jax.experimental.pallas import tpu as pltpu
from jax.sharding import PartitionSpec as P

HEAD_SIZE = 128
GROUP_QUERIES = 8
LANES = 128
LOG2_SCALE = float(HEAD_SIZE**-0.5 * np.log2(np.e))
MASKED = -1e30
LOWEST = -1e20
VMEM_LIMIT = 56 * 1024 * 1024

BF16, F32 = jnp.bfloat16, jnp.float32
SHORT = pl.CostEstimate(flops=0, bytes_accessed=0, transcendentals=0)


def fold_lanes(op, x):
    parts = [x[:, i : i + LANES] for i in range(0, x.shape[1], LANES)]
    while len(parts) > 1:
        parts = [op(*parts[i : i + 2]) if i + 1 < len(parts) else parts[i] for i in range(0, len(parts), 2)]
    return parts[0]


def attend_kernel(info, *refs, plane, blocks, rows, group_step, key_chunk, waits):
    q_refs, refs = refs[:plane], refs[plane:]
    kt_ref, v_ref, ks_ref, vs_ref = refs[:4]
    refs = refs[4 + waits :]
    o_refs, refs = refs[:plane], refs[plane:]
    weight_refs, refs = refs[:2], refs[2:]
    score_ref, shift_ref, aux_ref, pos_ref, ks_pad, vs_pad = refs
    me, my_plane, wanted = info[0], info[1], info[2]
    keys = v_ref.shape[0]
    block_rows = plane * rows
    tile_rows = group_step * block_rows
    steps = GROUP_QUERIES // group_step
    chunks = keys // key_chunk
    strip = min(tile_rows, 64)

    ks_pad[...] = jnp.zeros_like(ks_pad)
    vs_pad[...] = jnp.zeros_like(vs_pad)
    ks_pad[0:rows, :] = ks_ref[...]
    vs_pad[0:rows, :] = vs_ref[...]
    row = lax.broadcasted_iota(jnp.int32, (tile_rows, LANES), 0)
    col = lax.broadcasted_iota(jnp.int32, (tile_rows, LANES), 1)
    piece = lax.rem(lax.div(row, rows), plane)
    pos_ref[...] = jnp.where(
        col < rows, (piece ^ my_plane) * rows + lax.rem(row, rows) - me * rows - col, -(1 << 30)
    )
    lane = lax.broadcasted_iota(jnp.int32, (block_rows, LANES), 1)

    def place(tile):
        return info[3 + lax.div(tile, steps)], lax.rem(tile, steps) * group_step

    def load_queries(tile):
        slot, group = place(tile)
        parts = []
        for i in range(group_step):
            cols = pl.ds(pl.multiple_of((group + i) * HEAD_SIZE, HEAD_SIZE), HEAD_SIZE)
            parts += [q[slot, :, cols] for q in q_refs]
        return jnp.concatenate(parts, axis=0)

    def span_scores(q, tile):
        slot, _ = place(tile)
        start = info[3 + blocks + slot] * block_rows
        scores = lax.dot_general(q, ks_pad[...], (((1,), (1,)), ((), ())), preferred_element_type=F32)
        return jnp.where(pos_ref[...] + start >= 0, scores, MASKED)

    def shift_of(peak):
        top = jnp.max(peak, axis=1, keepdims=True) * LOG2_SCALE
        return jnp.broadcast_to(jnp.maximum(top, LOWEST).astype(BF16).astype(F32), (tile_rows, LANES))

    def finish(tile, shift, total, acc):
        slot, group = place(tile)
        total = jnp.sum(total, axis=1, keepdims=True)
        high = total.astype(BF16).astype(F32)
        low = total - high
        aux = jnp.where(group == 0, 0.0, aux_ref[...])
        for i in range(group_step):
            cols = pl.ds(pl.multiple_of((group + i) * HEAD_SIZE, HEAD_SIZE), HEAD_SIZE)
            part = slice(i * block_rows, (i + 1) * block_rows)
            aux = jnp.where(lane == group + i, shift[part], aux)
            aux = jnp.where(lane == group + i + GROUP_QUERIES, high[part], aux)
            aux = jnp.where(lane == group + i + 2 * GROUP_QUERIES, low[part], aux)
            for b, o in enumerate(o_refs):
                start = i * block_rows + b * rows
                o[slot, :, cols] = acc[start : start + rows].astype(BF16)
        aux_ref[...] = aux
        for b, o in enumerate(o_refs):
            o[slot, :, GROUP_QUERIES * HEAD_SIZE :] = aux[b * rows : (b + 1) * rows].astype(BF16)

    def score_chunk(q, peak, j):
        part = slice(j * key_chunk, (j + 1) * key_chunk)
        scores = jnp.dot(q, kt_ref[:, part], preferred_element_type=F32)
        score_ref[:, part] = scores
        return jnp.maximum(peak, fold_lanes(jnp.maximum, scores))

    def weigh_chunk(totals, j):
        weight_ref = weight_refs[j % 2]
        for n, r in enumerate(range(0, tile_rows, strip)):
            part = slice(r, r + strip)
            shift = shift_ref[part]
            for c in range(0, key_chunk, LANES):
                start = j * key_chunk + c
                weights = jnp.exp2(score_ref[part, start : start + LANES] * LOG2_SCALE - shift)
                totals[n] = totals[n] + weights
                weight_ref[part, c : c + LANES] = weights.astype(BF16)

    def apply_chunk(acc, j):
        values = v_ref[j * key_chunk : (j + 1) * key_chunk]
        return acc + jnp.dot(weight_refs[j % 2][...], values, preferred_element_type=F32)

    def step(now, later):
        weights = jnp.exp2(score_ref[:, keys:] * LOG2_SCALE - shift_ref[...])
        acc = jnp.dot(weights.astype(BF16), vs_pad[...], preferred_element_type=F32)
        totals = [weights[r : r + strip] for r in range(0, tile_rows, strip)]
        q = load_queries(later)
        peak = span_scores(q, later)
        score_ref[:, keys:] = peak
        for j in range(chunks):
            weigh_chunk(totals, j)
            peak = score_chunk(q, peak, j)
            if j > 0:
                acc = apply_chunk(acc, j - 1)
        acc = apply_chunk(acc, chunks - 1)
        finish(now, shift_ref[...], jnp.concatenate(totals, axis=0), acc)
        shift_ref[...] = shift_of(peak)

    count = wanted * steps

    @pl.when(count > 0)
    def _():
        q = load_queries(jnp.int32(0))
        peak = span_scores(q, jnp.int32(0))
        score_ref[:, keys:] = peak
        for j in range(chunks):
            peak = score_chunk(q, peak, j)
        shift_ref[...] = shift_of(peak)

        def body(t, _):
            step(t, jnp.minimum(t + 1, count - 1))
            return 0

        lax.fori_loop(0, count, body, 0)

    def span_only(t, _):
        scores = span_scores(load_queries(t), t)
        shift = shift_of(scores)
        weights = jnp.exp2(scores * LOG2_SCALE - shift)
        acc = jnp.dot(weights.astype(BF16), vs_pad[...], preferred_element_type=F32)
        finish(t, shift, weights, acc)
        return 0

    lax.fori_loop(count, blocks * steps, span_only, 0)


def attend_head(info, q_pieces, q_head, keys_t, values, span_keys, span_values, head, after):
    plane = len(q_pieces)
    blocks, rows, _ = q_pieces[0].shape
    cols = GROUP_QUERIES * HEAD_SIZE
    key_count = values.shape[0]
    group_step = 2
    tile_rows = group_step * plane * rows
    key_chunk = min(key_count, 512)
    out_cols = cols + LANES
    vmem = pltpu.MemorySpace.VMEM
    whole = pl.BlockSpec((blocks, rows, cols), lambda i, s: (0, 0, q_head))
    whole_out = pl.BlockSpec((blocks, rows, out_cols), lambda i, s: (0, 0, 0))
    span_block = pl.BlockSpec((rows, HEAD_SIZE), lambda i, s: (0, head))
    scored = blocks * plane * rows * GROUP_QUERIES * key_count
    return pl.pallas_call(
        functools.partial(
            attend_kernel,
            plane=plane,
            blocks=blocks,
            rows=rows,
            group_step=group_step,
            key_chunk=key_chunk,
            waits=len(after),
        ),
        grid_spec=pltpu.PrefetchScalarGridSpec(
            num_scalar_prefetch=1,
            grid=(1,),
            in_specs=[whole] * plane
            + [
                pl.BlockSpec((HEAD_SIZE, key_count), lambda i, s: (head, 0)),
                pl.BlockSpec((key_count, HEAD_SIZE), lambda i, s: (0, head)),
                span_block,
                span_block,
            ]
            + [pl.BlockSpec(memory_space=pl.ANY)] * len(after),
            out_specs=[whole_out] * plane,
            scratch_shapes=[vmem((tile_rows, key_chunk), BF16)] * 2
            + [
                vmem((tile_rows, key_count + LANES), F32),
                vmem((tile_rows, LANES), F32),
                vmem((plane * rows, LANES), F32),
                vmem((tile_rows, LANES), jnp.int32),
                vmem((LANES, HEAD_SIZE), BF16),
                vmem((LANES, HEAD_SIZE), BF16),
            ],
        ),
        out_shape=[jax.ShapeDtypeStruct((blocks, rows, out_cols), BF16)] * plane,
        compiler_params=pltpu.CompilerParams(vmem_limit_bytes=VMEM_LIMIT),
        cost_estimate=pl.CostEstimate(
            flops=8 * scored * HEAD_SIZE,
            bytes_accessed=4 * key_count * HEAD_SIZE + 4 * blocks * plane * rows * cols,
            transcendentals=scored,
        ),
        name="attend",
    )(info, *q_pieces, keys_t, values, span_keys, span_values, *after)


def combine(parts):
    width = GROUP_QUERIES * HEAD_SIZE
    aux = [p[:, width:].astype(F32) for p in parts]
    top = functools.reduce(jnp.maximum, aux)
    factors = [jnp.exp2(jnp.minimum(a - top, 0.0)) for a in aux]
    sums = [
        pltpu.roll(a, LANES - GROUP_QUERIES, 1) + pltpu.roll(a, LANES - 2 * GROUP_QUERIES, 1) for a in aux
    ]
    total = sum(f * s for f, s in zip(factors, sums))
    heads = []
    for g in range(GROUP_QUERIES):
        cols = slice(g * HEAD_SIZE, (g + 1) * HEAD_SIZE)
        heads.append(sum(f[:, g : g + 1] * p[:, cols].astype(F32) for f, p in zip(factors, parts)))
    return heads, top, total


def merge_kernel(*refs, count, waits):
    ins, outs = refs[:count], refs[count + waits :]
    for a, out in enumerate(outs):
        heads, top, total = combine([p[a] for p in ins])
        for g, x in enumerate(heads):
            out[:, g * HEAD_SIZE : (g + 1) * HEAD_SIZE] = x.astype(BF16)
        lane = lax.broadcasted_iota(jnp.int32, top.shape, 1)
        high = total.astype(BF16).astype(F32)
        aux = jnp.where(
            lane < GROUP_QUERIES,
            top,
            jnp.where(
                lane < 2 * GROUP_QUERIES,
                pltpu.roll(high, GROUP_QUERIES, 1),
                pltpu.roll(total - high, 2 * GROUP_QUERIES, 1),
            ),
        )
        aux = jnp.where(lane < 3 * GROUP_QUERIES, aux, 0.0)
        out[:, GROUP_QUERIES * HEAD_SIZE :] = aux.astype(BF16)


def normalize_kernel(*refs, count):
    ins, out = refs[:count], refs[-1]
    heads, _, total = combine([p[...] for p in ins])
    for g, x in enumerate(heads):
        out[:, g * HEAD_SIZE : (g + 1) * HEAD_SIZE] = (x / total[:, g : g + 1]).astype(BF16)


def waiting_specs(pieces, after):
    whole = pl.BlockSpec(memory_space=pltpu.MemorySpace.VMEM)
    return [whole] * len(pieces) + [pl.BlockSpec(memory_space=pl.ANY)] * len(after)


def merge_pieces(pieces, after):
    blocks, rows, cols = pieces[0].shape
    return pl.pallas_call(
        functools.partial(merge_kernel, count=len(pieces), waits=len(after)),
        in_specs=waiting_specs(pieces, after),
        out_shape=[jax.ShapeDtypeStruct((rows, cols), BF16)] * blocks,
        compiler_params=pltpu.CompilerParams(vmem_limit_bytes=VMEM_LIMIT),
        cost_estimate=SHORT,
        name="merge",
    )(*pieces, *after)


def normalize_pieces(pieces, after):
    rows, cols = pieces[0].shape
    return pl.pallas_call(
        functools.partial(normalize_kernel, count=len(pieces)),
        in_specs=waiting_specs(pieces, after),
        out_shape=jax.ShapeDtypeStruct((rows, cols - LANES), BF16),
        compiler_params=pltpu.CompilerParams(vmem_limit_bytes=VMEM_LIMIT),
        cost_estimate=SHORT,
        name="normalize",
    )(*pieces, *after)


def project_kernel(info, *refs, plane, blocks, rows, width):
    ins, (w_ref, *base_ref, out) = refs[:plane], refs[plane:]
    for b in range(plane):
        x = ins[b][...].reshape(blocks * rows, width)
        y = jnp.dot(x, w_ref[...], preferred_element_type=F32)
        for a in range(blocks):
            at = (info[3 + blocks + a], b ^ info[1])
            part = y[a * rows : (a + 1) * rows]
            out[at] = ((base_ref[0][at] + part) if base_ref else part).astype(out.dtype)


def project(info, pieces, weight, group, base, dtype):
    plane = len(pieces)
    blocks, rows, width = pieces[0].shape
    out_cols = weight.shape[1]
    span = plane * blocks * rows
    whole = pl.BlockSpec((blocks, rows, width), lambda i, s: (0, 0, 0))
    out_block = pl.BlockSpec((blocks, plane, rows, out_cols), lambda i, s: (0, 0, 0, 0))
    return pl.pallas_call(
        functools.partial(project_kernel, plane=plane, blocks=blocks, rows=rows, width=width),
        grid_spec=pltpu.PrefetchScalarGridSpec(
            num_scalar_prefetch=1,
            grid=(1,),
            in_specs=[whole] * plane
            + [pl.BlockSpec((width, out_cols), lambda i, s: (group, 0))]
            + [out_block] * len(base),
            out_specs=out_block,
        ),
        out_shape=jax.ShapeDtypeStruct((blocks, plane, rows, out_cols), dtype),
        compiler_params=pltpu.CompilerParams(vmem_limit_bytes=VMEM_LIMIT),
        cost_estimate=pl.CostEstimate(
            flops=2 * span * width * out_cols,
            bytes_accessed=2 * (width * out_cols + span * width),
            transcendentals=0,
        ),
        name="project",
    )(info, *pieces, weight, *base)


def exchange(x, axis, distance):
    count = lax.axis_size(axis)
    return lax.ppermute(x, axis, [(i, i ^ distance) for i in range(count)])


def local(queries, span_keys, span_values, context_keys, context_values, selected, out_weight):
    ctx_count, me = lax.axis_size("ctx"), lax.axis_index("ctx")
    head_count, my_head = lax.axis_size("head"), lax.axis_index("head")
    blocks = selected.shape[0]
    plane = ctx_count // blocks
    rows = queries.shape[0]
    heads = context_keys.shape[1] // HEAD_SIZE
    width = GROUP_QUERIES * HEAD_SIZE

    slot_block = lax.div(me, plane) ^ jnp.arange(blocks, dtype=jnp.int32)
    wanted = jnp.any(selected == me, axis=1)[slot_block]
    order = jnp.argsort(jnp.logical_not(wanted), stable=True).astype(jnp.int32)
    info = jnp.concatenate(
        [
            jnp.stack([me, lax.rem(me, plane), jnp.sum(wanted)]).astype(jnp.int32),
            order,
            slot_block.astype(jnp.int32),
        ]
    )

    def stack_blocks(x):
        return jnp.stack([x] + [exchange(x, "ctx", a * plane) for a in range(1, blocks)])

    def gather_plane(stack):
        return [stack] + [exchange(stack, "ctx", b) for b in range(1, plane)]

    first = stack_blocks(queries[:, :width])
    sources, stacks = [(gather_plane(first), 0)], []
    if heads > 1:
        held, _ = lax.optimization_barrier((queries[:, width:], first))
        stacks = [stack_blocks(held)]
        pieces = gather_plane(stacks[0])
        sources += [(pieces, i) for i in range(heads - 1)]

    keys_t = context_keys.T

    attended, merged, rows_of = [], [], []

    def attend(h, after):
        attended.append(
            attend_head(info, *sources[h], keys_t, context_values, span_keys, span_values, h, after)
        )

    def merge(h, after):
        own = attended[h]
        parts = [own[0]] + [exchange(own[b], "ctx", b) for b in range(1, plane)]
        merged.append(merge_pieces(parts, after))

    def normalize(h, after):
        own = merged[h]
        parts = [own[0]] + [exchange(own[a], "ctx", a * plane) for a in range(1, blocks)]
        rows_of.append(normalize_pieces(parts, after))

    latest = stacks
    for h in range(heads):
        attend(h, latest)
        latest = [attended[h][0]]
        if h >= 1:
            merge(h - 1, latest)
            latest = [merged[h - 1][0]]
        if h >= 2:
            normalize(h - 2, latest)
            latest = [rows_of[h - 2]]
    merge(heads - 1, latest)
    held, _ = lax.optimization_barrier((rows_of, merged[-1][0]))
    rows_of = list(held)
    for h in range(len(rows_of), heads):
        normalize(h, [merged[-1][0]])
    size = 2 if heads % 2 == 0 else 1
    groups = [list(range(h, h + size)) for h in range(0, heads, size)]
    total = []
    for g, group in enumerate(groups):
        stack = stack_blocks(jnp.concatenate([rows_of[h] for h in group], axis=1))
        if total:
            stack, _ = lax.optimization_barrier((stack, total[0]))
        dtype = BF16 if g == len(groups) - 1 else F32
        total = [project(info, gather_plane(stack), out_weight, g, total, dtype)]
    partial_out = total[0].reshape(ctx_count * rows, -1)
    share = partial_out.shape[0] // head_count
    total = lax.dynamic_slice_in_dim(partial_out, my_head * share, share, 0).astype(F32)
    for d in range(1, head_count):
        other = lax.dynamic_slice_in_dim(partial_out, (my_head ^ d) * share, share, 0)
        total = total + exchange(other, "head", d).astype(F32)
    return total.astype(BF16)


def solution(mesh):
    return jax.shard_map(
        local,
        mesh=mesh,
        in_specs=(
            P("ctx", "head"),
            P("ctx", "head"),
            P("ctx", "head"),
            P("ctx", "head"),
            P("ctx", "head"),
            P(),
            P("head", "ctx"),
        ),
        out_specs=P("head", "ctx"),
        check_vma=False,
    )
```

```python
import functools

import jax
import jax.numpy as jnp
import numpy as np
from jax import lax
from jax.experimental import pallas as pl
from jax.experimental.pallas import tpu as pltpu
from jax.sharding import PartitionSpec as P

HEAD_SIZE = 128
GROUP_QUERIES = 8
LANES = 128
LOG2_SCALE = float(HEAD_SIZE**-0.5 * np.log2(np.e))
MASKED = -1e30
LOWEST = -1e20
ATTEND_VMEM = 28 * 1024 * 1024
SHORT_VMEM = 16 * 1024 * 1024

BF16, F32 = jnp.bfloat16, jnp.float32
SHORT = pl.CostEstimate(flops=0, bytes_accessed=0, transcendentals=0)


def fold_lanes(op, x):
    parts = [x[:, i : i + LANES] for i in range(0, x.shape[1], LANES)]
    while len(parts) > 1:
        parts = [op(*parts[i : i + 2]) if i + 1 < len(parts) else parts[i] for i in range(0, len(parts), 2)]
    return parts[0]


def attend_kernel(info, *refs, plane, blocks, rows, group_step, key_chunk, waits):
    q_refs, refs = refs[:plane], refs[plane:]
    kt_ref, v_ref, ks_ref, vs_ref = refs[:4]
    refs = refs[4 + waits :]
    o_refs, refs = refs[:plane], refs[plane:]
    weight_refs, refs = refs[:2], refs[2:]
    score_ref, shift_ref, aux_ref, pos_ref, ks_pad, vs_pad = refs
    me, my_plane, wanted = info[0], info[1], info[2]
    keys = v_ref.shape[0]
    block_rows = plane * rows
    tile_rows = group_step * block_rows
    steps = GROUP_QUERIES // group_step
    chunks = keys // key_chunk
    strip = min(tile_rows, 64)

    ks_pad[...] = jnp.zeros_like(ks_pad)
    vs_pad[...] = jnp.zeros_like(vs_pad)
    ks_pad[0:rows, :] = ks_ref[...]
    vs_pad[0:rows, :] = vs_ref[...]
    row = lax.broadcasted_iota(jnp.int32, (rows, LANES), 0)
    col = lax.broadcasted_iota(jnp.int32, (rows, LANES), 1)
    for i in range(group_step):
        for b in range(plane):
            start = (i * plane + b) * rows
            base = ((b ^ my_plane) - me) * rows
            pos_ref[start : start + rows] = jnp.where(col < rows, row - col + base, -(1 << 30))
    lane = lax.broadcasted_iota(jnp.int32, (block_rows, LANES), 1)

    def place(tile):
        return info[3 + lax.div(tile, steps)], lax.rem(tile, steps) * group_step

    def load_queries(tile):
        slot, group = place(tile)
        parts = []
        for i in range(group_step):
            cols = pl.ds(pl.multiple_of((group + i) * HEAD_SIZE, HEAD_SIZE), HEAD_SIZE)
            parts += [q[slot, :, cols] for q in q_refs]
        return jnp.concatenate(parts, axis=0)

    def span_scores(q, tile):
        slot, _ = place(tile)
        start = info[3 + blocks + slot] * block_rows
        scores = lax.dot_general(q, ks_pad[...], (((1,), (1,)), ((), ())), preferred_element_type=F32)
        return jnp.where(pos_ref[...] + start >= 0, scores, MASKED)

    def shift_of(peak):
        top = jnp.max(peak, axis=1, keepdims=True) * LOG2_SCALE
        return jnp.broadcast_to(jnp.maximum(top, LOWEST).astype(BF16).astype(F32), (tile_rows, LANES))

    def finish(tile, shift, total, acc):
        slot, group = place(tile)
        total = jnp.sum(total, axis=1, keepdims=True)
        high = total.astype(BF16).astype(F32)
        low = total - high
        aux = jnp.where(group == 0, 0.0, aux_ref[...])
        for i in range(group_step):
            cols = pl.ds(pl.multiple_of((group + i) * HEAD_SIZE, HEAD_SIZE), HEAD_SIZE)
            part = slice(i * block_rows, (i + 1) * block_rows)
            aux = jnp.where(lane == group + i, shift[part], aux)
            aux = jnp.where(lane == group + i + GROUP_QUERIES, high[part], aux)
            aux = jnp.where(lane == group + i + 2 * GROUP_QUERIES, low[part], aux)
            for b, o in enumerate(o_refs):
                start = i * block_rows + b * rows
                o[slot, :, cols] = acc[start : start + rows].astype(BF16)
        aux_ref[...] = aux
        for b, o in enumerate(o_refs):
            o[slot, :, GROUP_QUERIES * HEAD_SIZE :] = aux[b * rows : (b + 1) * rows].astype(BF16)

    def score_chunk(q, peak, j):
        part = slice(j * key_chunk, (j + 1) * key_chunk)
        scores = jnp.dot(q, kt_ref[:, part], preferred_element_type=F32)
        score_ref[:, part] = scores
        return jnp.maximum(peak, fold_lanes(jnp.maximum, scores))

    def weigh_chunk(totals, j):
        weight_ref = weight_refs[j % 2]
        for n, r in enumerate(range(0, tile_rows, strip)):
            part = slice(r, r + strip)
            shift = shift_ref[part]
            for c in range(0, key_chunk, LANES):
                start = j * key_chunk + c
                weights = jnp.exp2(score_ref[part, start : start + LANES] * LOG2_SCALE - shift)
                totals[n] = totals[n] + weights
                weight_ref[part, c : c + LANES] = weights.astype(BF16)

    def apply_chunk(acc, j):
        values = v_ref[j * key_chunk : (j + 1) * key_chunk]
        return acc + jnp.dot(weight_refs[j % 2][...], values, preferred_element_type=F32)

    def step(now, later):
        weights = jnp.exp2(score_ref[:, keys:] * LOG2_SCALE - shift_ref[...])
        acc = jnp.dot(weights.astype(BF16), vs_pad[...], preferred_element_type=F32)
        totals = [weights[r : r + strip] for r in range(0, tile_rows, strip)]
        q = load_queries(later)
        peak = span_scores(q, later)
        score_ref[:, keys:] = peak
        for j in range(chunks):
            weigh_chunk(totals, j)
            peak = score_chunk(q, peak, j)
            if j > 0:
                acc = apply_chunk(acc, j - 1)
        acc = apply_chunk(acc, chunks - 1)
        finish(now, shift_ref[...], jnp.concatenate(totals, axis=0), acc)
        shift_ref[...] = shift_of(peak)

    count = wanted * steps

    @pl.when(count > 0)
    def _():
        q = load_queries(jnp.int32(0))
        peak = span_scores(q, jnp.int32(0))
        score_ref[:, keys:] = peak
        for j in range(chunks):
            peak = score_chunk(q, peak, j)
        shift_ref[...] = shift_of(peak)

        def body(t, _):
            step(t, jnp.minimum(t + 1, count - 1))
            return 0

        lax.fori_loop(0, count, body, 0)

    def span_only(t, _):
        scores = span_scores(load_queries(t), t)
        shift = shift_of(scores)
        weights = jnp.exp2(scores * LOG2_SCALE - shift)
        acc = jnp.dot(weights.astype(BF16), vs_pad[...], preferred_element_type=F32)
        finish(t, shift, weights, acc)
        return 0

    lax.fori_loop(count, blocks * steps, span_only, 0)


def attend_head(info, q_pieces, q_head, keys_t, values, span_keys, span_values, head, after):
    plane = len(q_pieces)
    blocks, rows, _ = q_pieces[0].shape
    cols = GROUP_QUERIES * HEAD_SIZE
    key_count = values.shape[0]
    group_step = 2
    tile_rows = group_step * plane * rows
    key_chunk = min(key_count, 512)
    out_cols = cols + LANES
    vmem = pltpu.MemorySpace.VMEM
    whole = pl.BlockSpec((blocks, rows, cols), lambda i, s: (0, 0, q_head))
    whole_out = pl.BlockSpec((blocks, rows, out_cols), lambda i, s: (0, 0, 0))
    span_block = pl.BlockSpec((rows, HEAD_SIZE), lambda i, s: (0, head))
    scored = blocks * plane * rows * GROUP_QUERIES * key_count
    return pl.pallas_call(
        functools.partial(
            attend_kernel,
            plane=plane,
            blocks=blocks,
            rows=rows,
            group_step=group_step,
            key_chunk=key_chunk,
            waits=len(after),
        ),
        grid_spec=pltpu.PrefetchScalarGridSpec(
            num_scalar_prefetch=1,
            grid=(1,),
            in_specs=[whole] * plane
            + [
                pl.BlockSpec((HEAD_SIZE, key_count), lambda i, s: (head, 0)),
                pl.BlockSpec((key_count, HEAD_SIZE), lambda i, s: (0, head)),
                span_block,
                span_block,
            ]
            + [pl.BlockSpec(memory_space=pl.ANY)] * len(after),
            out_specs=[whole_out] * plane,
            scratch_shapes=[vmem((tile_rows, key_chunk), BF16)] * 2
            + [
                vmem((tile_rows, key_count + LANES), F32),
                vmem((tile_rows, LANES), F32),
                vmem((plane * rows, LANES), F32),
                vmem((tile_rows, LANES), jnp.int32),
                vmem((LANES, HEAD_SIZE), BF16),
                vmem((LANES, HEAD_SIZE), BF16),
            ],
        ),
        out_shape=[jax.ShapeDtypeStruct((blocks, rows, out_cols), BF16)] * plane,
        compiler_params=pltpu.CompilerParams(vmem_limit_bytes=ATTEND_VMEM),
        cost_estimate=pl.CostEstimate(
            flops=8 * scored * HEAD_SIZE,
            bytes_accessed=4 * key_count * HEAD_SIZE + 4 * blocks * plane * rows * cols,
            transcendentals=scored,
        ),
        name="attend",
    )(info, *q_pieces, keys_t, values, span_keys, span_values, *after)


def combine(parts):
    width = GROUP_QUERIES * HEAD_SIZE
    aux = [p[:, width:].astype(F32) for p in parts]
    top = functools.reduce(jnp.maximum, aux)
    factors = [jnp.exp2(jnp.minimum(a - top, 0.0)) for a in aux]
    sums = [
        pltpu.roll(a, LANES - GROUP_QUERIES, 1) + pltpu.roll(a, LANES - 2 * GROUP_QUERIES, 1) for a in aux
    ]
    total = sum(f * s for f, s in zip(factors, sums))
    heads = []
    for g in range(GROUP_QUERIES):
        cols = slice(g * HEAD_SIZE, (g + 1) * HEAD_SIZE)
        heads.append(sum(f[:, g : g + 1] * p[:, cols].astype(F32) for f, p in zip(factors, parts)))
    return heads, top, total


def merge_kernel(*refs, heads, plane, waits):
    ins, outs = refs[: heads * plane], refs[heads * plane + waits :]
    width = GROUP_QUERIES * HEAD_SIZE
    for h in range(heads):
        first = h * (width + LANES)
        for a, out in enumerate(outs):
            parts, top, total = combine([p[a] for p in ins[h * plane : (h + 1) * plane]])
            for g, x in enumerate(parts):
                out[:, first + g * HEAD_SIZE : first + (g + 1) * HEAD_SIZE] = x.astype(BF16)
            lane = lax.broadcasted_iota(jnp.int32, top.shape, 1)
            high = total.astype(BF16).astype(F32)
            aux = jnp.where(
                lane < GROUP_QUERIES,
                top,
                jnp.where(
                    lane < 2 * GROUP_QUERIES,
                    pltpu.roll(high, GROUP_QUERIES, 1),
                    pltpu.roll(total - high, 2 * GROUP_QUERIES, 1),
                ),
            )
            aux = jnp.where(lane < 3 * GROUP_QUERIES, aux, 0.0)
            out[:, first + width : first + width + LANES] = aux.astype(BF16)


def normalize_kernel(*refs, heads, count):
    ins, out = refs[:count], refs[-1]
    width = GROUP_QUERIES * HEAD_SIZE
    for h in range(heads):
        first = h * (width + LANES)
        parts, _, total = combine([p[:, first : first + width + LANES] for p in ins])
        for g, x in enumerate(parts):
            start = h * width + g * HEAD_SIZE
            out[:, start : start + HEAD_SIZE] = (x / total[:, g : g + 1]).astype(BF16)


def waiting_specs(count, waits):
    whole = pl.BlockSpec(memory_space=pltpu.MemorySpace.VMEM)
    return [whole] * count + [pl.BlockSpec(memory_space=pl.ANY)] * waits


def merge_pieces(pieces, after):
    heads, plane = len(pieces), len(pieces[0])
    blocks, rows, cols = pieces[0][0].shape
    return pl.pallas_call(
        functools.partial(merge_kernel, heads=heads, plane=plane, waits=len(after)),
        in_specs=waiting_specs(heads * plane, len(after)),
        out_shape=[jax.ShapeDtypeStruct((rows, heads * cols), BF16)] * blocks,
        compiler_params=pltpu.CompilerParams(vmem_limit_bytes=SHORT_VMEM),
        cost_estimate=SHORT,
        name="merge",
    )(*[p for own in pieces for p in own], *after)


def normalize_pieces(pieces, after):
    rows, cols = pieces[0].shape
    heads = cols // (GROUP_QUERIES * HEAD_SIZE + LANES)
    return pl.pallas_call(
        functools.partial(normalize_kernel, heads=heads, count=len(pieces)),
        in_specs=waiting_specs(len(pieces), len(after)),
        out_shape=jax.ShapeDtypeStruct((rows, cols - heads * LANES), BF16),
        compiler_params=pltpu.CompilerParams(vmem_limit_bytes=SHORT_VMEM),
        cost_estimate=SHORT,
        name="normalize",
    )(*pieces, *after)


def project_kernel(info, *refs, chosen, blocks, rows, width):
    ins, (w_ref, *base_ref, out) = refs[: len(chosen)], refs[len(chosen) :]
    if base_ref:
        out[...] = base_ref[0][...].astype(out.dtype)
    for x_ref, b in zip(ins, chosen):
        x = x_ref[...].reshape(blocks * rows, width)
        y = jnp.dot(x, w_ref[...], preferred_element_type=F32)
        for a in range(blocks):
            at = (info[3 + blocks + a], b ^ info[1])
            part = y[a * rows : (a + 1) * rows]
            out[at] = ((base_ref[0][at] + part) if base_ref else part).astype(out.dtype)


def project(info, pieces, chosen, weight, group, base, dtype):
    plane = len(pieces)
    blocks, rows, width = pieces[0].shape
    out_cols = weight.shape[1]
    span = len(chosen) * blocks * rows
    whole = pl.BlockSpec((blocks, rows, width), lambda i, s: (0, 0, 0))
    out_block = pl.BlockSpec((blocks, plane, rows, out_cols), lambda i, s: (0, 0, 0, 0))
    return pl.pallas_call(
        functools.partial(project_kernel, chosen=chosen, blocks=blocks, rows=rows, width=width),
        grid_spec=pltpu.PrefetchScalarGridSpec(
            num_scalar_prefetch=1,
            grid=(1,),
            in_specs=[whole] * len(chosen)
            + [pl.BlockSpec((width, out_cols), lambda i, s: (group, 0))]
            + [out_block] * len(base),
            out_specs=out_block,
        ),
        out_shape=jax.ShapeDtypeStruct((blocks, plane, rows, out_cols), dtype),
        compiler_params=pltpu.CompilerParams(vmem_limit_bytes=SHORT_VMEM),
        cost_estimate=pl.CostEstimate(
            flops=2 * span * width * out_cols,
            bytes_accessed=2 * (width * out_cols + span * width),
            transcendentals=0,
        ),
        name="project",
    )(info, *[pieces[b] for b in chosen], weight, *base)


def exchange(x, axis, distance):
    count = lax.axis_size(axis)
    return lax.ppermute(x, axis, [(i, i ^ distance) for i in range(count)])


def local(queries, span_keys, span_values, context_keys, context_values, selected, out_weight):
    ctx_count, me = lax.axis_size("ctx"), lax.axis_index("ctx")
    head_count, my_head = lax.axis_size("head"), lax.axis_index("head")
    blocks = selected.shape[0]
    plane = ctx_count // blocks
    rows = queries.shape[0]
    heads = context_keys.shape[1] // HEAD_SIZE
    width = GROUP_QUERIES * HEAD_SIZE

    slot_block = lax.div(me, plane) ^ jnp.arange(blocks, dtype=jnp.int32)
    wanted = jnp.any(selected == me, axis=1)[slot_block]
    order = jnp.argsort(jnp.logical_not(wanted), stable=True).astype(jnp.int32)
    info = jnp.concatenate(
        [
            jnp.stack([me, lax.rem(me, plane), jnp.sum(wanted)]).astype(jnp.int32),
            order,
            slot_block.astype(jnp.int32),
        ]
    )

    def stack_blocks(x):
        return jnp.stack([x] + [exchange(x, "ctx", a * plane) for a in range(1, blocks)])

    def gather_plane(stack):
        return [stack] + [exchange(stack, "ctx", b) for b in range(1, plane)]

    first = stack_blocks(queries[:, :width])
    sources, stacks = [(gather_plane(first), 0)], []
    keys, _ = lax.optimization_barrier((context_keys, first))
    keys_t = keys.T
    if heads > 1:
        held, _ = lax.optimization_barrier((queries[:, width:], first))
        stacks = [stack_blocks(held)]
        pieces = gather_plane(stacks[0])
        sources += [(pieces, i) for i in range(heads - 1)]

    size = 2 if heads % 2 == 0 else 1
    attended, merged, rows_of = [], [], []

    def merge(after):
        group = range(len(merged) * size, (len(merged) + 1) * size)
        parts = [
            [attended[h][0]] + [exchange(attended[h][b], "ctx", b) for b in range(1, plane)] for h in group
        ]
        merged.append(merge_pieces(parts, after))
        return [merged[-1][0]]

    def normalize(after):
        own = merged[len(rows_of)]
        parts = [own[0]] + [exchange(own[a], "ctx", a * plane) for a in range(1, blocks)]
        rows_of.append(normalize_pieces(parts, after))
        return [rows_of[-1]]

    latest = stacks
    for h in range(heads):
        attended.append(
            attend_head(info, *sources[h], keys_t, context_values, span_keys, span_values, h, latest)
        )
        latest = [attended[h][0]]
        if len(rows_of) < len(merged):
            latest = normalize(latest)
        if h >= (len(merged) + 1) * size:
            latest = merge(latest)
    while len(merged) < heads // size:
        latest = merge(latest)
    while len(rows_of) < heads // size:
        latest = normalize(latest)

    total = []
    for g, rows_now in enumerate(rows_of):
        if g < len(rows_of) - 1:
            rows_now, _ = lax.optimization_barrier((rows_now, merged[-1][0]))
        pieces = gather_plane(stack_blocks(rows_now))
        if g < len(rows_of) - 1:
            total = [project(info, pieces, range(plane), out_weight, g, total, F32)]
        else:
            total = [project(info, pieces, range(plane // 2), out_weight, g, total, F32)]
            total = [project(info, pieces, range(plane // 2, plane), out_weight, g, total, BF16)]
    partial_out = total[0].reshape(ctx_count * rows, -1)
    share = partial_out.shape[0] // head_count
    total = lax.dynamic_slice_in_dim(partial_out, my_head * share, share, 0).astype(F32)
    for d in range(1, head_count):
        other = lax.dynamic_slice_in_dim(partial_out, (my_head ^ d) * share, share, 0)
        total = total + exchange(other, "head", d).astype(F32)
    return total.astype(BF16)


def solution(mesh):
    return jax.shard_map(
        local,
        mesh=mesh,
        in_specs=(
            P("ctx", "head"),
            P("ctx", "head"),
            P("ctx", "head"),
            P("ctx", "head"),
            P("ctx", "head"),
            P(),
            P("head", "ctx"),
        ),
        out_specs=P("head", "ctx"),
        check_vma=False,
    )
```

```python
import functools
import math

import jax
import jax.numpy as jnp
import numpy as np
from jax import lax
from jax.experimental import pallas as pl
from jax.experimental.pallas import tpu as pltpu
from jax.sharding import PartitionSpec as P

HEAD_SIZE = 128
GROUP_QUERIES = 8
LANES = 128
LOG2_SCALE = float(HEAD_SIZE**-0.5 * np.log2(np.e))
MASKED = -1e30
LOWEST = -1e20
ATTEND_VMEM = 28 * 1024 * 1024
SHORT_VMEM = 16 * 1024 * 1024

BF16, F32 = jnp.bfloat16, jnp.float32
SHORT = pl.CostEstimate(flops=0, bytes_accessed=0, transcendentals=0)


def fold_lanes(op, x):
    parts = [x[:, i : i + LANES] for i in range(0, x.shape[1], LANES)]
    while len(parts) > 1:
        parts = [op(*parts[i : i + 2]) if i + 1 < len(parts) else parts[i] for i in range(0, len(parts), 2)]
    return parts[0]


def attend_kernel(info, *refs, chosen, blocks, plane, rows, head, q_head, group_step, key_chunk, waits):
    count = len(chosen)
    q_refs, refs = refs[:count], refs[count:]
    kt_ref, v_ref, ks_ref, vs_ref = refs[:4]
    refs = refs[4 + waits :]
    o_refs, refs = refs[:count], refs[count:]
    weight_refs, refs = refs[:2], refs[2:]
    score_ref, shift_ref, aux_ref, pos_ref, ks_pad, vs_pad = refs
    me, my_plane, wanted = info[0], info[1], info[2]
    keys = v_ref.shape[0]
    block_rows = count * rows
    tile_rows = group_step * block_rows
    steps = GROUP_QUERIES // group_step
    chunks = keys // key_chunk
    strip = math.gcd(tile_rows, 64)
    own = slice(head * HEAD_SIZE, (head + 1) * HEAD_SIZE)
    q_first = q_head * GROUP_QUERIES

    ks_pad[...] = jnp.zeros_like(ks_pad)
    vs_pad[...] = jnp.zeros_like(vs_pad)
    ks_pad[0:rows, :] = ks_ref[:, own]
    vs_pad[0:rows, :] = vs_ref[:, own]
    row = lax.broadcasted_iota(jnp.int32, (rows, LANES), 0)
    col = lax.broadcasted_iota(jnp.int32, (rows, LANES), 1)
    for i in range(group_step):
        for n, b in enumerate(chosen):
            start = (i * count + n) * rows
            base = ((b ^ my_plane) - me) * rows
            pos_ref[start : start + rows] = jnp.where(col < rows, row - col + base, -(1 << 30))
    lane = lax.broadcasted_iota(jnp.int32, (block_rows, LANES), 1)

    def place(tile):
        return info[3 + lax.div(tile, steps)], lax.rem(tile, steps) * group_step

    def load_queries(tile):
        slot, group = place(tile)
        parts = []
        for i in range(group_step):
            cols = pl.ds(pl.multiple_of((q_first + group + i) * HEAD_SIZE, HEAD_SIZE), HEAD_SIZE)
            parts += [q[slot, :, cols] for q in q_refs]
        return jnp.concatenate(parts, axis=0)

    def span_scores(q, tile):
        slot, _ = place(tile)
        start = info[3 + blocks + slot] * (plane * rows)
        scores = lax.dot_general(q, ks_pad[...], (((1,), (1,)), ((), ())), preferred_element_type=F32)
        return jnp.where(pos_ref[...] + start >= 0, scores, MASKED)

    def shift_of(peak):
        top = jnp.max(peak, axis=1, keepdims=True) * LOG2_SCALE
        return jnp.broadcast_to(jnp.maximum(top, LOWEST).astype(BF16).astype(F32), (tile_rows, LANES))

    def finish(tile, shift, total, acc):
        slot, group = place(tile)
        total = jnp.sum(total, axis=1, keepdims=True)
        high = total.astype(BF16).astype(F32)
        low = total - high
        aux = jnp.where(group == 0, 0.0, aux_ref[...])
        for i in range(group_step):
            cols = pl.ds(pl.multiple_of((group + i) * HEAD_SIZE, HEAD_SIZE), HEAD_SIZE)
            part = slice(i * block_rows, (i + 1) * block_rows)
            aux = jnp.where(lane == group + i, shift[part], aux)
            aux = jnp.where(lane == group + i + GROUP_QUERIES, high[part], aux)
            aux = jnp.where(lane == group + i + 2 * GROUP_QUERIES, low[part], aux)
            for b, o in enumerate(o_refs):
                start = i * block_rows + b * rows
                o[slot, :, cols] = acc[start : start + rows].astype(BF16)
        aux_ref[...] = aux
        for b, o in enumerate(o_refs):
            o[slot, :, GROUP_QUERIES * HEAD_SIZE :] = aux[b * rows : (b + 1) * rows].astype(BF16)

    def score_chunk(q, peak, j):
        part = slice(j * key_chunk, (j + 1) * key_chunk)
        scores = jnp.dot(q, kt_ref[:, part], preferred_element_type=F32)
        score_ref[:, part] = scores
        return jnp.maximum(peak, fold_lanes(jnp.maximum, scores))

    def weigh_chunk(totals, j):
        weight_ref = weight_refs[j % 2]
        for n, r in enumerate(range(0, tile_rows, strip)):
            part = slice(r, r + strip)
            shift = shift_ref[part]
            for c in range(0, key_chunk, LANES):
                start = j * key_chunk + c
                weights = jnp.exp2(score_ref[part, start : start + LANES] * LOG2_SCALE - shift)
                totals[n] = totals[n] + weights
                weight_ref[part, c : c + LANES] = weights.astype(BF16)

    def apply_chunk(acc, j):
        values = v_ref[j * key_chunk : (j + 1) * key_chunk, own]
        return acc + jnp.dot(weight_refs[j % 2][...], values, preferred_element_type=F32)

    def step(now, later):
        weights = jnp.exp2(score_ref[:, keys:] * LOG2_SCALE - shift_ref[...])
        acc = jnp.dot(weights.astype(BF16), vs_pad[...], preferred_element_type=F32)
        totals = [weights[r : r + strip] for r in range(0, tile_rows, strip)]
        q = load_queries(later)
        peak = span_scores(q, later)
        score_ref[:, keys:] = peak
        for j in range(chunks):
            weigh_chunk(totals, j)
            peak = score_chunk(q, peak, j)
            if j > 0:
                acc = apply_chunk(acc, j - 1)
        acc = apply_chunk(acc, chunks - 1)
        finish(now, shift_ref[...], jnp.concatenate(totals, axis=0), acc)
        shift_ref[...] = shift_of(peak)

    tiles = wanted * steps

    @pl.when(tiles > 0)
    def _():
        q = load_queries(jnp.int32(0))
        peak = span_scores(q, jnp.int32(0))
        score_ref[:, keys:] = peak
        for j in range(chunks):
            peak = score_chunk(q, peak, j)
        shift_ref[...] = shift_of(peak)

        def body(t, _):
            step(t, jnp.minimum(t + 1, tiles - 1))
            return 0

        lax.fori_loop(0, tiles, body, 0)

    def span_only(t, _):
        scores = span_scores(load_queries(t), t)
        shift = shift_of(scores)
        weights = jnp.exp2(scores * LOG2_SCALE - shift)
        acc = jnp.dot(weights.astype(BF16), vs_pad[...], preferred_element_type=F32)
        finish(t, shift, weights, acc)
        return 0

    lax.fori_loop(tiles, blocks * steps, span_only, 0)


def attend_head(info, q_pieces, chosen, q_head, keys_t, values, span_keys, span_values, head, after):
    blocks, rows, _ = q_pieces[0].shape
    plane, count = len(q_pieces), len(chosen)
    cols = GROUP_QUERIES * HEAD_SIZE
    key_count = values.shape[0]
    group_step = min(GROUP_QUERIES, 2 * (plane // count))
    tile_rows = group_step * count * rows
    key_chunk = min(key_count, 512)
    vmem, smem = pltpu.MemorySpace.VMEM, pltpu.MemorySpace.SMEM
    scored = blocks * count * rows * GROUP_QUERIES * key_count
    return pl.pallas_call(
        functools.partial(
            attend_kernel,
            chosen=chosen,
            blocks=blocks,
            plane=plane,
            rows=rows,
            head=head,
            q_head=q_head,
            group_step=group_step,
            key_chunk=key_chunk,
            waits=len(after),
        ),
        in_specs=[pl.BlockSpec(memory_space=smem)]
        + [pl.BlockSpec(memory_space=vmem)] * (count + 4)
        + [pl.BlockSpec(memory_space=pl.ANY)] * len(after),
        out_specs=[pl.BlockSpec(memory_space=vmem)] * count,
        scratch_shapes=[vmem((tile_rows, key_chunk), BF16)] * 2
        + [
            vmem((tile_rows, key_count + LANES), F32),
            vmem((tile_rows, LANES), F32),
            vmem((count * rows, LANES), F32),
            vmem((tile_rows, LANES), jnp.int32),
            vmem((LANES, HEAD_SIZE), BF16),
            vmem((LANES, HEAD_SIZE), BF16),
        ],
        out_shape=[jax.ShapeDtypeStruct((blocks, rows, cols + LANES), BF16)] * count,
        compiler_params=pltpu.CompilerParams(vmem_limit_bytes=ATTEND_VMEM),
        cost_estimate=pl.CostEstimate(
            flops=8 * scored * HEAD_SIZE,
            bytes_accessed=4 * key_count * HEAD_SIZE + 4 * blocks * count * rows * cols,
            transcendentals=scored,
        ),
        name="attend",
    )(info, *[q_pieces[b] for b in chosen], keys_t, values, span_keys, span_values, *after)


def combine(parts):
    width = GROUP_QUERIES * HEAD_SIZE
    aux = [p[:, width:].astype(F32) for p in parts]
    top = functools.reduce(jnp.maximum, aux)
    factors = [jnp.exp2(jnp.minimum(a - top, 0.0)) for a in aux]
    sums = [
        pltpu.roll(a, LANES - GROUP_QUERIES, 1) + pltpu.roll(a, LANES - 2 * GROUP_QUERIES, 1) for a in aux
    ]
    total = sum(f * s for f, s in zip(factors, sums))
    heads = []
    for g in range(GROUP_QUERIES):
        cols = slice(g * HEAD_SIZE, (g + 1) * HEAD_SIZE)
        heads.append(sum(f[:, g : g + 1] * p[:, cols].astype(F32) for f, p in zip(factors, parts)))
    return heads, top, total


def merge_kernel(*refs, heads, plane, waits):
    ins, outs = refs[: heads * plane], refs[heads * plane + waits :]
    width = GROUP_QUERIES * HEAD_SIZE
    for h in range(heads):
        first = h * (width + LANES)
        for a, out in enumerate(outs):
            parts, top, total = combine([p[a] for p in ins[h * plane : (h + 1) * plane]])
            for g, x in enumerate(parts):
                out[:, first + g * HEAD_SIZE : first + (g + 1) * HEAD_SIZE] = x.astype(BF16)
            lane = lax.broadcasted_iota(jnp.int32, top.shape, 1)
            high = total.astype(BF16).astype(F32)
            aux = jnp.where(
                lane < GROUP_QUERIES,
                top,
                jnp.where(
                    lane < 2 * GROUP_QUERIES,
                    pltpu.roll(high, GROUP_QUERIES, 1),
                    pltpu.roll(total - high, 2 * GROUP_QUERIES, 1),
                ),
            )
            aux = jnp.where(lane < 3 * GROUP_QUERIES, aux, 0.0)
            out[:, first + width : first + width + LANES] = aux.astype(BF16)


def normalize_kernel(*refs, heads, count):
    ins, out = refs[:count], refs[-1]
    width = GROUP_QUERIES * HEAD_SIZE
    for h in range(heads):
        first = h * (width + LANES)
        parts, _, total = combine([p[:, first : first + width + LANES] for p in ins])
        for g, x in enumerate(parts):
            start = h * width + g * HEAD_SIZE
            out[:, start : start + HEAD_SIZE] = (x / total[:, g : g + 1]).astype(BF16)


def waiting_specs(count, waits):
    whole = pl.BlockSpec(memory_space=pltpu.MemorySpace.VMEM)
    return [whole] * count + [pl.BlockSpec(memory_space=pl.ANY)] * waits


def merge_pieces(pieces, after):
    heads, plane = len(pieces), len(pieces[0])
    blocks, rows, cols = pieces[0][0].shape
    return pl.pallas_call(
        functools.partial(merge_kernel, heads=heads, plane=plane, waits=len(after)),
        in_specs=waiting_specs(heads * plane, len(after)),
        out_shape=[jax.ShapeDtypeStruct((rows, heads * cols), BF16)] * blocks,
        compiler_params=pltpu.CompilerParams(vmem_limit_bytes=SHORT_VMEM),
        cost_estimate=SHORT,
        name="merge",
    )(*[p for own in pieces for p in own], *after)


def normalize_pieces(pieces, after):
    rows, cols = pieces[0].shape
    heads = cols // (GROUP_QUERIES * HEAD_SIZE + LANES)
    return pl.pallas_call(
        functools.partial(normalize_kernel, heads=heads, count=len(pieces)),
        in_specs=waiting_specs(len(pieces), len(after)),
        out_shape=jax.ShapeDtypeStruct((rows, cols - heads * LANES), BF16),
        compiler_params=pltpu.CompilerParams(vmem_limit_bytes=SHORT_VMEM),
        cost_estimate=SHORT,
        name="normalize",
    )(*pieces, *after)


def project_kernel(info, *refs, chosen, blocks, rows, width):
    ins, (w_ref, *base_ref, out) = refs[: len(chosen)], refs[len(chosen) :]
    out[...] = base_ref[0][...].astype(out.dtype) if base_ref else jnp.zeros_like(out)
    for x_ref, b in zip(ins, chosen):
        x = x_ref[...].reshape(blocks * rows, width)
        y = jnp.dot(x, w_ref[...], preferred_element_type=F32)
        for a in range(blocks):
            at = (info[3 + blocks + a], b ^ info[1])
            part = y[a * rows : (a + 1) * rows]
            out[at] = ((base_ref[0][at] + part) if base_ref else part).astype(out.dtype)


def project(info, pieces, chosen, weight, group, base, dtype):
    plane = len(pieces)
    blocks, rows, width = pieces[0].shape
    out_cols = weight.shape[1]
    span = len(chosen) * blocks * rows
    whole = pl.BlockSpec((blocks, rows, width), lambda i, s: (0, 0, 0))
    out_block = pl.BlockSpec((blocks, plane, rows, out_cols), lambda i, s: (0, 0, 0, 0))
    return pl.pallas_call(
        functools.partial(project_kernel, chosen=chosen, blocks=blocks, rows=rows, width=width),
        grid_spec=pltpu.PrefetchScalarGridSpec(
            num_scalar_prefetch=1,
            grid=(1,),
            in_specs=[whole] * len(chosen)
            + [pl.BlockSpec((width, out_cols), lambda i, s: (group, 0))]
            + [out_block] * len(base),
            out_specs=out_block,
        ),
        out_shape=jax.ShapeDtypeStruct((blocks, plane, rows, out_cols), dtype),
        compiler_params=pltpu.CompilerParams(vmem_limit_bytes=SHORT_VMEM),
        cost_estimate=pl.CostEstimate(
            flops=2 * span * width * out_cols,
            bytes_accessed=2 * (width * out_cols + span * width),
            transcendentals=0,
        ),
        name="project",
    )(info, *[pieces[b] for b in chosen], weight, *base)


def exchange(x, axis, distance):
    count = lax.axis_size(axis)
    return lax.ppermute(x, axis, [(i, i ^ distance) for i in range(count)])


def local(queries, span_keys, span_values, context_keys, context_values, selected, out_weight):
    ctx_count, me = lax.axis_size("ctx"), lax.axis_index("ctx")
    head_count, my_head = lax.axis_size("head"), lax.axis_index("head")
    blocks = selected.shape[0]
    plane = ctx_count // blocks
    rows = queries.shape[0]
    heads = context_keys.shape[1] // HEAD_SIZE
    width = GROUP_QUERIES * HEAD_SIZE

    slot_block = lax.div(me, plane) ^ jnp.arange(blocks, dtype=jnp.int32)
    wanted = jnp.any(selected == me, axis=1)[slot_block]
    order = jnp.argsort(jnp.logical_not(wanted), stable=True).astype(jnp.int32)
    info = jnp.concatenate(
        [
            jnp.stack([me, lax.rem(me, plane), jnp.sum(wanted)]).astype(jnp.int32),
            order,
            slot_block.astype(jnp.int32),
        ]
    )

    def stack_blocks(x):
        return jnp.stack([x] + [exchange(x, "ctx", a * plane) for a in range(1, blocks)])

    def gather_plane(stack):
        return [stack] + [exchange(stack, "ctx", b) for b in range(1, plane)]

    first = stack_blocks(queries[:, :width])
    sources, stacks = [(gather_plane(first), 0)], []
    keys, _ = lax.optimization_barrier((context_keys, first))
    keys_t = [
        (keys if h else context_keys)[:, h * HEAD_SIZE : (h + 1) * HEAD_SIZE].T for h in range(heads)
    ]
    if heads > 1:
        stacks = [stack_blocks(queries[:, width:])]
        pieces = gather_plane(stacks[0])
        sources += [(pieces, i) for i in range(heads - 1)]

    size = 2 if heads % 2 == 0 else 1
    attended, merged, rows_of = [], [], []

    def merge(after):
        group = range(len(merged) * size, (len(merged) + 1) * size)
        parts = [
            [attended[h][0]] + [exchange(attended[h][b], "ctx", b) for b in range(1, plane)] for h in group
        ]
        merged.append(merge_pieces(parts, after))
        return [merged[-1][0]]

    def normalize(after):
        own = merged[len(rows_of)]
        parts = [own[0]] + [exchange(own[a], "ctx", a * plane) for a in range(1, blocks)]
        rows_of.append(normalize_pieces(parts, after))
        return [rows_of[-1]]

    def attend(h, chosen, after):
        pieces, q_head = sources[h]
        return attend_head(
            info, pieces, chosen, q_head, keys_t[h], context_values, span_keys, span_values, h, after
        )

    latest = stacks
    for h in range(heads):
        start = 1 if h == heads - 1 else 0
        attended.append(attend(h, range(start, plane), latest))
        latest = [attended[h][0]]
        if len(rows_of) < len(merged):
            latest = normalize(latest)
        if start:
            attended[h] = attend(h, [0], latest) + attended[h]
            latest = [attended[h][0]]
        if h >= (len(merged) + 1) * size:
            latest = merge(latest)
    while len(merged) < heads // size:
        latest = merge(latest)
    while len(rows_of) < heads // size:
        latest = normalize(latest)

    total = []
    for g, rows_now in enumerate(rows_of):
        if g < len(rows_of) - 1:
            rows_now, _ = lax.optimization_barrier((rows_now, attended[-1][0]))
        pieces = gather_plane(stack_blocks(rows_now))
        if g < len(rows_of) - 1:
            total = [project(info, pieces, range(plane), out_weight, g, total, F32)]
        else:
            total = [project(info, pieces, range(plane // 2), out_weight, g, total, F32)]
            total = [project(info, pieces, range(plane // 2, plane), out_weight, g, total, BF16)]
    partial_out = total[0].reshape(ctx_count * rows, -1)
    share = partial_out.shape[0] // head_count
    total = lax.dynamic_slice_in_dim(partial_out, my_head * share, share, 0).astype(F32)
    for d in range(1, head_count):
        other = lax.dynamic_slice_in_dim(partial_out, (my_head ^ d) * share, share, 0)
        total = total + exchange(other, "head", d).astype(F32)
    return total.astype(BF16)


def solution(mesh):
    return jax.shard_map(
        local,
        mesh=mesh,
        in_specs=(
            P("ctx", "head"),
            P("ctx", "head"),
            P("ctx", "head"),
            P("ctx", "head"),
            P("ctx", "head"),
            P(),
            P("head", "ctx"),
        ),
        out_specs=P("head", "ctx"),
        check_vma=False,
    )
```

```python
import functools
import math

import jax
import jax.numpy as jnp
import numpy as np
from jax import lax
from jax.experimental import pallas as pl
from jax.experimental.pallas import tpu as pltpu
from jax.sharding import PartitionSpec as P

HEAD_SIZE = 128
GROUP_QUERIES = 8
LANES = 128
LOG2_SCALE = float(HEAD_SIZE**-0.5 * np.log2(np.e))
MASKED = -1e30
LOWEST = -1e20
ATTEND_VMEM = 28 * 1024 * 1024
SHORT_VMEM = 16 * 1024 * 1024

BF16, F32 = jnp.bfloat16, jnp.float32
SHORT = pl.CostEstimate(flops=0, bytes_accessed=0, transcendentals=0)


def fold_lanes(op, x):
    parts = [x[:, i : i + LANES] for i in range(0, x.shape[1], LANES)]
    while len(parts) > 1:
        parts = [op(*parts[i : i + 2]) if i + 1 < len(parts) else parts[i] for i in range(0, len(parts), 2)]
    return parts[0]


def attend_kernel(info, *refs, chosen, blocks, plane, rows, group_step, key_chunk, waits):
    count = len(chosen)
    q_refs, refs = refs[:count], refs[count:]
    kt_ref, v_ref, ks_ref, vs_ref = refs[:4]
    refs = refs[4 + waits :]
    o_ref, refs = refs[0], refs[1:]
    weight_refs, refs = refs[:2], refs[2:]
    score_ref, shift_ref, aux_ref, pos_ref, ks_pad, vs_pad = refs
    me, my_plane, wanted = info[0], info[1], info[2]
    keys = v_ref.shape[0]
    block_rows = count * rows
    tile_rows = group_step * block_rows
    steps = GROUP_QUERIES // group_step
    chunks = keys // key_chunk
    strip = math.gcd(tile_rows, 64)
    spots = [b ^ my_plane if o_ref.shape[0] == plane else n for n, b in enumerate(chosen)]

    ks_pad[...] = jnp.zeros_like(ks_pad)
    vs_pad[...] = jnp.zeros_like(vs_pad)
    ks_pad[0:rows, :] = ks_ref[...]
    vs_pad[0:rows, :] = vs_ref[...]
    row = lax.broadcasted_iota(jnp.int32, (rows, LANES), 0)
    col = lax.broadcasted_iota(jnp.int32, (rows, LANES), 1)
    for i in range(group_step):
        for n, b in enumerate(chosen):
            start = (i * count + n) * rows
            base = ((b ^ my_plane) - me) * rows
            pos_ref[start : start + rows] = jnp.where(col < rows, row - col + base, -(1 << 30))
    lane = lax.broadcasted_iota(jnp.int32, (block_rows, LANES), 1)

    def place(tile):
        return info[3 + lax.div(tile, steps)], lax.rem(tile, steps) * group_step

    def load_queries(tile):
        slot, group = place(tile)
        parts = []
        for i in range(group_step):
            cols = pl.ds(pl.multiple_of((group + i) * HEAD_SIZE, HEAD_SIZE), HEAD_SIZE)
            parts += [q[slot, :, cols] for q in q_refs]
        return jnp.concatenate(parts, axis=0)

    def span_scores(q, tile):
        slot, _ = place(tile)
        start = info[3 + blocks + slot] * (plane * rows)
        scores = lax.dot_general(q, ks_pad[...], (((1,), (1,)), ((), ())), preferred_element_type=F32)
        return jnp.where(pos_ref[...] + start >= 0, scores, MASKED)

    def shift_of(peak):
        top = jnp.max(peak, axis=1, keepdims=True) * LOG2_SCALE
        return jnp.broadcast_to(jnp.maximum(top, LOWEST).astype(BF16).astype(F32), (tile_rows, LANES))

    def finish(tile, shift, total, acc):
        slot, group = place(tile)
        total = jnp.sum(total, axis=1, keepdims=True)
        high = total.astype(BF16).astype(F32)
        low = total - high
        aux = jnp.where(group == 0, 0.0, aux_ref[...])
        for i in range(group_step):
            cols = pl.ds(pl.multiple_of((group + i) * HEAD_SIZE, HEAD_SIZE), HEAD_SIZE)
            part = slice(i * block_rows, (i + 1) * block_rows)
            aux = jnp.where(lane == group + i, shift[part], aux)
            aux = jnp.where(lane == group + i + GROUP_QUERIES, high[part], aux)
            aux = jnp.where(lane == group + i + 2 * GROUP_QUERIES, low[part], aux)
            for n, spot in enumerate(spots):
                start = i * block_rows + n * rows
                o_ref[spot, slot, :, cols] = acc[start : start + rows].astype(BF16)
        aux_ref[...] = aux
        for n, spot in enumerate(spots):
            o_ref[spot, slot, :, GROUP_QUERIES * HEAD_SIZE :] = aux[n * rows : (n + 1) * rows].astype(BF16)

    def score_chunk(q, peak, j):
        part = slice(j * key_chunk, (j + 1) * key_chunk)
        scores = jnp.dot(q, kt_ref[:, part], preferred_element_type=F32)
        score_ref[:, part] = scores
        return jnp.maximum(peak, fold_lanes(jnp.maximum, scores))

    def weigh_chunk(totals, j):
        weight_ref = weight_refs[j % 2]
        for n, r in enumerate(range(0, tile_rows, strip)):
            part = slice(r, r + strip)
            shift = shift_ref[part]
            for c in range(0, key_chunk, LANES):
                start = j * key_chunk + c
                weights = jnp.exp2(score_ref[part, start : start + LANES] * LOG2_SCALE - shift)
                totals[n] = totals[n] + weights
                weight_ref[part, c : c + LANES] = weights.astype(BF16)

    def apply_chunk(acc, j):
        values = v_ref[j * key_chunk : (j + 1) * key_chunk]
        return acc + jnp.dot(weight_refs[j % 2][...], values, preferred_element_type=F32)

    def step(now, later):
        weights = jnp.exp2(score_ref[:, keys:] * LOG2_SCALE - shift_ref[...])
        acc = jnp.dot(weights.astype(BF16), vs_pad[...], preferred_element_type=F32)
        totals = [weights[r : r + strip] for r in range(0, tile_rows, strip)]
        q = load_queries(later)
        peak = span_scores(q, later)
        score_ref[:, keys:] = peak
        for j in range(chunks):
            weigh_chunk(totals, j)
            peak = score_chunk(q, peak, j)
            if j > 0:
                acc = apply_chunk(acc, j - 1)
        acc = apply_chunk(acc, chunks - 1)
        finish(now, shift_ref[...], jnp.concatenate(totals, axis=0), acc)
        shift_ref[...] = shift_of(peak)

    tiles = wanted * steps

    @pl.when(tiles > 0)
    def _():
        q = load_queries(jnp.int32(0))
        peak = span_scores(q, jnp.int32(0))
        score_ref[:, keys:] = peak
        for j in range(chunks):
            peak = score_chunk(q, peak, j)
        shift_ref[...] = shift_of(peak)

        def body(t, _):
            step(t, jnp.minimum(t + 1, tiles - 1))
            return 0

        lax.fori_loop(0, tiles, body, 0)

    def span_only(t, _):
        scores = span_scores(load_queries(t), t)
        shift = shift_of(scores)
        weights = jnp.exp2(scores * LOG2_SCALE - shift)
        acc = jnp.dot(weights.astype(BF16), vs_pad[...], preferred_element_type=F32)
        finish(t, shift, weights, acc)
        return 0

    lax.fori_loop(tiles, blocks * steps, span_only, 0)


def attend_head(info, q_pieces, chosen, q_head, keys_t, values, span_keys, span_values, head, after):
    blocks, rows, _ = q_pieces[0].shape
    plane, count = len(q_pieces), len(chosen)
    cols = GROUP_QUERIES * HEAD_SIZE
    key_count = values.shape[0]
    group_step = min(GROUP_QUERIES, 2 * (plane // count))
    tile_rows = group_step * count * rows
    key_chunk = min(key_count, 512)
    vmem = pltpu.MemorySpace.VMEM
    out_shape = (plane if count > 1 else 1, blocks, rows, cols + LANES)
    span_block = pl.BlockSpec((rows, HEAD_SIZE), lambda i, s: (0, head))
    scored = blocks * count * rows * GROUP_QUERIES * key_count
    return pl.pallas_call(
        functools.partial(
            attend_kernel,
            chosen=chosen,
            blocks=blocks,
            plane=plane,
            rows=rows,
            group_step=group_step,
            key_chunk=key_chunk,
            waits=len(after),
        ),
        grid_spec=pltpu.PrefetchScalarGridSpec(
            num_scalar_prefetch=1,
            grid=(1,),
            in_specs=[pl.BlockSpec((blocks, rows, cols), lambda i, s: (0, 0, q_head))] * count
            + [
                pl.BlockSpec((HEAD_SIZE, key_count), lambda i, s: (0, 0)),
                pl.BlockSpec((key_count, HEAD_SIZE), lambda i, s: (0, head)),
                span_block,
                span_block,
            ]
            + [pl.BlockSpec(memory_space=pl.ANY)] * len(after),
            out_specs=pl.BlockSpec(out_shape, lambda i, s: (0, 0, 0, 0)),
            scratch_shapes=[vmem((tile_rows, key_chunk), BF16)] * 2
            + [
                vmem((tile_rows, key_count + LANES), F32),
                vmem((tile_rows, LANES), F32),
                vmem((count * rows, LANES), F32),
                vmem((tile_rows, LANES), jnp.int32),
                vmem((LANES, HEAD_SIZE), BF16),
                vmem((LANES, HEAD_SIZE), BF16),
            ],
        ),
        out_shape=jax.ShapeDtypeStruct(out_shape, BF16),
        compiler_params=pltpu.CompilerParams(vmem_limit_bytes=ATTEND_VMEM),
        cost_estimate=pl.CostEstimate(
            flops=8 * scored * HEAD_SIZE,
            bytes_accessed=4 * key_count * HEAD_SIZE + 4 * blocks * count * rows * cols,
            transcendentals=scored,
        ),
        name="attend",
    )(info, *[q_pieces[b] for b in chosen], keys_t, values, span_keys, span_values, *after)


def combine(parts):
    width = GROUP_QUERIES * HEAD_SIZE
    aux = [p[:, width:].astype(F32) for p in parts]
    top = functools.reduce(jnp.maximum, aux)
    factors = [jnp.exp2(jnp.minimum(a - top, 0.0)) for a in aux]
    sums = [
        pltpu.roll(a, LANES - GROUP_QUERIES, 1) + pltpu.roll(a, LANES - 2 * GROUP_QUERIES, 1) for a in aux
    ]
    total = sum(f * s for f, s in zip(factors, sums))
    heads = []
    for g in range(GROUP_QUERIES):
        cols = slice(g * HEAD_SIZE, (g + 1) * HEAD_SIZE)
        heads.append(sum(f[:, g : g + 1] * p[:, cols].astype(F32) for f, p in zip(factors, parts)))
    return heads, top, total


def merge_kernel(info, *refs, owned, waits):
    refs, out = list(refs[:-1]), refs[-1]
    width = GROUP_QUERIES * HEAD_SIZE
    blocks = out.shape[0]
    for h, alone in enumerate(owned):
        got = refs.pop(0)
        own = refs.pop(0) if alone else None
        first = h * (width + LANES)
        for a in range(blocks):
            at = info[3 + blocks + a]
            pieces = [got[b ^ info[1], a] for b in range(1 if alone else 0, got.shape[0])]
            parts, top, total = combine(pieces + ([own[0, a]] if alone else []))
            for g, x in enumerate(parts):
                out[at, :, first + g * HEAD_SIZE : first + (g + 1) * HEAD_SIZE] = x.astype(BF16)
            lane = lax.broadcasted_iota(jnp.int32, top.shape, 1)
            high = total.astype(BF16).astype(F32)
            aux = jnp.where(
                lane < GROUP_QUERIES,
                top,
                jnp.where(
                    lane < 2 * GROUP_QUERIES,
                    pltpu.roll(high, GROUP_QUERIES, 1),
                    pltpu.roll(total - high, 2 * GROUP_QUERIES, 1),
                ),
            )
            aux = jnp.where(lane < 3 * GROUP_QUERIES, aux, 0.0)
            out[at, :, first + width : first + width + LANES] = aux.astype(BF16)


def normalize_kernel(got, *refs, heads):
    out = refs[-1]
    width = GROUP_QUERIES * HEAD_SIZE
    for h in range(heads):
        first = h * (width + LANES)
        parts, _, total = combine([got[a, :, first : first + width + LANES] for a in range(got.shape[0])])
        for g, x in enumerate(parts):
            start = h * width + g * HEAD_SIZE
            row = (x / total[:, g : g + 1]).astype(BF16)
            for a in range(out.shape[0]):
                out[a, :, start : start + HEAD_SIZE] = row


def merge_pieces(info, pieces, after):
    _, blocks, rows, cols = pieces[0][0].shape
    arrays = [p for parts in pieces for p in parts]
    return pl.pallas_call(
        functools.partial(merge_kernel, owned=[len(parts) > 1 for parts in pieces], waits=len(after)),
        in_specs=[pl.BlockSpec(memory_space=pltpu.MemorySpace.SMEM)]
        + [pl.BlockSpec(memory_space=pltpu.MemorySpace.VMEM)] * len(arrays)
        + [pl.BlockSpec(memory_space=pl.ANY)] * len(after),
        out_shape=jax.ShapeDtypeStruct((blocks, rows, len(pieces) * cols), BF16),
        compiler_params=pltpu.CompilerParams(vmem_limit_bytes=SHORT_VMEM),
        cost_estimate=SHORT,
        name="merge",
    )(info, *arrays, *after)


def normalize_pieces(got, after):
    blocks, rows, cols = got.shape
    heads = cols // (GROUP_QUERIES * HEAD_SIZE + LANES)
    return pl.pallas_call(
        functools.partial(normalize_kernel, heads=heads),
        in_specs=[pl.BlockSpec(memory_space=pltpu.MemorySpace.VMEM)]
        + [pl.BlockSpec(memory_space=pl.ANY)] * len(after),
        out_shape=jax.ShapeDtypeStruct((blocks, rows, cols - heads * LANES), BF16),
        compiler_params=pltpu.CompilerParams(vmem_limit_bytes=SHORT_VMEM),
        cost_estimate=SHORT,
        name="normalize",
    )(got, *after)


def project_kernel(x_ref, w_ref, *refs):
    *base_ref, out = refs
    plane, blocks, rows, width = x_ref.shape
    for b in range(plane):
        y = jnp.dot(x_ref[b].reshape(blocks * rows, width), w_ref[...], preferred_element_type=F32)
        for a in range(blocks):
            part = y[a * rows : (a + 1) * rows]
            out[a, b] = ((base_ref[0][a, b] + part) if base_ref else part).astype(out.dtype)


def project(gathered, weight, group, base, dtype):
    plane, blocks, rows, width = gathered.shape
    out_cols = weight.shape[1]
    span = plane * blocks * rows
    out_block = pl.BlockSpec((blocks, plane, rows, out_cols), lambda i: (0, 0, 0, 0))
    return pl.pallas_call(
        project_kernel,
        grid=(1,),
        in_specs=[
            pl.BlockSpec((plane, blocks, rows, width), lambda i: (0, 0, 0, 0)),
            pl.BlockSpec((width, out_cols), lambda i: (group, 0)),
        ]
        + [out_block] * len(base),
        out_specs=out_block,
        out_shape=jax.ShapeDtypeStruct((blocks, plane, rows, out_cols), dtype),
        compiler_params=pltpu.CompilerParams(vmem_limit_bytes=SHORT_VMEM),
        cost_estimate=pl.CostEstimate(
            flops=2 * span * width * out_cols,
            bytes_accessed=2 * (width * out_cols + span * width),
            transcendentals=0,
        ),
        name="project",
    )(gathered, weight, *base)


def exchange(x, axis, distance):
    count = lax.axis_size(axis)
    return lax.ppermute(x, axis, [(i, i ^ distance) for i in range(count)])


def local(queries, span_keys, span_values, context_keys, context_values, selected, out_weight):
    ctx_count, me = lax.axis_size("ctx"), lax.axis_index("ctx")
    head_count, my_head = lax.axis_size("head"), lax.axis_index("head")
    blocks = selected.shape[0]
    plane = ctx_count // blocks
    rows = queries.shape[0]
    heads = context_keys.shape[1] // HEAD_SIZE
    width = GROUP_QUERIES * HEAD_SIZE

    slot_block = lax.div(me, plane) ^ jnp.arange(blocks, dtype=jnp.int32)
    wanted = jnp.any(selected == me, axis=1)[slot_block]
    order = jnp.argsort(jnp.logical_not(wanted), stable=True).astype(jnp.int32)
    info = jnp.concatenate(
        [
            jnp.stack([me, lax.rem(me, plane), jnp.sum(wanted)]).astype(jnp.int32),
            order,
            slot_block.astype(jnp.int32),
        ]
    )

    def stack_blocks(x):
        return jnp.stack([x] + [exchange(x, "ctx", a * plane) for a in range(1, blocks)])

    planes = [[z * plane + p for p in range(plane)] for z in range(blocks)]
    columns = [[z * plane + p for z in range(blocks)] for p in range(plane)]

    def swap(x, groups):
        return lax.all_to_all(x, "ctx", 0, 0, axis_index_groups=groups, tiled=True)

    def gather_plane(stack):
        return [stack] + [exchange(stack, "ctx", b) for b in range(1, plane)]

    first = stack_blocks(queries[:, :width])
    sources, stacks = [(gather_plane(first), 0)], []
    keys, _ = lax.optimization_barrier((context_keys, first))
    keys_t = [
        (keys if h else context_keys)[:, h * HEAD_SIZE : (h + 1) * HEAD_SIZE].T for h in range(heads)
    ]
    if heads > 1:
        held, _ = lax.optimization_barrier((queries[:, width:], first))
        stacks = [stack_blocks(held)]
        pieces = gather_plane(stacks[0])
        sources += [(pieces, i) for i in range(heads - 1)]

    size = 2 if heads % 2 == 0 else 1
    attended, merged, rows_of = [], [], []

    def merge(after):
        group = range(len(merged) * size, (len(merged) + 1) * size)
        parts = [[swap(attended[h][0], planes)] + attended[h][1:] for h in group]
        merged.append(merge_pieces(info, parts, after))
        return [merged[-1]]

    def normalize(after):
        rows_of.append(normalize_pieces(swap(merged[len(rows_of)], columns), after))
        return [rows_of[-1]]

    def attend(h, chosen, after):
        pieces, q_head = sources[h]
        return attend_head(
            info, pieces, chosen, q_head, keys_t[h], context_values, span_keys, span_values, h, after
        )

    latest = stacks
    for h in range(heads):
        start = 1 if h == heads - 1 else 0
        attended.append([attend(h, range(start, plane), latest)])
        latest = attended[h]
        if len(rows_of) < len(merged):
            latest = normalize(latest)
        if start:
            attended[h] = attended[h] + [attend(h, [0], latest)]
            latest = attended[h][1:]
        if h >= (len(merged) + 1) * size:
            latest = merge(latest)
    while len(merged) < heads // size:
        latest = merge(latest)
    while len(rows_of) < heads // size:
        latest = normalize(latest)

    total = []
    for g, rows_now in enumerate(rows_of):
        if g < len(rows_of) - 1:
            rows_now, _ = lax.optimization_barrier((rows_now, attended[-1][-1]))
        column = swap(rows_now, columns)
        gathered = swap(jnp.broadcast_to(column, (plane, *column.shape)), planes)
        total = [project(gathered, out_weight, g, total, BF16 if g == len(rows_of) - 1 else F32)]
    partial_out = total[0].reshape(ctx_count * rows, -1)
    share = partial_out.shape[0] // head_count
    total = lax.dynamic_slice_in_dim(partial_out, my_head * share, share, 0).astype(F32)
    for d in range(1, head_count):
        other = lax.dynamic_slice_in_dim(partial_out, (my_head ^ d) * share, share, 0)
        total = total + exchange(other, "head", d).astype(F32)
    return total.astype(BF16)


def solution(mesh):
    return jax.shard_map(
        local,
        mesh=mesh,
        in_specs=(
            P("ctx", "head"),
            P("ctx", "head"),
            P("ctx", "head"),
            P("ctx", "head"),
            P("ctx", "head"),
            P(),
            P("head", "ctx"),
        ),
        out_specs=P("head", "ctx"),
        check_vma=False,
    )
```

```python
import functools
import math

import jax
import jax.numpy as jnp
import numpy as np
from jax import lax
from jax.experimental import pallas as pl
from jax.experimental.pallas import tpu as pltpu
from jax.sharding import PartitionSpec as P

HEAD_SIZE = 128
GROUP_QUERIES = 8
LANES = 128
LOG2_SCALE = float(HEAD_SIZE**-0.5 * np.log2(np.e))
MASKED = -1e30
LOWEST = -1e20
ATTEND_VMEM = 28 * 1024 * 1024
SHORT_VMEM = 16 * 1024 * 1024

BF16, F32 = jnp.bfloat16, jnp.float32
SHORT = pl.CostEstimate(flops=0, bytes_accessed=0, transcendentals=0)


def fold_lanes(op, x):
    parts = [x[:, i : i + LANES] for i in range(0, x.shape[1], LANES)]
    while len(parts) > 1:
        parts = [op(*parts[i : i + 2]) if i + 1 < len(parts) else parts[i] for i in range(0, len(parts), 2)]
    return parts[0]


def attend_kernel(info, *refs, chosen, blocks, plane, rows, group_step, key_chunk, waits):
    count = len(chosen)
    q_refs, refs = refs[:count], refs[count:]
    kt_ref, v_ref, ks_ref, vs_ref = refs[:4]
    refs = refs[4 + waits :]
    o_refs, refs = refs[:count], refs[count:]
    weight_refs, refs = refs[:2], refs[2:]
    score_ref, shift_ref, aux_ref, pos_ref, ks_pad, vs_pad = refs
    me, my_plane, wanted = info[0], info[1], info[2]
    keys = v_ref.shape[0]
    block_rows = count * rows
    tile_rows = group_step * block_rows
    steps = GROUP_QUERIES // group_step
    chunks = keys // key_chunk
    strip = math.gcd(tile_rows, 64)

    ks_pad[...] = jnp.zeros_like(ks_pad)
    vs_pad[...] = jnp.zeros_like(vs_pad)
    ks_pad[0:rows, :] = ks_ref[...]
    vs_pad[0:rows, :] = vs_ref[...]
    row = lax.broadcasted_iota(jnp.int32, (rows, LANES), 0)
    col = lax.broadcasted_iota(jnp.int32, (rows, LANES), 1)
    for i in range(group_step):
        for n, b in enumerate(chosen):
            start = (i * count + n) * rows
            base = ((b ^ my_plane) - me) * rows
            pos_ref[start : start + rows] = jnp.where(col < rows, row - col + base, -(1 << 30))
    lane = lax.broadcasted_iota(jnp.int32, (block_rows, LANES), 1)

    def place(tile):
        return info[3 + lax.div(tile, steps)], lax.rem(tile, steps) * group_step

    def load_queries(tile):
        slot, group = place(tile)
        parts = []
        for i in range(group_step):
            cols = pl.ds(pl.multiple_of((group + i) * HEAD_SIZE, HEAD_SIZE), HEAD_SIZE)
            parts += [q[slot, :, cols] for q in q_refs]
        return jnp.concatenate(parts, axis=0)

    def span_scores(q, tile):
        slot, _ = place(tile)
        start = info[3 + blocks + slot] * (plane * rows)
        scores = lax.dot_general(q, ks_pad[...], (((1,), (1,)), ((), ())), preferred_element_type=F32)
        return jnp.where(pos_ref[...] + start >= 0, scores, MASKED)

    def shift_of(peak):
        top = jnp.max(peak, axis=1, keepdims=True) * LOG2_SCALE
        return jnp.broadcast_to(jnp.maximum(top, LOWEST).astype(BF16).astype(F32), (tile_rows, LANES))

    def finish(tile, shift, total, acc):
        slot, group = place(tile)
        total = jnp.sum(total, axis=1, keepdims=True)
        high = total.astype(BF16).astype(F32)
        low = total - high
        aux = jnp.where(group == 0, 0.0, aux_ref[...])
        for i in range(group_step):
            cols = pl.ds(pl.multiple_of((group + i) * HEAD_SIZE, HEAD_SIZE), HEAD_SIZE)
            part = slice(i * block_rows, (i + 1) * block_rows)
            aux = jnp.where(lane == group + i, shift[part], aux)
            aux = jnp.where(lane == group + i + GROUP_QUERIES, high[part], aux)
            aux = jnp.where(lane == group + i + 2 * GROUP_QUERIES, low[part], aux)
            for b, o in enumerate(o_refs):
                start = i * block_rows + b * rows
                o[slot, :, cols] = acc[start : start + rows].astype(BF16)
        aux_ref[...] = aux
        for b, o in enumerate(o_refs):
            o[slot, :, GROUP_QUERIES * HEAD_SIZE :] = aux[b * rows : (b + 1) * rows].astype(BF16)

    def score_chunk(q, peak, j):
        part = slice(j * key_chunk, (j + 1) * key_chunk)
        scores = jnp.dot(q, kt_ref[:, part], preferred_element_type=F32)
        score_ref[:, part] = scores
        return jnp.maximum(peak, fold_lanes(jnp.maximum, scores))

    def weigh_chunk(totals, j):
        weight_ref = weight_refs[j % 2]
        for n, r in enumerate(range(0, tile_rows, strip)):
            part = slice(r, r + strip)
            shift = shift_ref[part]
            for c in range(0, key_chunk, LANES):
                start = j * key_chunk + c
                weights = jnp.exp2(score_ref[part, start : start + LANES] * LOG2_SCALE - shift)
                totals[n] = totals[n] + weights
                weight_ref[part, c : c + LANES] = weights.astype(BF16)

    def apply_chunk(acc, j):
        values = v_ref[j * key_chunk : (j + 1) * key_chunk]
        return acc + jnp.dot(weight_refs[j % 2][...], values, preferred_element_type=F32)

    def step(now, later):
        weights = jnp.exp2(score_ref[:, keys:] * LOG2_SCALE - shift_ref[...])
        acc = jnp.dot(weights.astype(BF16), vs_pad[...], preferred_element_type=F32)
        totals = [weights[r : r + strip] for r in range(0, tile_rows, strip)]
        q = load_queries(later)
        peak = span_scores(q, later)
        score_ref[:, keys:] = peak
        for j in range(chunks):
            weigh_chunk(totals, j)
            peak = score_chunk(q, peak, j)
            if j > 0:
                acc = apply_chunk(acc, j - 1)
        acc = apply_chunk(acc, chunks - 1)
        finish(now, shift_ref[...], jnp.concatenate(totals, axis=0), acc)
        shift_ref[...] = shift_of(peak)

    tiles = wanted * steps

    @pl.when(tiles > 0)
    def _():
        q = load_queries(jnp.int32(0))
        peak = span_scores(q, jnp.int32(0))
        score_ref[:, keys:] = peak
        for j in range(chunks):
            peak = score_chunk(q, peak, j)
        shift_ref[...] = shift_of(peak)

        def body(t, _):
            step(t, jnp.minimum(t + 1, tiles - 1))
            return 0

        lax.fori_loop(0, tiles, body, 0)

    def span_only(t, _):
        scores = span_scores(load_queries(t), t)
        shift = shift_of(scores)
        weights = jnp.exp2(scores * LOG2_SCALE - shift)
        acc = jnp.dot(weights.astype(BF16), vs_pad[...], preferred_element_type=F32)
        finish(t, shift, weights, acc)
        return 0

    lax.fori_loop(tiles, blocks * steps, span_only, 0)


def attend_head(info, q_pieces, chosen, q_head, keys_t, values, span_keys, span_values, head, after):
    blocks, rows, _ = q_pieces[0].shape
    plane, count = len(q_pieces), len(chosen)
    cols = GROUP_QUERIES * HEAD_SIZE
    key_count = values.shape[0]
    group_step = min(GROUP_QUERIES, 4 * (plane // count))
    tile_rows = group_step * count * rows
    key_chunk = min(key_count, 512)
    vmem = pltpu.MemorySpace.VMEM
    span_block = pl.BlockSpec((rows, HEAD_SIZE), lambda i, s: (0, head))
    scored = blocks * count * rows * GROUP_QUERIES * key_count
    return pl.pallas_call(
        functools.partial(
            attend_kernel,
            chosen=chosen,
            blocks=blocks,
            plane=plane,
            rows=rows,
            group_step=group_step,
            key_chunk=key_chunk,
            waits=len(after),
        ),
        grid_spec=pltpu.PrefetchScalarGridSpec(
            num_scalar_prefetch=1,
            grid=(1,),
            in_specs=[pl.BlockSpec((blocks, rows, cols), lambda i, s: (0, 0, q_head))] * count
            + [
                pl.BlockSpec((HEAD_SIZE, key_count), lambda i, s: (head, 0)),
                pl.BlockSpec((key_count, HEAD_SIZE), lambda i, s: (0, head)),
                span_block,
                span_block,
            ]
            + [pl.BlockSpec(memory_space=pl.ANY)] * len(after),
            out_specs=[pl.BlockSpec((blocks, rows, cols + LANES), lambda i, s: (0, 0, 0))] * count,
            scratch_shapes=[vmem((tile_rows, key_chunk), BF16)] * 2
            + [
                vmem((tile_rows, key_count + LANES), F32),
                vmem((tile_rows, LANES), F32),
                vmem((count * rows, LANES), F32),
                vmem((tile_rows, LANES), jnp.int32),
                vmem((LANES, HEAD_SIZE), BF16),
                vmem((LANES, HEAD_SIZE), BF16),
            ],
        ),
        out_shape=[jax.ShapeDtypeStruct((blocks, rows, cols + LANES), BF16)] * count,
        compiler_params=pltpu.CompilerParams(vmem_limit_bytes=ATTEND_VMEM),
        cost_estimate=pl.CostEstimate(
            flops=8 * scored * HEAD_SIZE,
            bytes_accessed=4 * key_count * HEAD_SIZE + 4 * blocks * count * rows * cols,
            transcendentals=scored,
        ),
        name="attend",
    )(info, *[q_pieces[b] for b in chosen], keys_t, values, span_keys, span_values, *after)


def combine(parts):
    width = GROUP_QUERIES * HEAD_SIZE
    aux = [p[:, width:].astype(F32) for p in parts]
    top = functools.reduce(jnp.maximum, aux)
    factors = [jnp.exp2(jnp.minimum(a - top, 0.0)) for a in aux]
    sums = [
        pltpu.roll(a, LANES - GROUP_QUERIES, 1) + pltpu.roll(a, LANES - 2 * GROUP_QUERIES, 1) for a in aux
    ]
    total = sum(f * s for f, s in zip(factors, sums))
    heads = []
    for g in range(GROUP_QUERIES):
        cols = slice(g * HEAD_SIZE, (g + 1) * HEAD_SIZE)
        heads.append(sum(f[:, g : g + 1] * p[:, cols].astype(F32) for f, p in zip(factors, parts)))
    return heads, top, total


def merge_kernel(*refs, heads, plane, waits):
    ins, outs = refs[: heads * plane], refs[heads * plane + waits :]
    width = GROUP_QUERIES * HEAD_SIZE
    for h in range(heads):
        first = h * (width + LANES)
        for a, out in enumerate(outs):
            parts, top, total = combine([p[a] for p in ins[h * plane : (h + 1) * plane]])
            for g, x in enumerate(parts):
                out[:, first + g * HEAD_SIZE : first + (g + 1) * HEAD_SIZE] = x.astype(BF16)
            lane = lax.broadcasted_iota(jnp.int32, top.shape, 1)
            high = total.astype(BF16).astype(F32)
            aux = jnp.where(
                lane < GROUP_QUERIES,
                top,
                jnp.where(
                    lane < 2 * GROUP_QUERIES,
                    pltpu.roll(high, GROUP_QUERIES, 1),
                    pltpu.roll(total - high, 2 * GROUP_QUERIES, 1),
                ),
            )
            aux = jnp.where(lane < 3 * GROUP_QUERIES, aux, 0.0)
            out[:, first + width : first + width + LANES] = aux.astype(BF16)


def normalize_kernel(*refs, heads, count):
    ins, out = refs[:count], refs[-1]
    width = GROUP_QUERIES * HEAD_SIZE
    for h in range(heads):
        first = h * (width + LANES)
        parts, _, total = combine([p[:, first : first + width + LANES] for p in ins])
        for g, x in enumerate(parts):
            start = h * width + g * HEAD_SIZE
            out[:, start : start + HEAD_SIZE] = (x / total[:, g : g + 1]).astype(BF16)


def waiting_specs(count, waits):
    whole = pl.BlockSpec(memory_space=pltpu.MemorySpace.VMEM)
    return [whole] * count + [pl.BlockSpec(memory_space=pl.ANY)] * waits


def merge_pieces(pieces, after):
    heads, plane = len(pieces), len(pieces[0])
    blocks, rows, cols = pieces[0][0].shape
    return pl.pallas_call(
        functools.partial(merge_kernel, heads=heads, plane=plane, waits=len(after)),
        in_specs=waiting_specs(heads * plane, len(after)),
        out_shape=[jax.ShapeDtypeStruct((rows, heads * cols), BF16)] * blocks,
        compiler_params=pltpu.CompilerParams(vmem_limit_bytes=SHORT_VMEM),
        cost_estimate=SHORT,
        name="merge",
    )(*[p for own in pieces for p in own], *after)


def normalize_pieces(pieces, after):
    rows, cols = pieces[0].shape
    heads = cols // (GROUP_QUERIES * HEAD_SIZE + LANES)
    return pl.pallas_call(
        functools.partial(normalize_kernel, heads=heads, count=len(pieces)),
        in_specs=waiting_specs(len(pieces), len(after)),
        out_shape=jax.ShapeDtypeStruct((rows, cols - heads * LANES), BF16),
        compiler_params=pltpu.CompilerParams(vmem_limit_bytes=SHORT_VMEM),
        cost_estimate=SHORT,
        name="normalize",
    )(*pieces, *after)


def project_kernel(info, *refs, order, chosen, rows, width):
    ins, (w_ref, *base_ref, out) = refs[: len(chosen)], refs[len(chosen) :]
    out[...] = base_ref[0][...].astype(out.dtype) if base_ref else jnp.zeros_like(out)
    for x_ref, b in zip(ins, chosen):
        x = x_ref[...].reshape(len(order) * rows, width)
        y = jnp.dot(x, w_ref[...], preferred_element_type=F32)
        for n, a in enumerate(order):
            at = (info[3 + len(order) + a], b ^ info[1])
            part = y[n * rows : (n + 1) * rows]
            out[at] = ((base_ref[0][at] + part) if base_ref else part).astype(out.dtype)


def project(info, pieces, order, chosen, weight, group, base, dtype):
    plane = len(pieces)
    blocks, rows, width = pieces[0].shape
    out_cols = weight.shape[1]
    span = len(chosen) * blocks * rows
    whole = pl.BlockSpec((blocks, rows, width), lambda i, s: (0, 0, 0))
    out_block = pl.BlockSpec((blocks, plane, rows, out_cols), lambda i, s: (0, 0, 0, 0))
    return pl.pallas_call(
        functools.partial(project_kernel, order=order, chosen=chosen, rows=rows, width=width),
        grid_spec=pltpu.PrefetchScalarGridSpec(
            num_scalar_prefetch=1,
            grid=(1,),
            in_specs=[whole] * len(chosen)
            + [pl.BlockSpec((width, out_cols), lambda i, s: (group, 0))]
            + [out_block] * len(base),
            out_specs=out_block,
        ),
        out_shape=jax.ShapeDtypeStruct((blocks, plane, rows, out_cols), dtype),
        compiler_params=pltpu.CompilerParams(vmem_limit_bytes=SHORT_VMEM),
        cost_estimate=pl.CostEstimate(
            flops=2 * span * width * out_cols,
            bytes_accessed=2 * (width * out_cols + span * width),
            transcendentals=0,
        ),
        name="project",
    )(info, *[pieces[b] for b in chosen], weight, *base)


def exchange(x, axis, distance):
    count = lax.axis_size(axis)
    return lax.ppermute(x, axis, [(i, i ^ distance) for i in range(count)])


def local(queries, span_keys, span_values, context_keys, context_values, selected, out_weight):
    ctx_count, me = lax.axis_size("ctx"), lax.axis_index("ctx")
    head_count, my_head = lax.axis_size("head"), lax.axis_index("head")
    blocks = selected.shape[0]
    plane = ctx_count // blocks
    rows = queries.shape[0]
    heads = context_keys.shape[1] // HEAD_SIZE
    width = GROUP_QUERIES * HEAD_SIZE

    slot_block = lax.div(me, plane) ^ jnp.arange(blocks, dtype=jnp.int32)
    wanted = jnp.any(selected == me, axis=1)[slot_block]
    order = jnp.argsort(jnp.logical_not(wanted), stable=True).astype(jnp.int32)
    info = jnp.concatenate(
        [
            jnp.stack([me, lax.rem(me, plane), jnp.sum(wanted)]).astype(jnp.int32),
            order,
            slot_block.astype(jnp.int32),
        ]
    )

    def stack_blocks(x):
        return jnp.stack([x] + [exchange(x, "ctx", a * plane) for a in range(1, blocks)])

    def doubled(column):
        stack, order, distance = column
        if not distance:
            return column
        stack = jnp.concatenate([stack, exchange(stack, "ctx", distance * plane)])
        return stack, order + [a ^ distance for a in order], distance // 2

    def gather_plane(stack):
        return [stack] + [exchange(stack, "ctx", b) for b in range(1, plane)]

    first = stack_blocks(queries[:, :width])
    sources, stacks = [(gather_plane(first), 0)], []
    keys, _ = lax.optimization_barrier((context_keys, first))
    keys_t = keys.T
    if heads > 1:
        held, _ = lax.optimization_barrier((queries[:, width:], first))
        stacks = [stack_blocks(held)]
        pieces = gather_plane(stacks[0])
        sources += [(pieces, i) for i in range(heads - 1)]

    size = 2 if heads % 2 == 0 else 1
    attended, merged, rows_of = [], [], []

    received = {}

    def receive(h):
        if h not in received:
            received[h] = [exchange(x, "ctx", b) for b, x in zip(range(1, plane), attended[h][1 - plane :])]
        return received[h]

    def merge(after):
        group = range(len(merged) * size, (len(merged) + 1) * size)
        parts = [[attended[h][0]] + receive(h) for h in group]
        merged.append(merge_pieces(parts, after))
        return [merged[-1][0]]

    def normalize(after):
        own = merged[len(rows_of)]
        parts = [own[0]] + [exchange(own[a], "ctx", a * plane) for a in range(1, blocks)]
        rows_of.append(normalize_pieces(parts, after))
        return [rows_of[-1]]

    def attend(h, chosen, after):
        pieces, q_head = sources[h]
        return attend_head(
            info, pieces, chosen, q_head, keys_t, context_values, span_keys, span_values, h, after
        )

    latest = stacks
    for h in range(heads):
        start = 1 if h == heads - 1 else 0
        attended.append(attend(h, range(start, plane), latest))
        latest = [attended[h][0]]
        if len(rows_of) < len(merged):
            latest = normalize(latest)
        if start:
            before = receive(h - 1) if h else []
            attended[h] = attend(h, [0], latest + before) + attended[h]
            latest = [attended[h][0]]
        if h >= (len(merged) + 1) * size:
            latest = merge(latest)
    columns = []

    def gather_round():
        columns.extend((x[None], [0], blocks // 2) for x in rows_of[len(columns) :])
        if len(merged) == heads // size and columns:
            held, _ = lax.optimization_barrier(([column[0] for column in columns], merged[-1][0]))
            columns[:] = [(x, *column[1:]) for x, column in zip(held, columns)]
        columns[:] = [doubled(column) for column in columns]
        return [column[0] for column in columns]

    while len(merged) < heads // size:
        latest = merge(latest + gather_round())
    while len(rows_of) < heads // size:
        latest = normalize(latest + gather_round())
    while any(distance for _, _, distance in columns) or len(columns) < len(rows_of):
        gather_round()

    total = []
    for g, (stack, order, _) in enumerate(columns):
        if g:
            stack, _ = lax.optimization_barrier((stack, pieces))
        pieces = gather_plane(stack)
        if g < len(rows_of) - 1:
            total = [project(info, pieces, order, range(plane), out_weight, g, total, F32)]
        else:
            total = [project(info, pieces, order, range(plane // 2), out_weight, g, total, F32)]
            total = [project(info, pieces, order, range(plane // 2, plane), out_weight, g, total, BF16)]
    partial_out = total[0].reshape(ctx_count * rows, -1)
    share = partial_out.shape[0] // head_count
    total = lax.dynamic_slice_in_dim(partial_out, my_head * share, share, 0).astype(F32)
    for d in range(1, head_count):
        other = lax.dynamic_slice_in_dim(partial_out, (my_head ^ d) * share, share, 0)
        total = total + exchange(other, "head", d).astype(F32)
    return total.astype(BF16)


def solution(mesh):
    return jax.shard_map(
        local,
        mesh=mesh,
        in_specs=(
            P("ctx", "head"),
            P("ctx", "head"),
            P("ctx", "head"),
            P("ctx", "head"),
            P("ctx", "head"),
            P(),
            P("head", "ctx"),
        ),
        out_specs=P("head", "ctx"),
        check_vma=False,
    )
```

```python
import functools
import math

import jax
import jax.numpy as jnp
import numpy as np
from jax import lax
from jax.experimental import pallas as pl
from jax.experimental.pallas import tpu as pltpu
from jax.sharding import PartitionSpec as P

HEAD_SIZE = 128
GROUP_QUERIES = 8
LANES = 128
LOG2_SCALE = float(HEAD_SIZE**-0.5 * np.log2(np.e))
MASKED = -1e30
LOWEST = -1e20
ATTEND_VMEM = 28 * 1024 * 1024
SHORT_VMEM = 16 * 1024 * 1024

BF16, F32 = jnp.bfloat16, jnp.float32
SHORT = pl.CostEstimate(flops=0, bytes_accessed=0, transcendentals=0)


def fold_lanes(op, x):
    parts = [x[:, i : i + LANES] for i in range(0, x.shape[1], LANES)]
    while len(parts) > 1:
        parts = [op(*parts[i : i + 2]) if i + 1 < len(parts) else parts[i] for i in range(0, len(parts), 2)]
    return parts[0]


def attend_kernel(info, *refs, chosen, blocks, plane, rows, group_step, key_chunk, waits):
    count = len(chosen)
    q_refs, refs = refs[:count], refs[count:]
    kt_ref, v_ref, ks_ref, vs_ref = refs[:4]
    refs = refs[4 + waits :]
    o_refs, refs = refs[:count], refs[count:]
    weight_refs, refs = refs[:2], refs[2:]
    score_ref, shift_ref, aux_ref, pos_ref, ks_pad, vs_pad = refs
    me, my_plane, wanted = info[0], info[1], info[2]
    keys = v_ref.shape[0]
    block_rows = count * rows
    tile_rows = group_step * block_rows
    steps = GROUP_QUERIES // group_step
    chunks = keys // key_chunk
    strip = math.gcd(tile_rows, 64)

    ks_pad[...] = jnp.zeros_like(ks_pad)
    vs_pad[...] = jnp.zeros_like(vs_pad)
    ks_pad[0:rows, :] = ks_ref[...]
    vs_pad[0:rows, :] = vs_ref[...]
    row = lax.broadcasted_iota(jnp.int32, (rows, LANES), 0)
    col = lax.broadcasted_iota(jnp.int32, (rows, LANES), 1)
    for i in range(group_step):
        for n, b in enumerate(chosen):
            start = (i * count + n) * rows
            base = ((b ^ my_plane) - me) * rows
            pos_ref[start : start + rows] = jnp.where(col < rows, row - col + base, -(1 << 30))
    lane = lax.broadcasted_iota(jnp.int32, (block_rows, LANES), 1)

    def place(tile):
        return info[3 + lax.div(tile, steps)], lax.rem(tile, steps) * group_step

    def load_queries(tile):
        slot, group = place(tile)
        parts = []
        for i in range(group_step):
            cols = pl.ds(pl.multiple_of((group + i) * HEAD_SIZE, HEAD_SIZE), HEAD_SIZE)
            parts += [q[slot, :, cols] for q in q_refs]
        return jnp.concatenate(parts, axis=0)

    def span_scores(q, tile):
        slot, _ = place(tile)
        start = info[3 + blocks + slot] * (plane * rows)
        scores = lax.dot_general(q, ks_pad[...], (((1,), (1,)), ((), ())), preferred_element_type=F32)
        return jnp.where(pos_ref[...] + start >= 0, scores, MASKED)

    def shift_of(peak):
        top = jnp.max(peak, axis=1, keepdims=True) * LOG2_SCALE
        return jnp.broadcast_to(jnp.maximum(top, LOWEST).astype(BF16).astype(F32), (tile_rows, LANES))

    def finish(tile, shift, total, acc):
        slot, group = place(tile)
        total = jnp.sum(total, axis=1, keepdims=True)
        high = total.astype(BF16).astype(F32)
        low = total - high
        aux = jnp.where(group == 0, 0.0, aux_ref[...])
        for i in range(group_step):
            cols = pl.ds(pl.multiple_of((group + i) * HEAD_SIZE, HEAD_SIZE), HEAD_SIZE)
            part = slice(i * block_rows, (i + 1) * block_rows)
            aux = jnp.where(lane == group + i, shift[part], aux)
            aux = jnp.where(lane == group + i + GROUP_QUERIES, high[part], aux)
            aux = jnp.where(lane == group + i + 2 * GROUP_QUERIES, low[part], aux)
            for b, o in enumerate(o_refs):
                start = i * block_rows + b * rows
                o[slot, :, cols] = acc[start : start + rows].astype(BF16)
        aux_ref[...] = aux
        for b, o in enumerate(o_refs):
            o[slot, :, GROUP_QUERIES * HEAD_SIZE :] = aux[b * rows : (b + 1) * rows].astype(BF16)

    def score_chunk(q, peak, j):
        part = slice(j * key_chunk, (j + 1) * key_chunk)
        scores = jnp.dot(q, kt_ref[:, part], preferred_element_type=F32)
        score_ref[:, part] = scores
        return jnp.maximum(peak, fold_lanes(jnp.maximum, scores))

    def weigh_chunk(totals, j):
        weight_ref = weight_refs[j % 2]
        for n, r in enumerate(range(0, tile_rows, strip)):
            part = slice(r, r + strip)
            shift = shift_ref[part]
            for c in range(0, key_chunk, LANES):
                start = j * key_chunk + c
                weights = jnp.exp2(score_ref[part, start : start + LANES] * LOG2_SCALE - shift)
                totals[n] = totals[n] + weights
                weight_ref[part, c : c + LANES] = weights.astype(BF16)

    def apply_chunk(acc, j):
        values = v_ref[j * key_chunk : (j + 1) * key_chunk]
        return acc + jnp.dot(weight_refs[j % 2][...], values, preferred_element_type=F32)

    def step(now, later):
        weights = jnp.exp2(score_ref[:, keys:] * LOG2_SCALE - shift_ref[...])
        acc = jnp.dot(weights.astype(BF16), vs_pad[...], preferred_element_type=F32)
        totals = [weights[r : r + strip] for r in range(0, tile_rows, strip)]
        q = load_queries(later)
        peak = span_scores(q, later)
        score_ref[:, keys:] = peak
        for j in range(chunks):
            weigh_chunk(totals, j)
            peak = score_chunk(q, peak, j)
            if j > 0:
                acc = apply_chunk(acc, j - 1)
        acc = apply_chunk(acc, chunks - 1)
        finish(now, shift_ref[...], jnp.concatenate(totals, axis=0), acc)
        shift_ref[...] = shift_of(peak)

    tiles = wanted * steps

    @pl.when(tiles > 0)
    def _():
        q = load_queries(jnp.int32(0))
        peak = span_scores(q, jnp.int32(0))
        score_ref[:, keys:] = peak
        for j in range(chunks):
            peak = score_chunk(q, peak, j)
        shift_ref[...] = shift_of(peak)

        def body(t, _):
            step(t, jnp.minimum(t + 1, tiles - 1))
            return 0

        lax.fori_loop(0, tiles, body, 0)

    def span_only(t, _):
        scores = span_scores(load_queries(t), t)
        shift = shift_of(scores)
        weights = jnp.exp2(scores * LOG2_SCALE - shift)
        acc = jnp.dot(weights.astype(BF16), vs_pad[...], preferred_element_type=F32)
        finish(t, shift, weights, acc)
        return 0

    lax.fori_loop(tiles, blocks * steps, span_only, 0)


def attend_head(info, q_pieces, chosen, q_head, keys_t, values, span_keys, span_values, head, after):
    blocks, rows, _ = q_pieces[0].shape
    plane, count = len(q_pieces), len(chosen)
    cols = GROUP_QUERIES * HEAD_SIZE
    key_count = values.shape[0]
    group_step = min(GROUP_QUERIES, 2 * (plane // count))
    tile_rows = group_step * count * rows
    key_chunk = min(key_count, 512)
    vmem = pltpu.MemorySpace.VMEM
    span_block = pl.BlockSpec((rows, HEAD_SIZE), lambda i, s: (0, head))
    scored = blocks * count * rows * GROUP_QUERIES * key_count
    return pl.pallas_call(
        functools.partial(
            attend_kernel,
            chosen=chosen,
            blocks=blocks,
            plane=plane,
            rows=rows,
            group_step=group_step,
            key_chunk=key_chunk,
            waits=len(after),
        ),
        grid_spec=pltpu.PrefetchScalarGridSpec(
            num_scalar_prefetch=1,
            grid=(1,),
            in_specs=[pl.BlockSpec((blocks, rows, cols), lambda i, s: (0, 0, q_head))] * count
            + [
                pl.BlockSpec((HEAD_SIZE, key_count), lambda i, s: (0, 0)),
                pl.BlockSpec((key_count, HEAD_SIZE), lambda i, s: (0, head)),
                span_block,
                span_block,
            ]
            + [pl.BlockSpec(memory_space=pl.ANY)] * len(after),
            out_specs=[pl.BlockSpec((blocks, rows, cols + LANES), lambda i, s: (0, 0, 0))] * count,
            scratch_shapes=[vmem((tile_rows, key_chunk), BF16)] * 2
            + [
                vmem((tile_rows, key_count + LANES), F32),
                vmem((tile_rows, LANES), F32),
                vmem((count * rows, LANES), F32),
                vmem((tile_rows, LANES), jnp.int32),
                vmem((LANES, HEAD_SIZE), BF16),
                vmem((LANES, HEAD_SIZE), BF16),
            ],
        ),
        out_shape=[jax.ShapeDtypeStruct((blocks, rows, cols + LANES), BF16)] * count,
        compiler_params=pltpu.CompilerParams(vmem_limit_bytes=ATTEND_VMEM),
        cost_estimate=pl.CostEstimate(
            flops=8 * scored * HEAD_SIZE,
            bytes_accessed=4 * key_count * HEAD_SIZE + 4 * blocks * count * rows * cols,
            transcendentals=scored,
        ),
        name="attend",
    )(info, *[q_pieces[b] for b in chosen], keys_t, values, span_keys, span_values, *after)


def combine(parts):
    width = GROUP_QUERIES * HEAD_SIZE
    aux = [p[:, width:].astype(F32) for p in parts]
    top = functools.reduce(jnp.maximum, aux)
    factors = [jnp.exp2(jnp.minimum(a - top, 0.0)) for a in aux]
    sums = [
        pltpu.roll(a, LANES - GROUP_QUERIES, 1) + pltpu.roll(a, LANES - 2 * GROUP_QUERIES, 1) for a in aux
    ]
    total = sum(f * s for f, s in zip(factors, sums))
    heads = []
    for g in range(GROUP_QUERIES):
        cols = slice(g * HEAD_SIZE, (g + 1) * HEAD_SIZE)
        heads.append(sum(f[:, g : g + 1] * p[:, cols].astype(F32) for f, p in zip(factors, parts)))
    return heads, top, total


def merge_kernel(*refs, heads, plane, waits):
    ins, outs = refs[: heads * plane], refs[heads * plane + waits :]
    width = GROUP_QUERIES * HEAD_SIZE
    for h in range(heads):
        first = h * (width + LANES)
        for a, out in enumerate(outs):
            parts, top, total = combine([p[a] for p in ins[h * plane : (h + 1) * plane]])
            for g, x in enumerate(parts):
                out[:, first + g * HEAD_SIZE : first + (g + 1) * HEAD_SIZE] = x.astype(BF16)
            lane = lax.broadcasted_iota(jnp.int32, top.shape, 1)
            high = total.astype(BF16).astype(F32)
            aux = jnp.where(
                lane < GROUP_QUERIES,
                top,
                jnp.where(
                    lane < 2 * GROUP_QUERIES,
                    pltpu.roll(high, GROUP_QUERIES, 1),
                    pltpu.roll(total - high, 2 * GROUP_QUERIES, 1),
                ),
            )
            aux = jnp.where(lane < 3 * GROUP_QUERIES, aux, 0.0)
            out[:, first + width : first + width + LANES] = aux.astype(BF16)


def normalize_kernel(*refs, heads, count):
    ins, out = refs[:count], refs[-1]
    width = GROUP_QUERIES * HEAD_SIZE
    for h in range(heads):
        first = h * (width + LANES)
        parts, _, total = combine([p[:, first : first + width + LANES] for p in ins])
        for g, x in enumerate(parts):
            start = h * width + g * HEAD_SIZE
            out[:, start : start + HEAD_SIZE] = (x / total[:, g : g + 1]).astype(BF16)


def waiting_specs(count, waits):
    whole = pl.BlockSpec(memory_space=pltpu.MemorySpace.VMEM)
    return [whole] * count + [pl.BlockSpec(memory_space=pl.ANY)] * waits


def merge_pieces(pieces, after):
    heads, plane = len(pieces), len(pieces[0])
    blocks, rows, cols = pieces[0][0].shape
    return pl.pallas_call(
        functools.partial(merge_kernel, heads=heads, plane=plane, waits=len(after)),
        in_specs=waiting_specs(heads * plane, len(after)),
        out_shape=[jax.ShapeDtypeStruct((rows, heads * cols), BF16)] * blocks,
        compiler_params=pltpu.CompilerParams(vmem_limit_bytes=SHORT_VMEM),
        cost_estimate=SHORT,
        name="merge",
    )(*[p for own in pieces for p in own], *after)


def normalize_pieces(pieces, after):
    rows, cols = pieces[0].shape
    heads = cols // (GROUP_QUERIES * HEAD_SIZE + LANES)
    return pl.pallas_call(
        functools.partial(normalize_kernel, heads=heads, count=len(pieces)),
        in_specs=waiting_specs(len(pieces), len(after)),
        out_shape=jax.ShapeDtypeStruct((rows, cols - heads * LANES), BF16),
        compiler_params=pltpu.CompilerParams(vmem_limit_bytes=SHORT_VMEM),
        cost_estimate=SHORT,
        name="normalize",
    )(*pieces, *after)


def project_kernel(info, *refs, order, chosen, rows, width):
    ins, (w_ref, *base_ref, out) = refs[: len(chosen)], refs[len(chosen) :]
    out[...] = base_ref[0][...].astype(out.dtype) if base_ref else jnp.zeros_like(out)
    for x_ref, b in zip(ins, chosen):
        x = x_ref[...].reshape(len(order) * rows, width)
        y = jnp.dot(x, w_ref[...], preferred_element_type=F32)
        for n, a in enumerate(order):
            at = (info[3 + len(order) + a], b ^ info[1])
            part = y[n * rows : (n + 1) * rows]
            out[at] = ((base_ref[0][at] + part) if base_ref else part).astype(out.dtype)


def project(info, pieces, order, chosen, weight, group, base, dtype):
    plane = len(pieces)
    blocks, rows, width = pieces[0].shape
    out_cols = weight.shape[1]
    span = len(chosen) * blocks * rows
    whole = pl.BlockSpec((blocks, rows, width), lambda i, s: (0, 0, 0))
    out_block = pl.BlockSpec((blocks, plane, rows, out_cols), lambda i, s: (0, 0, 0, 0))
    return pl.pallas_call(
        functools.partial(project_kernel, order=order, chosen=chosen, rows=rows, width=width),
        grid_spec=pltpu.PrefetchScalarGridSpec(
            num_scalar_prefetch=1,
            grid=(1,),
            in_specs=[whole] * len(chosen)
            + [pl.BlockSpec((width, out_cols), lambda i, s: (group, 0))]
            + [out_block] * len(base),
            out_specs=out_block,
        ),
        out_shape=jax.ShapeDtypeStruct((blocks, plane, rows, out_cols), dtype),
        compiler_params=pltpu.CompilerParams(vmem_limit_bytes=SHORT_VMEM),
        cost_estimate=pl.CostEstimate(
            flops=2 * span * width * out_cols,
            bytes_accessed=2 * (width * out_cols + span * width),
            transcendentals=0,
        ),
        name="project",
    )(info, *[pieces[b] for b in chosen], weight, *base)


def exchange(x, axis, distance):
    count = lax.axis_size(axis)
    return lax.ppermute(x, axis, [(i, i ^ distance) for i in range(count)])


def local(queries, span_keys, span_values, context_keys, context_values, selected, out_weight):
    ctx_count, me = lax.axis_size("ctx"), lax.axis_index("ctx")
    head_count, my_head = lax.axis_size("head"), lax.axis_index("head")
    blocks = selected.shape[0]
    plane = ctx_count // blocks
    rows = queries.shape[0]
    heads = context_keys.shape[1] // HEAD_SIZE
    width = GROUP_QUERIES * HEAD_SIZE

    slot_block = lax.div(me, plane) ^ jnp.arange(blocks, dtype=jnp.int32)
    wanted = jnp.any(selected == me, axis=1)[slot_block]
    order = jnp.argsort(jnp.logical_not(wanted), stable=True).astype(jnp.int32)
    info = jnp.concatenate(
        [
            jnp.stack([me, lax.rem(me, plane), jnp.sum(wanted)]).astype(jnp.int32),
            order,
            slot_block.astype(jnp.int32),
        ]
    )

    def doubled(column):
        stack, order, distance = column
        if not distance:
            return column
        stack = jnp.concatenate([stack, exchange(stack, "ctx", distance * plane)])
        return stack, order + [a ^ distance for a in order], distance // 2

    def stack_blocks(x):
        return jnp.stack([x] + [exchange(x, "ctx", a * plane) for a in range(1, blocks)])

    def gather_plane(stack):
        return [stack] + [exchange(stack, "ctx", b) for b in range(1, plane)]

    first = stack_blocks(queries[:, :width])
    sources, stacks = [(gather_plane(first), 0)], []
    keys_t = []
    for h in range(heads):
        keys, _ = lax.optimization_barrier(
            (context_keys[:, h * HEAD_SIZE : (h + 1) * HEAD_SIZE], sources[0][0][1] if h else info)
        )
        keys_t.append(keys.T)
    if heads > 1:
        held, _ = lax.optimization_barrier((queries[:, width:], first))
        stacks = [stack_blocks(held)]
        pieces = gather_plane(stacks[0])
        sources += [(pieces, i) for i in range(heads - 1)]

    size = 2 if heads % 2 == 0 else 1
    attended, merged, rows_of = [], [], []

    received = {}

    def receive(h):
        if h not in received:
            received[h] = [exchange(x, "ctx", b) for b, x in zip(range(1, plane), attended[h][1 - plane :])]
        return received[h]

    def merge(after):
        group = range(len(merged) * size, (len(merged) + 1) * size)
        parts = [[attended[h][0]] + receive(h) for h in group]
        merged.append(merge_pieces(parts, after))
        return [merged[-1][0]]

    def normalize(after):
        own = merged[len(rows_of)]
        parts = [own[0]] + [exchange(own[a], "ctx", a * plane) for a in range(1, blocks)]
        rows_of.append(normalize_pieces(parts, after))
        return [rows_of[-1]]

    def attend(h, chosen, after):
        pieces, q_head = sources[h]
        return attend_head(
            info, pieces, chosen, q_head, keys_t[h], context_values, span_keys, span_values, h, after
        )

    latest = stacks
    for h in range(heads):
        start = 1 if h == heads - 1 else 0
        attended.append(attend(h, range(start, plane), latest))
        latest = [attended[h][0]]
        if len(rows_of) < len(merged):
            latest = normalize(latest)
        if start:
            before = receive(h - 1) if h else []
            attended[h] = attend(h, [0], latest + before) + attended[h]
            latest = [attended[h][0]]
        if h >= (len(merged) + 1) * size:
            latest = merge(latest)
    columns = []

    def gather_round():
        columns.extend((x[None], [0], blocks // 2) for x in rows_of[len(columns) :])
        if len(merged) == heads // size and columns:
            held, *_ = lax.optimization_barrier(
                ([column[0] for column in columns], attended[-1][0], receive(heads - 1))
            )
            columns[:] = [(x, *column[1:]) for x, column in zip(held, columns)]
        columns[:] = [doubled(column) for column in columns]
        return [column[0] for column in columns]

    while len(merged) < heads // size:
        latest = merge(latest + gather_round())
    gathered = []
    while len(rows_of) < heads // size:
        after = gather_round()
        if columns and not columns[0][2]:
            gathered = [gather_plane(after[0])]
            after = [gathered[0][b] for b in (1, 2) if b < plane]
        latest = normalize(latest + after)
    while any(distance for _, _, distance in columns) or len(columns) < len(rows_of):
        gather_round()

    total = []
    for g, (stack, order, _) in enumerate(columns):
        if g:
            stack, _ = lax.optimization_barrier((stack, pieces))
        pieces = gathered.pop() if gathered else gather_plane(stack)
        if g < len(rows_of) - 1:
            total = [project(info, pieces, order, range(plane), out_weight, g, total, F32)]
        else:
            total = [project(info, pieces, order, range(plane // 2), out_weight, g, total, F32)]
            total = [project(info, pieces, order, range(plane // 2, plane), out_weight, g, total, BF16)]
    partial_out = total[0].reshape(ctx_count * rows, -1)
    share = partial_out.shape[0] // head_count
    total = lax.dynamic_slice_in_dim(partial_out, my_head * share, share, 0).astype(F32)
    for d in range(1, head_count):
        other = lax.dynamic_slice_in_dim(partial_out, (my_head ^ d) * share, share, 0)
        total = total + exchange(other, "head", d).astype(F32)
    return total.astype(BF16)


def solution(mesh):
    return jax.shard_map(
        local,
        mesh=mesh,
        in_specs=(
            P("ctx", "head"),
            P("ctx", "head"),
            P("ctx", "head"),
            P("ctx", "head"),
            P("ctx", "head"),
            P(),
            P("head", "ctx"),
        ),
        out_specs=P("head", "ctx"),
        check_vma=False,
    )
```

```python
import functools
import math

import jax
import jax.numpy as jnp
import numpy as np
from jax import lax
from jax.experimental import pallas as pl
from jax.experimental.pallas import tpu as pltpu
from jax.sharding import PartitionSpec as P

HEAD_SIZE = 128
GROUP_QUERIES = 8
LANES = 128
LOG2_SCALE = float(HEAD_SIZE**-0.5 * np.log2(np.e))
MASKED = -1e30
LOWEST = -1e20
ATTEND_VMEM = 28 * 1024 * 1024
SHORT_VMEM = 16 * 1024 * 1024

BF16, F32 = jnp.bfloat16, jnp.float32
SHORT = pl.CostEstimate(flops=0, bytes_accessed=0, transcendentals=0)


def fold_lanes(op, x):
    parts = [x[:, i : i + LANES] for i in range(0, x.shape[1], LANES)]
    while len(parts) > 1:
        parts = [op(*parts[i : i + 2]) if i + 1 < len(parts) else parts[i] for i in range(0, len(parts), 2)]
    return parts[0]


def attend_kernel(info, *refs, chosen, blocks, plane, rows, group_step, key_chunk, waits):
    count = len(chosen)
    q_refs, refs = refs[:count], refs[count:]
    kt_ref, v_ref, ks_ref, vs_ref = refs[:4]
    refs = refs[4 + waits :]
    o_refs, refs = refs[:count], refs[count:]
    weight_refs, refs = refs[:2], refs[2:]
    score_ref, shift_ref, aux_ref, pos_ref, ks_pad, vs_pad = refs
    me, my_plane, wanted = info[0], info[1], info[2]
    keys = v_ref.shape[0]
    block_rows = count * rows
    tile_rows = group_step * block_rows
    steps = GROUP_QUERIES // group_step
    chunks = keys // key_chunk
    strip = math.gcd(tile_rows, 64)

    ks_pad[...] = jnp.zeros_like(ks_pad)
    vs_pad[...] = jnp.zeros_like(vs_pad)
    ks_pad[0:rows, :] = ks_ref[...]
    vs_pad[0:rows, :] = vs_ref[...]
    row = lax.broadcasted_iota(jnp.int32, (rows, LANES), 0)
    col = lax.broadcasted_iota(jnp.int32, (rows, LANES), 1)
    for i in range(group_step):
        for n, b in enumerate(chosen):
            start = (i * count + n) * rows
            base = ((b ^ my_plane) - me) * rows
            pos_ref[start : start + rows] = jnp.where(col < rows, row - col + base, -(1 << 30))
    lane = lax.broadcasted_iota(jnp.int32, (block_rows, LANES), 1)

    def place(tile):
        return info[3 + lax.div(tile, steps)], lax.rem(tile, steps) * group_step

    def load_queries(tile):
        slot, group = place(tile)
        parts = []
        for i in range(group_step):
            cols = pl.ds(pl.multiple_of((group + i) * HEAD_SIZE, HEAD_SIZE), HEAD_SIZE)
            parts += [q[slot, :, cols] for q in q_refs]
        return jnp.concatenate(parts, axis=0)

    def span_scores(q, tile):
        slot, _ = place(tile)
        start = info[3 + blocks + slot] * (plane * rows)
        scores = lax.dot_general(q, ks_pad[...], (((1,), (1,)), ((), ())), preferred_element_type=F32)
        return jnp.where(pos_ref[...] + start >= 0, scores, MASKED)

    def shift_of(peak):
        top = jnp.max(peak, axis=1, keepdims=True) * LOG2_SCALE
        return jnp.broadcast_to(jnp.maximum(top, LOWEST).astype(BF16).astype(F32), (tile_rows, LANES))

    def finish(tile, shift, total, acc):
        slot, group = place(tile)
        total = jnp.sum(total, axis=1, keepdims=True)
        high = total.astype(BF16).astype(F32)
        low = total - high
        aux = jnp.where(group == 0, 0.0, aux_ref[...])
        for i in range(group_step):
            cols = pl.ds(pl.multiple_of((group + i) * HEAD_SIZE, HEAD_SIZE), HEAD_SIZE)
            part = slice(i * block_rows, (i + 1) * block_rows)
            aux = jnp.where(lane == group + i, shift[part], aux)
            aux = jnp.where(lane == group + i + GROUP_QUERIES, high[part], aux)
            aux = jnp.where(lane == group + i + 2 * GROUP_QUERIES, low[part], aux)
            for b, o in enumerate(o_refs):
                start = i * block_rows + b * rows
                o[slot, :, cols] = acc[start : start + rows].astype(BF16)
        aux_ref[...] = aux
        for b, o in enumerate(o_refs):
            o[slot, :, GROUP_QUERIES * HEAD_SIZE :] = aux[b * rows : (b + 1) * rows].astype(BF16)

    def score_chunk(q, peak, j):
        part = slice(j * key_chunk, (j + 1) * key_chunk)
        scores = jnp.dot(q, kt_ref[:, part], preferred_element_type=F32)
        score_ref[:, part] = scores
        return jnp.maximum(peak, fold_lanes(jnp.maximum, scores))

    def weigh_chunk(totals, j):
        weight_ref = weight_refs[j % 2]
        for n, r in enumerate(range(0, tile_rows, strip)):
            part = slice(r, r + strip)
            shift = shift_ref[part]
            for c in range(0, key_chunk, LANES):
                start = j * key_chunk + c
                weights = jnp.exp2(score_ref[part, start : start + LANES] * LOG2_SCALE - shift)
                totals[n] = totals[n] + weights
                weight_ref[part, c : c + LANES] = weights.astype(BF16)

    def apply_chunk(acc, j):
        values = v_ref[j * key_chunk : (j + 1) * key_chunk]
        return acc + jnp.dot(weight_refs[j % 2][...], values, preferred_element_type=F32)

    def step(now, later):
        weights = jnp.exp2(score_ref[:, keys:] * LOG2_SCALE - shift_ref[...])
        acc = jnp.dot(weights.astype(BF16), vs_pad[...], preferred_element_type=F32)
        totals = [weights[r : r + strip] for r in range(0, tile_rows, strip)]
        q = load_queries(later)
        peak = span_scores(q, later)
        score_ref[:, keys:] = peak
        for j in range(chunks):
            weigh_chunk(totals, j)
            peak = score_chunk(q, peak, j)
            if j > 0:
                acc = apply_chunk(acc, j - 1)
        acc = apply_chunk(acc, chunks - 1)
        finish(now, shift_ref[...], jnp.concatenate(totals, axis=0), acc)
        shift_ref[...] = shift_of(peak)

    tiles = wanted * steps

    @pl.when(tiles > 0)
    def _():
        q = load_queries(jnp.int32(0))
        peak = span_scores(q, jnp.int32(0))
        score_ref[:, keys:] = peak
        for j in range(chunks):
            peak = score_chunk(q, peak, j)
        shift_ref[...] = shift_of(peak)

        def body(t, _):
            step(t, jnp.minimum(t + 1, tiles - 1))
            return 0

        lax.fori_loop(0, tiles, body, 0)

    def span_only(t, _):
        scores = span_scores(load_queries(t), t)
        shift = shift_of(scores)
        weights = jnp.exp2(scores * LOG2_SCALE - shift)
        acc = jnp.dot(weights.astype(BF16), vs_pad[...], preferred_element_type=F32)
        finish(t, shift, weights, acc)
        return 0

    lax.fori_loop(tiles, blocks * steps, span_only, 0)


def attend_head(info, q_pieces, chosen, q_head, keys_t, values, span_keys, span_values, head, after):
    blocks, rows, _ = q_pieces[0].shape
    plane, count = len(q_pieces), len(chosen)
    cols = GROUP_QUERIES * HEAD_SIZE
    key_count = values.shape[0]
    group_step = min(GROUP_QUERIES, 2 * (plane // count))
    tile_rows = group_step * count * rows
    key_chunk = min(key_count, 512)
    vmem = pltpu.MemorySpace.VMEM
    span_block = pl.BlockSpec((rows, HEAD_SIZE), lambda i, s: (0, head))
    scored = blocks * count * rows * GROUP_QUERIES * key_count
    return pl.pallas_call(
        functools.partial(
            attend_kernel,
            chosen=chosen,
            blocks=blocks,
            plane=plane,
            rows=rows,
            group_step=group_step,
            key_chunk=key_chunk,
            waits=len(after),
        ),
        grid_spec=pltpu.PrefetchScalarGridSpec(
            num_scalar_prefetch=1,
            grid=(1,),
            in_specs=[pl.BlockSpec((blocks, rows, cols), lambda i, s: (0, 0, q_head))] * count
            + [
                pl.BlockSpec((HEAD_SIZE, key_count), lambda i, s: (head, 0)),
                pl.BlockSpec((key_count, HEAD_SIZE), lambda i, s: (0, head)),
                span_block,
                span_block,
            ]
            + [pl.BlockSpec(memory_space=pl.ANY)] * len(after),
            out_specs=[pl.BlockSpec((blocks, rows, cols + LANES), lambda i, s: (0, 0, 0))] * count,
            scratch_shapes=[vmem((tile_rows, key_chunk), BF16)] * 2
            + [
                vmem((tile_rows, key_count + LANES), F32),
                vmem((tile_rows, LANES), F32),
                vmem((count * rows, LANES), F32),
                vmem((tile_rows, LANES), jnp.int32),
                vmem((LANES, HEAD_SIZE), BF16),
                vmem((LANES, HEAD_SIZE), BF16),
            ],
        ),
        out_shape=[jax.ShapeDtypeStruct((blocks, rows, cols + LANES), BF16)] * count,
        compiler_params=pltpu.CompilerParams(vmem_limit_bytes=ATTEND_VMEM),
        cost_estimate=pl.CostEstimate(
            flops=8 * scored * HEAD_SIZE,
            bytes_accessed=4 * key_count * HEAD_SIZE + 4 * blocks * count * rows * cols,
            transcendentals=scored,
        ),
        name="attend",
    )(info, *[q_pieces[b] for b in chosen], keys_t, values, span_keys, span_values, *after)


def transpose_kernel(x_ref, *refs):
    refs[-1][...] = x_ref[...].T


def transpose_keys(keys, after):
    count, cols = keys.shape
    chunk = min(count, 1024)
    return pl.pallas_call(
        transpose_kernel,
        grid=(count // chunk,),
        in_specs=[pl.BlockSpec((chunk, cols), lambda i: (i, 0))] + [pl.BlockSpec(memory_space=pl.ANY)] * len(after),
        out_specs=pl.BlockSpec((cols, chunk), lambda i: (0, i)),
        out_shape=jax.ShapeDtypeStruct((cols, count), keys.dtype),
        compiler_params=pltpu.CompilerParams(vmem_limit_bytes=SHORT_VMEM),
        cost_estimate=pl.CostEstimate(flops=0, bytes_accessed=4 * keys.size, transcendentals=0),
        name="transpose",
    )(keys, *after)


def combine(parts):
    width = GROUP_QUERIES * HEAD_SIZE
    aux = [p[:, width:].astype(F32) for p in parts]
    top = functools.reduce(jnp.maximum, aux)
    factors = [jnp.exp2(jnp.minimum(a - top, 0.0)) for a in aux]
    sums = [
        pltpu.roll(a, LANES - GROUP_QUERIES, 1) + pltpu.roll(a, LANES - 2 * GROUP_QUERIES, 1) for a in aux
    ]
    total = sum(f * s for f, s in zip(factors, sums))
    heads = []
    for g in range(GROUP_QUERIES):
        cols = slice(g * HEAD_SIZE, (g + 1) * HEAD_SIZE)
        heads.append(sum(f[:, g : g + 1] * p[:, cols].astype(F32) for f, p in zip(factors, parts)))
    return heads, top, total


def merge_kernel(*refs, heads, plane, waits):
    ins, outs = refs[: heads * plane], refs[heads * plane + waits :]
    width = GROUP_QUERIES * HEAD_SIZE
    for h in range(heads):
        first = h * (width + LANES)
        for a, out in enumerate(outs):
            parts, top, total = combine([p[a] for p in ins[h * plane : (h + 1) * plane]])
            for g, x in enumerate(parts):
                out[:, first + g * HEAD_SIZE : first + (g + 1) * HEAD_SIZE] = x.astype(BF16)
            lane = lax.broadcasted_iota(jnp.int32, top.shape, 1)
            high = total.astype(BF16).astype(F32)
            aux = jnp.where(
                lane < GROUP_QUERIES,
                top,
                jnp.where(
                    lane < 2 * GROUP_QUERIES,
                    pltpu.roll(high, GROUP_QUERIES, 1),
                    pltpu.roll(total - high, 2 * GROUP_QUERIES, 1),
                ),
            )
            aux = jnp.where(lane < 3 * GROUP_QUERIES, aux, 0.0)
            out[:, first + width : first + width + LANES] = aux.astype(BF16)


def normalize_kernel(*refs, heads, count):
    ins, out = refs[:count], refs[-1]
    width = GROUP_QUERIES * HEAD_SIZE
    for h in range(heads):
        first = h * (width + LANES)
        parts, _, total = combine([p[:, first : first + width + LANES] for p in ins])
        for g, x in enumerate(parts):
            start = h * width + g * HEAD_SIZE
            out[:, start : start + HEAD_SIZE] = (x / total[:, g : g + 1]).astype(BF16)


def waiting_specs(count, waits):
    whole = pl.BlockSpec(memory_space=pltpu.MemorySpace.VMEM)
    return [whole] * count + [pl.BlockSpec(memory_space=pl.ANY)] * waits


def merge_pieces(pieces, after):
    heads, plane = len(pieces), len(pieces[0])
    blocks, rows, cols = pieces[0][0].shape
    return pl.pallas_call(
        functools.partial(merge_kernel, heads=heads, plane=plane, waits=len(after)),
        in_specs=waiting_specs(heads * plane, len(after)),
        out_shape=[jax.ShapeDtypeStruct((rows, heads * cols), BF16)] * blocks,
        compiler_params=pltpu.CompilerParams(vmem_limit_bytes=SHORT_VMEM),
        cost_estimate=SHORT,
        name="merge",
    )(*[p for own in pieces for p in own], *after)


def normalize_pieces(pieces, after):
    rows, cols = pieces[0].shape
    heads = cols // (GROUP_QUERIES * HEAD_SIZE + LANES)
    return pl.pallas_call(
        functools.partial(normalize_kernel, heads=heads, count=len(pieces)),
        in_specs=waiting_specs(len(pieces), len(after)),
        out_shape=jax.ShapeDtypeStruct((rows, cols - heads * LANES), BF16),
        compiler_params=pltpu.CompilerParams(vmem_limit_bytes=SHORT_VMEM),
        cost_estimate=SHORT,
        name="normalize",
    )(*pieces, *after)


def project_kernel(info, *refs, order, chosen, rows, width):
    ins, (w_ref, *base_ref, out) = refs[: len(chosen)], refs[len(chosen) :]
    out[...] = base_ref[0][...].astype(out.dtype) if base_ref else jnp.zeros_like(out)
    for x_ref, b in zip(ins, chosen):
        x = x_ref[...].reshape(len(order) * rows, width)
        y = jnp.dot(x, w_ref[...], preferred_element_type=F32)
        for n, a in enumerate(order):
            at = (info[3 + len(order) + a], b ^ info[1])
            part = y[n * rows : (n + 1) * rows]
            out[at] = ((base_ref[0][at] + part) if base_ref else part).astype(out.dtype)


def project(info, pieces, order, chosen, weight, group, base, dtype):
    plane = len(pieces)
    blocks, rows, width = pieces[0].shape
    out_cols = weight.shape[1]
    span = len(chosen) * blocks * rows
    whole = pl.BlockSpec((blocks, rows, width), lambda i, s: (0, 0, 0))
    out_block = pl.BlockSpec((blocks, plane, rows, out_cols), lambda i, s: (0, 0, 0, 0))
    return pl.pallas_call(
        functools.partial(project_kernel, order=order, chosen=chosen, rows=rows, width=width),
        grid_spec=pltpu.PrefetchScalarGridSpec(
            num_scalar_prefetch=1,
            grid=(1,),
            in_specs=[whole] * len(chosen)
            + [pl.BlockSpec((width, out_cols), lambda i, s: (group, 0))]
            + [out_block] * len(base),
            out_specs=out_block,
        ),
        out_shape=jax.ShapeDtypeStruct((blocks, plane, rows, out_cols), dtype),
        compiler_params=pltpu.CompilerParams(vmem_limit_bytes=SHORT_VMEM),
        cost_estimate=pl.CostEstimate(
            flops=2 * span * width * out_cols,
            bytes_accessed=2 * (width * out_cols + span * width),
            transcendentals=0,
        ),
        name="project",
    )(info, *[pieces[b] for b in chosen], weight, *base)


def exchange(x, axis, distance):
    count = lax.axis_size(axis)
    return lax.ppermute(x, axis, [(i, i ^ distance) for i in range(count)])


def local(queries, span_keys, span_values, context_keys, context_values, selected, out_weight):
    ctx_count, me = lax.axis_size("ctx"), lax.axis_index("ctx")
    head_count, my_head = lax.axis_size("head"), lax.axis_index("head")
    blocks = selected.shape[0]
    plane = ctx_count // blocks
    rows = queries.shape[0]
    heads = context_keys.shape[1] // HEAD_SIZE
    width = GROUP_QUERIES * HEAD_SIZE

    slot_block = lax.div(me, plane) ^ jnp.arange(blocks, dtype=jnp.int32)
    wanted = jnp.any(selected == me, axis=1)[slot_block]
    order = jnp.argsort(jnp.logical_not(wanted), stable=True).astype(jnp.int32)
    info = jnp.concatenate(
        [
            jnp.stack([me, lax.rem(me, plane), jnp.sum(wanted)]).astype(jnp.int32),
            order,
            slot_block.astype(jnp.int32),
        ]
    )

    def doubled(column):
        stack, order, distance = column
        if not distance:
            return column
        stack = jnp.concatenate([stack, exchange(stack, "ctx", distance * plane)])
        return stack, order + [a ^ distance for a in order], distance // 2

    def stack_blocks(x):
        return jnp.stack([x] + [exchange(x, "ctx", a * plane) for a in range(1, blocks)])

    def gather_plane(stack):
        return [stack] + [exchange(stack, "ctx", b) for b in range(1, plane)]

    first = stack_blocks(queries[:, :width])
    sources, stacks = [(gather_plane(first), 0)], []
    if heads > 1:
        held, _ = lax.optimization_barrier((queries[:, width:], first))
        early = [exchange(held, "ctx", a * plane) for a in range(1, blocks)]
        keys_t = transpose_keys(context_keys, early[:1])
        held, _ = lax.optimization_barrier((held, keys_t))
        stacks = [jnp.stack([held] + early)]
        pieces = gather_plane(stacks[0])
        sources += [(pieces, i) for i in range(heads - 1)]
    else:
        keys_t = transpose_keys(context_keys, [])

    size = 2 if heads % 2 == 0 else 1
    attended, merged, rows_of = [], [], []

    received = {}

    def receive(h):
        if h not in received:
            received[h] = [exchange(x, "ctx", b) for b, x in zip(range(1, plane), attended[h][1 - plane :])]
        return received[h]

    def merge(after):
        group = range(len(merged) * size, (len(merged) + 1) * size)
        parts = [[attended[h][0]] + receive(h) for h in group]
        merged.append(merge_pieces(parts, after))
        return [merged[-1][0]]

    def normalize(after):
        own = merged[len(rows_of)]
        parts = [own[0]] + [exchange(own[a], "ctx", a * plane) for a in range(1, blocks)]
        rows_of.append(normalize_pieces(parts, after))
        return [rows_of[-1]]

    def attend(h, chosen, after):
        pieces, q_head = sources[h]
        return attend_head(
            info, pieces, chosen, q_head, keys_t, context_values, span_keys, span_values, h, after
        )

    latest = stacks
    for h in range(heads):
        start = 1 if h == heads - 1 else 0
        attended.append(attend(h, range(start, plane), latest))
        latest = [attended[h][0]]
        if len(rows_of) < len(merged):
            latest = normalize(latest)
        if start:
            before = receive(h - 1) if h else []
            attended[h] = attend(h, [0], latest + before) + attended[h]
            latest = [attended[h][0]]
        if h >= (len(merged) + 1) * size:
            latest = merge(latest)
    columns = []

    def gather_round():
        columns.extend((x[None], [0], blocks // 2) for x in rows_of[len(columns) :])
        if len(merged) == heads // size and columns:
            held, *_ = lax.optimization_barrier(
                ([column[0] for column in columns], attended[-1][0], receive(heads - 1))
            )
            columns[:] = [(x, *column[1:]) for x, column in zip(held, columns)]
        columns[:] = [doubled(column) for column in columns]
        return [column[0] for column in columns]

    while len(merged) < heads // size:
        latest = merge(latest + gather_round())
    gathered = []
    while len(rows_of) < heads // size:
        after = gather_round()
        if columns and not columns[0][2]:
            gathered = [gather_plane(after[0])]
            after = [gathered[0][b] for b in (1, 2) if b < plane]
        latest = normalize(latest + after)
    while any(distance for _, _, distance in columns) or len(columns) < len(rows_of):
        gather_round()

    total = []
    for g, (stack, order, _) in enumerate(columns):
        if g:
            stack, _ = lax.optimization_barrier((stack, pieces))
        pieces = gathered.pop() if gathered else gather_plane(stack)
        if g < len(rows_of) - 1:
            total = [project(info, pieces, order, range(plane), out_weight, g, total, F32)]
        else:
            total = [project(info, pieces, order, range(plane // 2), out_weight, g, total, F32)]
            total = [project(info, pieces, order, range(plane // 2, plane), out_weight, g, total, BF16)]
    partial_out = total[0].reshape(ctx_count * rows, -1)
    share = partial_out.shape[0] // head_count
    total = lax.dynamic_slice_in_dim(partial_out, my_head * share, share, 0).astype(F32)
    for d in range(1, head_count):
        other = lax.dynamic_slice_in_dim(partial_out, (my_head ^ d) * share, share, 0)
        total = total + exchange(other, "head", d).astype(F32)
    return total.astype(BF16)


def solution(mesh):
    return jax.shard_map(
        local,
        mesh=mesh,
        in_specs=(
            P("ctx", "head"),
            P("ctx", "head"),
            P("ctx", "head"),
            P("ctx", "head"),
            P("ctx", "head"),
            P(),
            P("head", "ctx"),
        ),
        out_specs=P("head", "ctx"),
        check_vma=False,
    )
```

```python
import functools
import math

import jax
import jax.numpy as jnp
import numpy as np
from jax import lax
from jax.experimental import pallas as pl
from jax.experimental.pallas import tpu as pltpu
from jax.sharding import PartitionSpec as P

HEAD_SIZE = 128
GROUP_QUERIES = 8
LANES = 128
LOG2_SCALE = float(HEAD_SIZE**-0.5 * np.log2(np.e))
MASKED = -1e30
LOWEST = -1e20
ATTEND_VMEM = 28 * 1024 * 1024
SHORT_VMEM = 16 * 1024 * 1024

BF16, F32 = jnp.bfloat16, jnp.float32
SHORT = pl.CostEstimate(flops=0, bytes_accessed=0, transcendentals=0)


def fold_lanes(op, x):
    parts = [x[:, i : i + LANES] for i in range(0, x.shape[1], LANES)]
    while len(parts) > 1:
        parts = [op(*parts[i : i + 2]) if i + 1 < len(parts) else parts[i] for i in range(0, len(parts), 2)]
    return parts[0]


def attend_kernel(info, *refs, chosen, blocks, plane, rows, group_step, key_chunk, waits):
    count = len(chosen)
    q_refs, refs = refs[:count], refs[count:]
    kt_ref, v_ref, ks_ref, vs_ref = refs[:4]
    refs = refs[4 + waits :]
    o_refs, refs = refs[:count], refs[count:]
    weight_refs, refs = refs[:2], refs[2:]
    score_ref, shift_ref, aux_ref, pos_ref, ks_pad, vs_pad = refs
    me, my_plane, wanted = info[0], info[1], info[2]
    keys = v_ref.shape[0]
    block_rows = count * rows
    tile_rows = group_step * block_rows
    steps = GROUP_QUERIES // group_step
    chunks = keys // key_chunk
    strip = math.gcd(tile_rows, 64)

    ks_pad[...] = jnp.zeros_like(ks_pad)
    vs_pad[...] = jnp.zeros_like(vs_pad)
    ks_pad[0:rows, :] = ks_ref[...]
    vs_pad[0:rows, :] = vs_ref[...]
    row = lax.broadcasted_iota(jnp.int32, (rows, LANES), 0)
    col = lax.broadcasted_iota(jnp.int32, (rows, LANES), 1)
    for i in range(group_step):
        for n, b in enumerate(chosen):
            start = (i * count + n) * rows
            base = ((b ^ my_plane) - me) * rows
            pos_ref[start : start + rows] = jnp.where(col < rows, row - col + base, -(1 << 30))
    lane = lax.broadcasted_iota(jnp.int32, (block_rows, LANES), 1)

    def place(tile):
        return info[3 + lax.div(tile, steps)], lax.rem(tile, steps) * group_step

    def load_queries(tile):
        slot, group = place(tile)
        parts = []
        for i in range(group_step):
            cols = pl.ds(pl.multiple_of((group + i) * HEAD_SIZE, HEAD_SIZE), HEAD_SIZE)
            parts += [q[slot, :, cols] for q in q_refs]
        return jnp.concatenate(parts, axis=0)

    def span_scores(q, tile):
        slot, _ = place(tile)
        start = info[3 + blocks + slot] * (plane * rows)
        scores = lax.dot_general(q, ks_pad[...], (((1,), (1,)), ((), ())), preferred_element_type=F32)
        return jnp.where(pos_ref[...] + start >= 0, scores, MASKED)

    def shift_of(peak):
        top = jnp.max(peak, axis=1, keepdims=True) * LOG2_SCALE
        return jnp.broadcast_to(jnp.maximum(top, LOWEST).astype(BF16).astype(F32), (tile_rows, LANES))

    def finish(tile, shift, total, acc):
        slot, group = place(tile)
        total = jnp.sum(total, axis=1, keepdims=True)
        high = total.astype(BF16).astype(F32)
        low = total - high
        aux = jnp.where(group == 0, 0.0, aux_ref[...])
        for i in range(group_step):
            cols = pl.ds(pl.multiple_of((group + i) * HEAD_SIZE, HEAD_SIZE), HEAD_SIZE)
            part = slice(i * block_rows, (i + 1) * block_rows)
            aux = jnp.where(lane == group + i, shift[part], aux)
            aux = jnp.where(lane == group + i + GROUP_QUERIES, high[part], aux)
            aux = jnp.where(lane == group + i + 2 * GROUP_QUERIES, low[part], aux)
            for b, o in enumerate(o_refs):
                start = i * block_rows + b * rows
                o[slot, :, cols] = acc[start : start + rows].astype(BF16)
        aux_ref[...] = aux
        for b, o in enumerate(o_refs):
            o[slot, :, GROUP_QUERIES * HEAD_SIZE :] = aux[b * rows : (b + 1) * rows].astype(BF16)

    def score_chunk(q, peak, j):
        part = slice(j * key_chunk, (j + 1) * key_chunk)
        scores = jnp.dot(q, kt_ref[:, part], preferred_element_type=F32)
        score_ref[:, part] = scores
        return jnp.maximum(peak, fold_lanes(jnp.maximum, scores))

    def weigh_chunk(totals, j):
        weight_ref = weight_refs[j % 2]
        for n, r in enumerate(range(0, tile_rows, strip)):
            part = slice(r, r + strip)
            shift = shift_ref[part]
            for c in range(0, key_chunk, LANES):
                start = j * key_chunk + c
                weights = jnp.exp2(score_ref[part, start : start + LANES] * LOG2_SCALE - shift)
                totals[n] = totals[n] + weights
                weight_ref[part, c : c + LANES] = weights.astype(BF16)

    def apply_chunk(acc, j):
        values = v_ref[j * key_chunk : (j + 1) * key_chunk]
        return acc + jnp.dot(weight_refs[j % 2][...], values, preferred_element_type=F32)

    def step(now, later):
        weights = jnp.exp2(score_ref[:, keys:] * LOG2_SCALE - shift_ref[...])
        acc = jnp.dot(weights.astype(BF16), vs_pad[...], preferred_element_type=F32)
        totals = [weights[r : r + strip] for r in range(0, tile_rows, strip)]
        q = load_queries(later)
        peak = span_scores(q, later)
        score_ref[:, keys:] = peak
        for j in range(chunks):
            weigh_chunk(totals, j)
            peak = score_chunk(q, peak, j)
            if j > 0:
                acc = apply_chunk(acc, j - 1)
        acc = apply_chunk(acc, chunks - 1)
        finish(now, shift_ref[...], jnp.concatenate(totals, axis=0), acc)
        shift_ref[...] = shift_of(peak)

    tiles = wanted * steps

    @pl.when(tiles > 0)
    def _():
        q = load_queries(jnp.int32(0))
        peak = span_scores(q, jnp.int32(0))
        score_ref[:, keys:] = peak
        for j in range(chunks):
            peak = score_chunk(q, peak, j)
        shift_ref[...] = shift_of(peak)

        def body(t, _):
            step(t, jnp.minimum(t + 1, tiles - 1))
            return 0

        lax.fori_loop(0, tiles, body, 0)

    def span_only(t, _):
        scores = span_scores(load_queries(t), t)
        shift = shift_of(scores)
        weights = jnp.exp2(scores * LOG2_SCALE - shift)
        acc = jnp.dot(weights.astype(BF16), vs_pad[...], preferred_element_type=F32)
        finish(t, shift, weights, acc)
        return 0

    lax.fori_loop(tiles, blocks * steps, span_only, 0)


def attend_head(info, q_pieces, chosen, q_head, keys_t, values, span_keys, span_values, head, after):
    blocks, rows, _ = q_pieces[0].shape
    plane, count = len(q_pieces), len(chosen)
    cols = GROUP_QUERIES * HEAD_SIZE
    key_count = values.shape[0]
    group_step = min(GROUP_QUERIES, 2 * (plane // count))
    tile_rows = group_step * count * rows
    key_chunk = min(key_count, 256)
    vmem = pltpu.MemorySpace.VMEM
    span_block = pl.BlockSpec((rows, HEAD_SIZE), lambda i, s: (0, head))
    scored = blocks * count * rows * GROUP_QUERIES * key_count
    return pl.pallas_call(
        functools.partial(
            attend_kernel,
            chosen=chosen,
            blocks=blocks,
            plane=plane,
            rows=rows,
            group_step=group_step,
            key_chunk=key_chunk,
            waits=len(after),
        ),
        grid_spec=pltpu.PrefetchScalarGridSpec(
            num_scalar_prefetch=1,
            grid=(1,),
            in_specs=[pl.BlockSpec((blocks, rows, cols), lambda i, s: (0, 0, q_head))] * count
            + [
                pl.BlockSpec((HEAD_SIZE, key_count), lambda i, s: (head, 0)),
                pl.BlockSpec((key_count, HEAD_SIZE), lambda i, s: (0, head)),
                span_block,
                span_block,
            ]
            + [pl.BlockSpec(memory_space=pl.ANY)] * len(after),
            out_specs=[pl.BlockSpec((blocks, rows, cols + LANES), lambda i, s: (0, 0, 0))] * count,
            scratch_shapes=[vmem((tile_rows, key_chunk), BF16)] * 2
            + [
                vmem((tile_rows, key_count + LANES), F32),
                vmem((tile_rows, LANES), F32),
                vmem((count * rows, LANES), F32),
                vmem((tile_rows, LANES), jnp.int32),
                vmem((LANES, HEAD_SIZE), BF16),
                vmem((LANES, HEAD_SIZE), BF16),
            ],
        ),
        out_shape=[jax.ShapeDtypeStruct((blocks, rows, cols + LANES), BF16)] * count,
        compiler_params=pltpu.CompilerParams(vmem_limit_bytes=ATTEND_VMEM),
        cost_estimate=pl.CostEstimate(
            flops=8 * scored * HEAD_SIZE,
            bytes_accessed=4 * key_count * HEAD_SIZE + 4 * blocks * count * rows * cols,
            transcendentals=scored,
        ),
        name="attend",
    )(info, *[q_pieces[b] for b in chosen], keys_t, values, span_keys, span_values, *after)


def transpose_kernel(x_ref, *refs):
    refs[-1][...] = x_ref[...].T


def transpose_keys(keys, after):
    count, cols = keys.shape
    chunk = min(count, 1024)
    return pl.pallas_call(
        transpose_kernel,
        grid=(count // chunk,),
        in_specs=[pl.BlockSpec((chunk, cols), lambda i: (i, 0))] + [pl.BlockSpec(memory_space=pl.ANY)] * len(after),
        out_specs=pl.BlockSpec((cols, chunk), lambda i: (0, i)),
        out_shape=jax.ShapeDtypeStruct((cols, count), keys.dtype),
        compiler_params=pltpu.CompilerParams(vmem_limit_bytes=SHORT_VMEM),
        cost_estimate=pl.CostEstimate(flops=0, bytes_accessed=4 * keys.size, transcendentals=0),
        name="transpose",
    )(keys, *after)


def combine(parts):
    width = GROUP_QUERIES * HEAD_SIZE
    aux = [p[:, width:].astype(F32) for p in parts]
    top = functools.reduce(jnp.maximum, aux)
    factors = [jnp.exp2(jnp.minimum(a - top, 0.0)) for a in aux]
    sums = [
        pltpu.roll(a, LANES - GROUP_QUERIES, 1) + pltpu.roll(a, LANES - 2 * GROUP_QUERIES, 1) for a in aux
    ]
    total = sum(f * s for f, s in zip(factors, sums))
    heads = []
    for g in range(GROUP_QUERIES):
        cols = slice(g * HEAD_SIZE, (g + 1) * HEAD_SIZE)
        heads.append(sum(f[:, g : g + 1] * p[:, cols].astype(F32) for f, p in zip(factors, parts)))
    return heads, top, total


def merge_kernel(*refs, heads, plane, waits):
    ins, outs = refs[: heads * plane], refs[heads * plane + waits :]
    width = GROUP_QUERIES * HEAD_SIZE
    for h in range(heads):
        first = h * (width + LANES)
        for a, out in enumerate(outs):
            parts, top, total = combine([p[a] for p in ins[h * plane : (h + 1) * plane]])
            for g, x in enumerate(parts):
                out[:, first + g * HEAD_SIZE : first + (g + 1) * HEAD_SIZE] = x.astype(BF16)
            lane = lax.broadcasted_iota(jnp.int32, top.shape, 1)
            high = total.astype(BF16).astype(F32)
            aux = jnp.where(
                lane < GROUP_QUERIES,
                top,
                jnp.where(
                    lane < 2 * GROUP_QUERIES,
                    pltpu.roll(high, GROUP_QUERIES, 1),
                    pltpu.roll(total - high, 2 * GROUP_QUERIES, 1),
                ),
            )
            aux = jnp.where(lane < 3 * GROUP_QUERIES, aux, 0.0)
            out[:, first + width : first + width + LANES] = aux.astype(BF16)


def normalize_kernel(*refs, heads, count):
    ins, out = refs[:count], refs[-1]
    width = GROUP_QUERIES * HEAD_SIZE
    for h in range(heads):
        first = h * (width + LANES)
        parts, _, total = combine([p[:, first : first + width + LANES] for p in ins])
        for g, x in enumerate(parts):
            start = h * width + g * HEAD_SIZE
            out[:, start : start + HEAD_SIZE] = (x / total[:, g : g + 1]).astype(BF16)


def waiting_specs(count, waits):
    whole = pl.BlockSpec(memory_space=pltpu.MemorySpace.VMEM)
    return [whole] * count + [pl.BlockSpec(memory_space=pl.ANY)] * waits


def merge_pieces(pieces, after):
    heads, plane = len(pieces), len(pieces[0])
    blocks, rows, cols = pieces[0][0].shape
    return pl.pallas_call(
        functools.partial(merge_kernel, heads=heads, plane=plane, waits=len(after)),
        in_specs=waiting_specs(heads * plane, len(after)),
        out_shape=[jax.ShapeDtypeStruct((rows, heads * cols), BF16)] * blocks,
        compiler_params=pltpu.CompilerParams(vmem_limit_bytes=SHORT_VMEM),
        cost_estimate=SHORT,
        name="merge",
    )(*[p for own in pieces for p in own], *after)


def normalize_pieces(pieces, after):
    rows, cols = pieces[0].shape
    heads = cols // (GROUP_QUERIES * HEAD_SIZE + LANES)
    return pl.pallas_call(
        functools.partial(normalize_kernel, heads=heads, count=len(pieces)),
        in_specs=waiting_specs(len(pieces), len(after)),
        out_shape=jax.ShapeDtypeStruct((rows, cols - heads * LANES), BF16),
        compiler_params=pltpu.CompilerParams(vmem_limit_bytes=SHORT_VMEM),
        cost_estimate=SHORT,
        name="normalize",
    )(*pieces, *after)


def project_kernel(info, *refs, order, chosen, parts, rows):
    ins, (w_ref, *base_ref, out) = list(refs[: sum(parts)]), refs[sum(parts) :]
    out[...] = base_ref[0][...].astype(out.dtype) if base_ref else jnp.zeros_like(out)
    for b, count in zip(chosen, parts):
        y, first = 0.0, 0
        for _ in range(count):
            x_ref = ins.pop(0)
            width = x_ref.shape[-1]
            x = x_ref[...].reshape(len(order) * rows, width)
            y = y + jnp.dot(x, w_ref[first : first + width], preferred_element_type=F32)
            first += width
        for n, a in enumerate(order):
            at = (info[3 + len(order) + a], b ^ info[1])
            part = y[n * rows : (n + 1) * rows]
            out[at] = ((base_ref[0][at] + part) if base_ref else part).astype(out.dtype)


def project(info, pieces, order, chosen, weight, group, base, dtype):
    plane = len(pieces)
    blocks, rows, width = pieces[0][0].shape
    out_cols = weight.shape[1]
    span = len(chosen) * blocks * rows
    arrays = [x for b in chosen for x in pieces[b]]
    out_block = pl.BlockSpec((blocks, plane, rows, out_cols), lambda i, s: (0, 0, 0, 0))
    return pl.pallas_call(
        functools.partial(
            project_kernel, order=order, chosen=chosen, parts=[len(pieces[b]) for b in chosen], rows=rows
        ),
        grid_spec=pltpu.PrefetchScalarGridSpec(
            num_scalar_prefetch=1,
            grid=(1,),
            in_specs=[pl.BlockSpec(x.shape, lambda i, s: (0, 0, 0)) for x in arrays]
            + [pl.BlockSpec((width, out_cols), lambda i, s: (group, 0))]
            + [out_block] * len(base),
            out_specs=out_block,
        ),
        out_shape=jax.ShapeDtypeStruct((blocks, plane, rows, out_cols), dtype),
        compiler_params=pltpu.CompilerParams(vmem_limit_bytes=SHORT_VMEM),
        cost_estimate=pl.CostEstimate(
            flops=2 * span * width * out_cols,
            bytes_accessed=2 * (width * out_cols + span * width),
            transcendentals=0,
        ),
        name="project",
    )(info, *arrays, weight, *base)


def exchange(x, axis, distance):
    count = lax.axis_size(axis)
    return lax.ppermute(x, axis, [(i, i ^ distance) for i in range(count)])


def local(queries, span_keys, span_values, context_keys, context_values, selected, out_weight):
    ctx_count, me = lax.axis_size("ctx"), lax.axis_index("ctx")
    head_count, my_head = lax.axis_size("head"), lax.axis_index("head")
    blocks = selected.shape[0]
    plane = ctx_count // blocks
    rows = queries.shape[0]
    heads = context_keys.shape[1] // HEAD_SIZE
    width = GROUP_QUERIES * HEAD_SIZE

    slot_block = lax.div(me, plane) ^ jnp.arange(blocks, dtype=jnp.int32)
    wanted = jnp.any(selected == me, axis=1)[slot_block]
    order = jnp.argsort(jnp.logical_not(wanted), stable=True).astype(jnp.int32)
    info = jnp.concatenate(
        [
            jnp.stack([me, lax.rem(me, plane), jnp.sum(wanted)]).astype(jnp.int32),
            order,
            slot_block.astype(jnp.int32),
        ]
    )

    def doubled(column):
        stack, order, distance = column
        if not distance:
            return column
        stack = jnp.concatenate([stack, exchange(stack, "ctx", distance * plane)])
        return stack, order + [a ^ distance for a in order], distance // 2

    def stack_blocks(x):
        return jnp.stack([x] + [exchange(x, "ctx", a * plane) for a in range(1, blocks)])

    def gather_plane(stack):
        return [stack] + [exchange(stack, "ctx", b) for b in range(1, plane)]

    def gather_rows(stack):
        if plane != 4:
            return [[x] for x in gather_plane(stack)]
        near = [exchange(stack, "ctx", 1), exchange(stack, "ctx", 2)]
        half = stack.shape[-1] // 2
        far = [exchange(near[0][..., :half], "ctx", 2), exchange(near[1][..., half:], "ctx", 1)]
        return [[stack], [near[0]], [near[1]], far]

    first = stack_blocks(queries[:, :width])
    sources, stacks = [(gather_plane(first), 0)], []
    if heads > 1:
        held, _ = lax.optimization_barrier((queries[:, width:], first))
        early = [exchange(held, "ctx", a * plane) for a in range(1, blocks)]
        keys_t = transpose_keys(context_keys, early[:1])
        held, _ = lax.optimization_barrier((held, keys_t))
        stacks = [jnp.stack([held] + early)]
        pieces = gather_plane(stacks[0])
        sources += [(pieces, i) for i in range(heads - 1)]
    else:
        keys_t = transpose_keys(context_keys, [])

    size = 2 if heads % 2 == 0 else 1
    attended, merged, rows_of = [], [], []

    received = {}

    def receive(h):
        if h not in received:
            received[h] = [exchange(x, "ctx", b) for b, x in zip(range(1, plane), attended[h][1 - plane :])]
        return received[h]

    def merge(after):
        group = range(len(merged) * size, (len(merged) + 1) * size)
        parts = [[attended[h][0]] + receive(h) for h in group]
        merged.append(merge_pieces(parts, after))
        return [merged[-1][0]]

    def normalize(after):
        own = merged[len(rows_of)]
        parts = [own[0]] + [exchange(own[a], "ctx", a * plane) for a in range(1, blocks)]
        rows_of.append(normalize_pieces(parts, after))
        return [rows_of[-1]]

    def attend(h, chosen, after):
        pieces, q_head = sources[h]
        return attend_head(
            info, pieces, chosen, q_head, keys_t, context_values, span_keys, span_values, h, after
        )

    latest = stacks
    for h in range(heads):
        start = 1 if h == heads - 1 else 0
        attended.append(attend(h, range(start, plane), latest))
        latest = [attended[h][0]]
        if len(rows_of) < len(merged):
            latest = normalize(latest)
        if start:
            before = receive(h - 1) if h else []
            attended[h] = attend(h, [0], latest + before) + attended[h]
            latest = [attended[h][0]]
        if h >= (len(merged) + 1) * size:
            latest = merge(latest)
    columns = []

    def gather_round():
        columns.extend((x[None], [0], blocks // 2) for x in rows_of[len(columns) :])
        if len(merged) == heads // size and columns:
            held, *_ = lax.optimization_barrier(
                ([column[0] for column in columns], attended[-1][0], receive(heads - 1))
            )
            columns[:] = [(x, *column[1:]) for x, column in zip(held, columns)]
        columns[:] = [doubled(column) for column in columns]
        return [column[0] for column in columns]

    while len(merged) < heads // size:
        latest = merge(latest + gather_round())
    gathered = []
    while len(rows_of) < heads // size:
        after = gather_round()
        if columns and not columns[0][2]:
            gathered = [gather_rows(after[0])]
            after = [x for b in (1, 2) if b < plane for x in gathered[0][b]]
        latest = normalize(latest + after)
    while any(distance for _, _, distance in columns) or len(columns) < len(rows_of):
        gather_round()

    total = []
    for g, (stack, order, _) in enumerate(columns):
        if g:
            stack, _ = lax.optimization_barrier((stack, pieces))
        pieces = gathered.pop() if gathered else gather_rows(stack)
        if g < len(rows_of) - 1:
            total = [project(info, pieces, order, range(plane), out_weight, g, total, F32)]
        else:
            total = [project(info, pieces, order, range(plane - 1), out_weight, g, total, F32)]
            total = [project(info, pieces, order, range(plane - 1, plane), out_weight, g, total, BF16)]
    partial_out = total[0].reshape(ctx_count * rows, -1)
    share = partial_out.shape[0] // head_count
    total = lax.dynamic_slice_in_dim(partial_out, my_head * share, share, 0).astype(F32)
    for d in range(1, head_count):
        other = lax.dynamic_slice_in_dim(partial_out, (my_head ^ d) * share, share, 0)
        total = total + exchange(other, "head", d).astype(F32)
    return total.astype(BF16)


def solution(mesh):
    return jax.shard_map(
        local,
        mesh=mesh,
        in_specs=(
            P("ctx", "head"),
            P("ctx", "head"),
            P("ctx", "head"),
            P("ctx", "head"),
            P("ctx", "head"),
            P(),
            P("head", "ctx"),
        ),
        out_specs=P("head", "ctx"),
        check_vma=False,
    )
```

```python
import functools
import math

import jax
import jax.numpy as jnp
import numpy as np
from jax import lax
from jax.experimental import pallas as pl
from jax.experimental.pallas import tpu as pltpu
from jax.sharding import PartitionSpec as P

HEAD_SIZE = 128
GROUP_QUERIES = 8
LANES = 128
LOG2_SCALE = float(HEAD_SIZE**-0.5 * np.log2(np.e))
MASKED = -1e30
LOWEST = -1e20
ATTEND_VMEM = 28 * 1024 * 1024
SHORT_VMEM = 16 * 1024 * 1024

BF16, F32 = jnp.bfloat16, jnp.float32
SHORT = pl.CostEstimate(flops=0, bytes_accessed=0, transcendentals=0)


def fold_lanes(op, x):
    parts = [x[:, i : i + LANES] for i in range(0, x.shape[1], LANES)]
    while len(parts) > 1:
        parts = [op(*parts[i : i + 2]) if i + 1 < len(parts) else parts[i] for i in range(0, len(parts), 2)]
    return parts[0]


def attend_kernel(info, *refs, chosen, blocks, plane, rows, group_step, key_chunk, waits):
    count = len(chosen)
    q_refs, refs = refs[:count], refs[count:]
    kt_ref, v_ref, ks_ref, vs_ref = refs[:4]
    refs = refs[4 + waits :]
    o_refs, refs = refs[:count], refs[count:]
    weight_refs, refs = refs[:2], refs[2:]
    score_ref, shift_ref, aux_ref, pos_ref, ks_pad, vs_pad = refs
    me, my_plane, wanted = info[0], info[1], info[2]
    keys = v_ref.shape[0]
    block_rows = count * rows
    tile_rows = group_step * block_rows
    steps = GROUP_QUERIES // group_step
    chunks = keys // key_chunk
    strip = math.gcd(tile_rows, 64)

    ks_pad[...] = jnp.zeros_like(ks_pad)
    vs_pad[...] = jnp.zeros_like(vs_pad)
    ks_pad[0:rows, :] = ks_ref[...]
    vs_pad[0:rows, :] = vs_ref[...]
    row = lax.broadcasted_iota(jnp.int32, (rows, LANES), 0)
    col = lax.broadcasted_iota(jnp.int32, (rows, LANES), 1)
    for i in range(group_step):
        for n, b in enumerate(chosen):
            start = (i * count + n) * rows
            base = ((b ^ my_plane) - me) * rows
            pos_ref[start : start + rows] = jnp.where(col < rows, row - col + base, -(1 << 30))
    lane = lax.broadcasted_iota(jnp.int32, (block_rows, LANES), 1)

    def place(tile):
        return info[3 + lax.div(tile, steps)], lax.rem(tile, steps) * group_step

    def load_queries(tile):
        slot, group = place(tile)
        parts = []
        for i in range(group_step):
            cols = pl.ds(pl.multiple_of((group + i) * HEAD_SIZE, HEAD_SIZE), HEAD_SIZE)
            parts += [q[slot, :, cols] for q in q_refs]
        return jnp.concatenate(parts, axis=0)

    def span_scores(q, tile):
        slot, _ = place(tile)
        start = info[3 + blocks + slot] * (plane * rows)
        scores = lax.dot_general(q, ks_pad[...], (((1,), (1,)), ((), ())), preferred_element_type=F32)
        return jnp.where(pos_ref[...] + start >= 0, scores, MASKED)

    def shift_of(peak):
        top = jnp.max(peak, axis=1, keepdims=True) * LOG2_SCALE
        return jnp.broadcast_to(jnp.maximum(top, LOWEST).astype(BF16).astype(F32), (tile_rows, LANES))

    def finish(tile, shift, total, acc):
        slot, group = place(tile)
        total = jnp.sum(total, axis=1, keepdims=True)
        high = total.astype(BF16).astype(F32)
        low = total - high
        aux = jnp.where(group == 0, 0.0, aux_ref[...])
        for i in range(group_step):
            cols = pl.ds(pl.multiple_of((group + i) * HEAD_SIZE, HEAD_SIZE), HEAD_SIZE)
            part = slice(i * block_rows, (i + 1) * block_rows)
            aux = jnp.where(lane == group + i, shift[part], aux)
            aux = jnp.where(lane == group + i + GROUP_QUERIES, high[part], aux)
            aux = jnp.where(lane == group + i + 2 * GROUP_QUERIES, low[part], aux)
            for b, o in enumerate(o_refs):
                start = i * block_rows + b * rows
                o[slot, :, cols] = acc[start : start + rows].astype(BF16)
        aux_ref[...] = aux
        for b, o in enumerate(o_refs):
            o[slot, :, GROUP_QUERIES * HEAD_SIZE :] = aux[b * rows : (b + 1) * rows].astype(BF16)

    def score_chunk(q, peak, j):
        part = slice(j * key_chunk, (j + 1) * key_chunk)
        scores = jnp.dot(q, kt_ref[:, part], preferred_element_type=F32)
        score_ref[:, part] = scores
        return jnp.maximum(peak, fold_lanes(jnp.maximum, scores))

    def weigh_chunk(totals, j):
        weight_ref = weight_refs[j % 2]
        for n, r in enumerate(range(0, tile_rows, strip)):
            part = slice(r, r + strip)
            shift = shift_ref[part]
            for c in range(0, key_chunk, LANES):
                start = j * key_chunk + c
                weights = jnp.exp2(score_ref[part, start : start + LANES] * LOG2_SCALE - shift)
                totals[n] = totals[n] + weights
                weight_ref[part, c : c + LANES] = weights.astype(BF16)

    def apply_chunk(acc, j):
        values = v_ref[j * key_chunk : (j + 1) * key_chunk]
        return acc + jnp.dot(weight_refs[j % 2][...], values, preferred_element_type=F32)

    def step(now, later):
        weights = jnp.exp2(score_ref[:, keys:] * LOG2_SCALE - shift_ref[...])
        acc = jnp.dot(weights.astype(BF16), vs_pad[...], preferred_element_type=F32)
        totals = [weights[r : r + strip] for r in range(0, tile_rows, strip)]
        q = load_queries(later)
        peak = span_scores(q, later)
        score_ref[:, keys:] = peak
        for j in range(chunks):
            weigh_chunk(totals, j)
            peak = score_chunk(q, peak, j)
            if j > 0:
                acc = apply_chunk(acc, j - 1)
        acc = apply_chunk(acc, chunks - 1)
        finish(now, shift_ref[...], jnp.concatenate(totals, axis=0), acc)
        shift_ref[...] = shift_of(peak)

    tiles = wanted * steps

    @pl.when(tiles > 0)
    def _():
        q = load_queries(jnp.int32(0))
        peak = span_scores(q, jnp.int32(0))
        score_ref[:, keys:] = peak
        for j in range(chunks):
            peak = score_chunk(q, peak, j)
        shift_ref[...] = shift_of(peak)

        unroll = 2 if steps % 2 == 0 and tile_rows % 256 == 0 else 1

        def body(i, _):
            for n in range(unroll):
                t = i * unroll + n
                step(t, jnp.minimum(t + 1, tiles - 1))
            return 0

        lax.fori_loop(0, lax.div(tiles, unroll), body, 0)

    def span_only(t, _):
        scores = span_scores(load_queries(t), t)
        shift = shift_of(scores)
        weights = jnp.exp2(scores * LOG2_SCALE - shift)
        acc = jnp.dot(weights.astype(BF16), vs_pad[...], preferred_element_type=F32)
        finish(t, shift, weights, acc)
        return 0

    lax.fori_loop(tiles, blocks * steps, span_only, 0)


def attend_head(info, q_pieces, chosen, q_head, keys_t, values, span_keys, span_values, head, after):
    blocks, rows, _ = q_pieces[0].shape
    plane, count = len(q_pieces), len(chosen)
    cols = GROUP_QUERIES * HEAD_SIZE
    key_count = values.shape[0]
    group_step = min(GROUP_QUERIES, 2 * (plane // count))
    tile_rows = group_step * count * rows
    key_chunk = min(key_count, 256 if tile_rows % 256 == 0 else 512)
    vmem = pltpu.MemorySpace.VMEM
    span_block = pl.BlockSpec((rows, HEAD_SIZE), lambda i, s: (0, head))
    scored = blocks * count * rows * GROUP_QUERIES * key_count
    return pl.pallas_call(
        functools.partial(
            attend_kernel,
            chosen=chosen,
            blocks=blocks,
            plane=plane,
            rows=rows,
            group_step=group_step,
            key_chunk=key_chunk,
            waits=len(after),
        ),
        grid_spec=pltpu.PrefetchScalarGridSpec(
            num_scalar_prefetch=1,
            grid=(1,),
            in_specs=[pl.BlockSpec((blocks, rows, cols), lambda i, s: (0, 0, q_head))] * count
            + [
                pl.BlockSpec((HEAD_SIZE, key_count), lambda i, s: (head, 0)),
                pl.BlockSpec((key_count, HEAD_SIZE), lambda i, s: (0, head)),
                span_block,
                span_block,
            ]
            + [pl.BlockSpec(memory_space=pl.ANY)] * len(after),
            out_specs=[pl.BlockSpec((blocks, rows, cols + LANES), lambda i, s: (0, 0, 0))] * count,
            scratch_shapes=[vmem((tile_rows, key_chunk), BF16)] * 2
            + [
                vmem((tile_rows, key_count + LANES), F32),
                vmem((tile_rows, LANES), F32),
                vmem((count * rows, LANES), F32),
                vmem((tile_rows, LANES), jnp.int32),
                vmem((LANES, HEAD_SIZE), BF16),
                vmem((LANES, HEAD_SIZE), BF16),
            ],
        ),
        out_shape=[jax.ShapeDtypeStruct((blocks, rows, cols + LANES), BF16)] * count,
        compiler_params=pltpu.CompilerParams(vmem_limit_bytes=ATTEND_VMEM),
        cost_estimate=pl.CostEstimate(
            flops=8 * scored * HEAD_SIZE,
            bytes_accessed=4 * key_count * HEAD_SIZE + 4 * blocks * count * rows * cols,
            transcendentals=scored,
        ),
        name="attend",
    )(info, *[q_pieces[b] for b in chosen], keys_t, values, span_keys, span_values, *after)


def transpose_kernel(x_ref, *refs):
    refs[-1][...] = x_ref[...].T


def transpose_keys(keys, after):
    count, cols = keys.shape
    chunk = min(count, 1024)
    return pl.pallas_call(
        transpose_kernel,
        grid=(count // chunk,),
        in_specs=[pl.BlockSpec((chunk, cols), lambda i: (i, 0))] + [pl.BlockSpec(memory_space=pl.ANY)] * len(after),
        out_specs=pl.BlockSpec((cols, chunk), lambda i: (0, i)),
        out_shape=jax.ShapeDtypeStruct((cols, count), keys.dtype),
        compiler_params=pltpu.CompilerParams(vmem_limit_bytes=SHORT_VMEM),
        cost_estimate=pl.CostEstimate(flops=0, bytes_accessed=4 * keys.size, transcendentals=0),
        name="transpose",
    )(keys, *after)


def combine(parts):
    width = GROUP_QUERIES * HEAD_SIZE
    aux = [p[:, width:].astype(F32) for p in parts]
    top = functools.reduce(jnp.maximum, aux)
    factors = [jnp.exp2(jnp.minimum(a - top, 0.0)) for a in aux]
    sums = [
        pltpu.roll(a, LANES - GROUP_QUERIES, 1) + pltpu.roll(a, LANES - 2 * GROUP_QUERIES, 1) for a in aux
    ]
    total = sum(f * s for f, s in zip(factors, sums))
    heads = []
    for g in range(GROUP_QUERIES):
        cols = slice(g * HEAD_SIZE, (g + 1) * HEAD_SIZE)
        heads.append(sum(f[:, g : g + 1] * p[:, cols].astype(F32) for f, p in zip(factors, parts)))
    return heads, top, total


def merge_kernel(*refs, heads, plane, waits):
    ins, outs = refs[: heads * plane], refs[heads * plane + waits :]
    width = GROUP_QUERIES * HEAD_SIZE
    for h in range(heads):
        first = h * (width + LANES)
        for a, out in enumerate(outs):
            parts, top, total = combine([p[a] for p in ins[h * plane : (h + 1) * plane]])
            for g, x in enumerate(parts):
                out[:, first + g * HEAD_SIZE : first + (g + 1) * HEAD_SIZE] = x.astype(BF16)
            lane = lax.broadcasted_iota(jnp.int32, top.shape, 1)
            high = total.astype(BF16).astype(F32)
            aux = jnp.where(
                lane < GROUP_QUERIES,
                top,
                jnp.where(
                    lane < 2 * GROUP_QUERIES,
                    pltpu.roll(high, GROUP_QUERIES, 1),
                    pltpu.roll(total - high, 2 * GROUP_QUERIES, 1),
                ),
            )
            aux = jnp.where(lane < 3 * GROUP_QUERIES, aux, 0.0)
            out[:, first + width : first + width + LANES] = aux.astype(BF16)


def normalize_kernel(*refs, heads, count):
    ins, out = refs[:count], refs[-1]
    width = GROUP_QUERIES * HEAD_SIZE
    for h in range(heads):
        first = h * (width + LANES)
        parts, _, total = combine([p[:, first : first + width + LANES] for p in ins])
        for g, x in enumerate(parts):
            start = h * width + g * HEAD_SIZE
            out[:, start : start + HEAD_SIZE] = (x / total[:, g : g + 1]).astype(BF16)


def waiting_specs(count, waits):
    whole = pl.BlockSpec(memory_space=pltpu.MemorySpace.VMEM)
    return [whole] * count + [pl.BlockSpec(memory_space=pl.ANY)] * waits


def merge_pieces(pieces, after):
    heads, plane = len(pieces), len(pieces[0])
    blocks, rows, cols = pieces[0][0].shape
    return pl.pallas_call(
        functools.partial(merge_kernel, heads=heads, plane=plane, waits=len(after)),
        in_specs=waiting_specs(heads * plane, len(after)),
        out_shape=[jax.ShapeDtypeStruct((rows, heads * cols), BF16)] * blocks,
        compiler_params=pltpu.CompilerParams(vmem_limit_bytes=SHORT_VMEM),
        cost_estimate=SHORT,
        name="merge",
    )(*[p for own in pieces for p in own], *after)


def normalize_pieces(pieces, after):
    rows, cols = pieces[0].shape
    heads = cols // (GROUP_QUERIES * HEAD_SIZE + LANES)
    return pl.pallas_call(
        functools.partial(normalize_kernel, heads=heads, count=len(pieces)),
        in_specs=waiting_specs(len(pieces), len(after)),
        out_shape=jax.ShapeDtypeStruct((rows, cols - heads * LANES), BF16),
        compiler_params=pltpu.CompilerParams(vmem_limit_bytes=SHORT_VMEM),
        cost_estimate=SHORT,
        name="normalize",
    )(*pieces, *after)


def project_kernel(info, *refs, order, chosen, rows, width):
    ins, (w_ref, *base_ref, out) = refs[: len(chosen)], refs[len(chosen) :]
    out[...] = base_ref[0][...].astype(out.dtype) if base_ref else jnp.zeros_like(out)
    for x_ref, b in zip(ins, chosen):
        x = x_ref[...].reshape(len(order) * rows, width)
        y = jnp.dot(x, w_ref[...], preferred_element_type=F32)
        for n, a in enumerate(order):
            at = (info[3 + len(order) + a], b ^ info[1])
            part = y[n * rows : (n + 1) * rows]
            out[at] = ((base_ref[0][at] + part) if base_ref else part).astype(out.dtype)


def project(info, pieces, order, chosen, weight, group, base, dtype):
    plane = len(pieces)
    blocks, rows, width = pieces[0].shape
    out_cols = weight.shape[1]
    span = len(chosen) * blocks * rows
    whole = pl.BlockSpec((blocks, rows, width), lambda i, s: (0, 0, 0))
    out_block = pl.BlockSpec((blocks, plane, rows, out_cols), lambda i, s: (0, 0, 0, 0))
    return pl.pallas_call(
        functools.partial(project_kernel, order=order, chosen=chosen, rows=rows, width=width),
        grid_spec=pltpu.PrefetchScalarGridSpec(
            num_scalar_prefetch=1,
            grid=(1,),
            in_specs=[whole] * len(chosen)
            + [pl.BlockSpec((width, out_cols), lambda i, s: (group, 0))]
            + [out_block] * len(base),
            out_specs=out_block,
        ),
        out_shape=jax.ShapeDtypeStruct((blocks, plane, rows, out_cols), dtype),
        compiler_params=pltpu.CompilerParams(vmem_limit_bytes=SHORT_VMEM),
        cost_estimate=pl.CostEstimate(
            flops=2 * span * width * out_cols,
            bytes_accessed=2 * (width * out_cols + span * width),
            transcendentals=0,
        ),
        name="project",
    )(info, *[pieces[b] for b in chosen], weight, *base)


def exchange(x, axis, distance):
    count = lax.axis_size(axis)
    return lax.ppermute(x, axis, [(i, i ^ distance) for i in range(count)])


def local(queries, span_keys, span_values, context_keys, context_values, selected, out_weight):
    ctx_count, me = lax.axis_size("ctx"), lax.axis_index("ctx")
    head_count, my_head = lax.axis_size("head"), lax.axis_index("head")
    blocks = selected.shape[0]
    plane = ctx_count // blocks
    rows = queries.shape[0]
    heads = context_keys.shape[1] // HEAD_SIZE
    width = GROUP_QUERIES * HEAD_SIZE

    slot_block = lax.div(me, plane) ^ jnp.arange(blocks, dtype=jnp.int32)
    wanted = jnp.any(selected == me, axis=1)[slot_block]
    order = jnp.argsort(jnp.logical_not(wanted), stable=True).astype(jnp.int32)
    info = jnp.concatenate(
        [
            jnp.stack([me, lax.rem(me, plane), jnp.sum(wanted)]).astype(jnp.int32),
            order,
            slot_block.astype(jnp.int32),
        ]
    )

    def doubled(column):
        stack, order, distance = column
        if not distance:
            return column
        stack = jnp.concatenate([stack, exchange(stack, "ctx", distance * plane)])
        return stack, order + [a ^ distance for a in order], distance // 2

    def stack_blocks(x):
        return jnp.stack([x] + [exchange(x, "ctx", a * plane) for a in range(1, blocks)])

    def gather_plane(stack):
        return [stack] + [exchange(stack, "ctx", b) for b in range(1, plane)]

    first = stack_blocks(queries[:, :width])
    sources, stacks = [(gather_plane(first), 0)], []
    if heads > 1:
        held, _ = lax.optimization_barrier((queries[:, width:], first))
        early = [exchange(held, "ctx", a * plane) for a in range(1, blocks)]
        keys_t = transpose_keys(context_keys, early[:1])
        held, _ = lax.optimization_barrier((held, keys_t))
        stacks = [jnp.stack([held] + early)]
        pieces = gather_plane(stacks[0])
        sources += [(pieces, i) for i in range(heads - 1)]
    else:
        keys_t = transpose_keys(context_keys, [])

    size = 2 if heads % 2 == 0 else 1
    attended, merged, rows_of = [], [], []

    received = {}

    def receive(h):
        if h not in received:
            received[h] = [exchange(x, "ctx", b) for b, x in zip(range(1, plane), attended[h][1 - plane :])]
        return received[h]

    def merge(after):
        group = range(len(merged) * size, (len(merged) + 1) * size)
        parts = [[attended[h][0]] + receive(h) for h in group]
        merged.append(merge_pieces(parts, after))
        return [merged[-1][0]]

    def normalize(after):
        own = merged[len(rows_of)]
        parts = [own[0]] + [exchange(own[a], "ctx", a * plane) for a in range(1, blocks)]
        rows_of.append(normalize_pieces(parts, after))
        return [rows_of[-1]]

    def attend(h, chosen, after):
        pieces, q_head = sources[h]
        return attend_head(
            info, pieces, chosen, q_head, keys_t, context_values, span_keys, span_values, h, after
        )

    latest = stacks
    for h in range(heads):
        start = 1 if h == heads - 1 else 0
        attended.append(attend(h, range(start, plane), latest))
        latest = [attended[h][0]]
        if len(rows_of) < len(merged):
            latest = normalize(latest)
        if start:
            before = receive(h - 1) if h else []
            attended[h] = attend(h, [0], latest + before) + attended[h]
            latest = [attended[h][0]]
        if h >= (len(merged) + 1) * size:
            latest = merge(latest)
    columns = []

    def gather_round():
        columns.extend((x[None], [0], blocks // 2) for x in rows_of[len(columns) :])
        if len(merged) == heads // size and columns:
            held, *_ = lax.optimization_barrier(
                ([column[0] for column in columns], attended[-1][0], receive(heads - 1))
            )
            columns[:] = [(x, *column[1:]) for x, column in zip(held, columns)]
        columns[:] = [doubled(column) for column in columns]
        return [column[0] for column in columns]

    while len(merged) < heads // size:
        latest = merge(latest + gather_round())
    gathered = []
    while len(rows_of) < heads // size:
        after = gather_round()
        if columns and not columns[0][2]:
            gathered = [gather_plane(after[0])]
            after = [gathered[0][b] for b in (1, 2) if b < plane]
        latest = normalize(latest + after)
    while any(distance for _, _, distance in columns) or len(columns) < len(rows_of):
        gather_round()

    total = []
    for g, (stack, order, _) in enumerate(columns):
        if g:
            stack, _ = lax.optimization_barrier((stack, pieces))
        pieces = gathered.pop() if gathered else gather_plane(stack)
        if g < len(rows_of) - 1:
            total = [project(info, pieces, order, range(plane), out_weight, g, total, F32)]
        else:
            total = [project(info, pieces, order, range(plane // 2), out_weight, g, total, F32)]
            total = [project(info, pieces, order, range(plane // 2, plane), out_weight, g, total, BF16)]
    partial_out = total[0].reshape(ctx_count * rows, -1)
    share = partial_out.shape[0] // head_count
    total = lax.dynamic_slice_in_dim(partial_out, my_head * share, share, 0).astype(F32)
    for d in range(1, head_count):
        other = lax.dynamic_slice_in_dim(partial_out, (my_head ^ d) * share, share, 0)
        total = total + exchange(other, "head", d).astype(F32)
    return total.astype(BF16)


def solution(mesh):
    return jax.shard_map(
        local,
        mesh=mesh,
        in_specs=(
            P("ctx", "head"),
            P("ctx", "head"),
            P("ctx", "head"),
            P("ctx", "head"),
            P("ctx", "head"),
            P(),
            P("head", "ctx"),
        ),
        out_specs=P("head", "ctx"),
        check_vma=False,
    )
```

```python
import functools
import math

import jax
import jax.numpy as jnp
import numpy as np
from jax import lax
from jax.experimental import pallas as pl
from jax.experimental.pallas import tpu as pltpu
from jax.sharding import PartitionSpec as P

HEAD_SIZE = 128
GROUP_QUERIES = 8
LANES = 128
LOG2_SCALE = float(HEAD_SIZE**-0.5 * np.log2(np.e))
MASKED = -1e30
LOWEST = -1e20
ATTEND_VMEM = 28 * 1024 * 1024
SHORT_VMEM = 16 * 1024 * 1024

BF16, F32 = jnp.bfloat16, jnp.float32
SHORT = pl.CostEstimate(flops=0, bytes_accessed=0, transcendentals=0)


def fold_lanes(op, x):
    parts = [x[:, i : i + LANES] for i in range(0, x.shape[1], LANES)]
    while len(parts) > 1:
        parts = [op(*parts[i : i + 2]) if i + 1 < len(parts) else parts[i] for i in range(0, len(parts), 2)]
    return parts[0]


def attend_kernel(info, *refs, chosen, blocks, plane, rows, group_step, key_chunk, waits):
    count = len(chosen)
    q_refs, refs = refs[:count], refs[count:]
    kt_ref, v_ref, ks_ref, vs_ref = refs[:4]
    refs = refs[4 + waits :]
    o_refs, refs = refs[:count], refs[count:]
    weight_refs, refs = refs[:2], refs[2:]
    score_ref, shift_ref, aux_ref, pos_ref, ks_pad, vs_pad = refs
    me, my_plane, wanted = info[0], info[1], info[2]
    keys = v_ref.shape[0]
    block_rows = count * rows
    tile_rows = group_step * block_rows
    steps = GROUP_QUERIES // group_step
    chunks = keys // key_chunk
    strip = math.gcd(tile_rows, 64)

    ks_pad[...] = jnp.zeros_like(ks_pad)
    vs_pad[...] = jnp.zeros_like(vs_pad)
    ks_pad[0:rows, :] = ks_ref[...]
    vs_pad[0:rows, :] = vs_ref[...]
    row = lax.broadcasted_iota(jnp.int32, (rows, LANES), 0)
    col = lax.broadcasted_iota(jnp.int32, (rows, LANES), 1)
    for i in range(group_step):
        for n, b in enumerate(chosen):
            start = (i * count + n) * rows
            base = ((b ^ my_plane) - me) * rows
            pos_ref[start : start + rows] = jnp.where(col < rows, row - col + base, -(1 << 30))
    lane = lax.broadcasted_iota(jnp.int32, (block_rows, LANES), 1)

    def place(tile):
        return info[3 + lax.div(tile, steps)], lax.rem(tile, steps) * group_step

    def load_queries(tile):
        slot, group = place(tile)
        parts = []
        for i in range(group_step):
            cols = pl.ds(pl.multiple_of((group + i) * HEAD_SIZE, HEAD_SIZE), HEAD_SIZE)
            parts += [q[slot, :, cols] for q in q_refs]
        return jnp.concatenate(parts, axis=0)

    def span_scores(q, tile):
        slot, _ = place(tile)
        start = info[3 + blocks + slot] * (plane * rows)
        scores = lax.dot_general(q, ks_pad[...], (((1,), (1,)), ((), ())), preferred_element_type=F32)
        return jnp.where(pos_ref[...] + start >= 0, scores, MASKED)

    def shift_of(peak):
        top = jnp.max(peak, axis=1, keepdims=True) * LOG2_SCALE
        return jnp.broadcast_to(jnp.maximum(top, LOWEST).astype(BF16).astype(F32), (tile_rows, LANES))

    def finish(tile, shift, total, acc):
        slot, group = place(tile)
        total = jnp.sum(total, axis=1, keepdims=True)
        high = total.astype(BF16).astype(F32)
        low = total - high
        aux = jnp.where(group == 0, 0.0, aux_ref[...])
        for i in range(group_step):
            cols = pl.ds(pl.multiple_of((group + i) * HEAD_SIZE, HEAD_SIZE), HEAD_SIZE)
            part = slice(i * block_rows, (i + 1) * block_rows)
            aux = jnp.where(lane == group + i, shift[part], aux)
            aux = jnp.where(lane == group + i + GROUP_QUERIES, high[part], aux)
            aux = jnp.where(lane == group + i + 2 * GROUP_QUERIES, low[part], aux)
            for b, o in enumerate(o_refs):
                start = i * block_rows + b * rows
                o[slot, :, cols] = acc[start : start + rows].astype(BF16)
        aux_ref[...] = aux
        for b, o in enumerate(o_refs):
            o[slot, :, GROUP_QUERIES * HEAD_SIZE :] = aux[b * rows : (b + 1) * rows].astype(BF16)

    def score_chunk(q, peak, j):
        part = slice(j * key_chunk, (j + 1) * key_chunk)
        scores = jnp.dot(q, kt_ref[:, part], preferred_element_type=F32)
        score_ref[:, part] = scores
        return jnp.maximum(peak, fold_lanes(jnp.maximum, scores))

    def weigh_chunk(totals, j):
        weight_ref = weight_refs[j % 2]
        for n, r in enumerate(range(0, tile_rows, strip)):
            part = slice(r, r + strip)
            shift = shift_ref[part]
            for c in range(0, key_chunk, LANES):
                start = j * key_chunk + c
                weights = jnp.exp2(score_ref[part, start : start + LANES] * LOG2_SCALE - shift)
                totals[n] = totals[n] + weights
                weight_ref[part, c : c + LANES] = weights.astype(BF16)

    def apply_chunk(acc, j):
        values = v_ref[j * key_chunk : (j + 1) * key_chunk]
        return acc + jnp.dot(weight_refs[j % 2][...], values, preferred_element_type=F32)

    def step(now, later):
        weights = jnp.exp2(score_ref[:, keys:] * LOG2_SCALE - shift_ref[...])
        acc = jnp.dot(weights.astype(BF16), vs_pad[...], preferred_element_type=F32)
        totals = [weights[r : r + strip] for r in range(0, tile_rows, strip)]
        q = load_queries(later)
        peak = span_scores(q, later)
        score_ref[:, keys:] = peak
        for j in range(chunks):
            weigh_chunk(totals, j)
            peak = score_chunk(q, peak, j)
            if j > 0:
                acc = apply_chunk(acc, j - 1)
        acc = apply_chunk(acc, chunks - 1)
        finish(now, shift_ref[...], jnp.concatenate(totals, axis=0), acc)
        shift_ref[...] = shift_of(peak)

    tiles = wanted * steps

    @pl.when(tiles > 0)
    def _():
        q = load_queries(jnp.int32(0))
        peak = span_scores(q, jnp.int32(0))
        score_ref[:, keys:] = peak
        for j in range(chunks):
            peak = score_chunk(q, peak, j)
        shift_ref[...] = shift_of(peak)

        def body(t, _):
            step(t, jnp.minimum(t + 1, tiles - 1))
            return 0

        lax.fori_loop(0, tiles, body, 0)

    def span_only(t, _):
        scores = span_scores(load_queries(t), t)
        shift = shift_of(scores)
        weights = jnp.exp2(scores * LOG2_SCALE - shift)
        acc = jnp.dot(weights.astype(BF16), vs_pad[...], preferred_element_type=F32)
        finish(t, shift, weights, acc)
        return 0

    lax.fori_loop(tiles, blocks * steps, span_only, 0)


def attend_head(info, q_pieces, chosen, q_head, keys_t, values, span_keys, span_values, head, after):
    blocks, rows, _ = q_pieces[0].shape
    plane, count = len(q_pieces), len(chosen)
    cols = GROUP_QUERIES * HEAD_SIZE
    key_count = values.shape[0]
    group_step = min(GROUP_QUERIES, 2 * (plane // count))
    tile_rows = group_step * count * rows
    key_chunk = min(key_count, 256 if tile_rows % 256 == 0 else 512)
    vmem = pltpu.MemorySpace.VMEM
    span_block = pl.BlockSpec((rows, HEAD_SIZE), lambda i, s: (0, head))
    scored = blocks * count * rows * GROUP_QUERIES * key_count
    return pl.pallas_call(
        functools.partial(
            attend_kernel,
            chosen=chosen,
            blocks=blocks,
            plane=plane,
            rows=rows,
            group_step=group_step,
            key_chunk=key_chunk,
            waits=len(after),
        ),
        grid_spec=pltpu.PrefetchScalarGridSpec(
            num_scalar_prefetch=1,
            grid=(1,),
            in_specs=[pl.BlockSpec((blocks, rows, cols), lambda i, s: (0, 0, q_head))] * count
            + [
                pl.BlockSpec((HEAD_SIZE, key_count), lambda i, s: (head, 0)),
                pl.BlockSpec((key_count, HEAD_SIZE), lambda i, s: (0, head)),
                span_block,
                span_block,
            ]
            + [pl.BlockSpec(memory_space=pl.ANY)] * len(after),
            out_specs=[pl.BlockSpec((blocks, rows, cols + LANES), lambda i, s: (0, 0, 0))] * count,
            scratch_shapes=[vmem((tile_rows, key_chunk), BF16)] * 2
            + [
                vmem((tile_rows, key_count + LANES), F32),
                vmem((tile_rows, LANES), F32),
                vmem((count * rows, LANES), F32),
                vmem((tile_rows, LANES), jnp.int32),
                vmem((LANES, HEAD_SIZE), BF16),
                vmem((LANES, HEAD_SIZE), BF16),
            ],
        ),
        out_shape=[jax.ShapeDtypeStruct((blocks, rows, cols + LANES), BF16)] * count,
        compiler_params=pltpu.CompilerParams(vmem_limit_bytes=ATTEND_VMEM),
        cost_estimate=pl.CostEstimate(
            flops=8 * scored * HEAD_SIZE,
            bytes_accessed=4 * key_count * HEAD_SIZE + 4 * blocks * count * rows * cols,
            transcendentals=scored,
        ),
        name="attend",
    )(info, *[q_pieces[b] for b in chosen], keys_t, values, span_keys, span_values, *after)


def transpose_kernel(x_ref, *refs):
    refs[-1][...] = x_ref[...].T


def transpose_keys(keys, after):
    count, cols = keys.shape
    chunk = min(count, 1024)
    return pl.pallas_call(
        transpose_kernel,
        grid=(count // chunk,),
        in_specs=[pl.BlockSpec((chunk, cols), lambda i: (i, 0))] + [pl.BlockSpec(memory_space=pl.ANY)] * len(after),
        out_specs=pl.BlockSpec((cols, chunk), lambda i: (0, i)),
        out_shape=jax.ShapeDtypeStruct((cols, count), keys.dtype),
        compiler_params=pltpu.CompilerParams(vmem_limit_bytes=SHORT_VMEM),
        cost_estimate=pl.CostEstimate(flops=0, bytes_accessed=4 * keys.size, transcendentals=0),
        name="transpose",
    )(keys, *after)


def combine(parts):
    width = GROUP_QUERIES * HEAD_SIZE
    aux = [p[:, width:].astype(F32) for p in parts]
    top = functools.reduce(jnp.maximum, aux)
    factors = [jnp.exp2(jnp.minimum(a - top, 0.0)) for a in aux]
    sums = [
        pltpu.roll(a, LANES - GROUP_QUERIES, 1) + pltpu.roll(a, LANES - 2 * GROUP_QUERIES, 1) for a in aux
    ]
    total = sum(f * s for f, s in zip(factors, sums))
    heads = []
    for g in range(GROUP_QUERIES):
        cols = slice(g * HEAD_SIZE, (g + 1) * HEAD_SIZE)
        heads.append(sum(f[:, g : g + 1] * p[:, cols].astype(F32) for f, p in zip(factors, parts)))
    return heads, top, total


def merge_kernel(*refs, heads, plane, waits):
    ins, outs = refs[: heads * plane], refs[heads * plane + waits :]
    width = GROUP_QUERIES * HEAD_SIZE
    for h in range(heads):
        first = h * (width + LANES)
        for a, out in enumerate(outs):
            parts, top, total = combine([p[a] for p in ins[h * plane : (h + 1) * plane]])
            for g, x in enumerate(parts):
                out[:, first + g * HEAD_SIZE : first + (g + 1) * HEAD_SIZE] = x.astype(BF16)
            lane = lax.broadcasted_iota(jnp.int32, top.shape, 1)
            high = total.astype(BF16).astype(F32)
            aux = jnp.where(
                lane < GROUP_QUERIES,
                top,
                jnp.where(
                    lane < 2 * GROUP_QUERIES,
                    pltpu.roll(high, GROUP_QUERIES, 1),
                    pltpu.roll(total - high, 2 * GROUP_QUERIES, 1),
                ),
            )
            aux = jnp.where(lane < 3 * GROUP_QUERIES, aux, 0.0)
            out[:, first + width : first + width + LANES] = aux.astype(BF16)


def normalize_kernel(*refs, heads, count):
    ins, out = refs[:count], refs[-1]
    width = GROUP_QUERIES * HEAD_SIZE
    for h in range(heads):
        first = h * (width + LANES)
        parts, _, total = combine([p[:, first : first + width + LANES] for p in ins])
        for g, x in enumerate(parts):
            start = h * width + g * HEAD_SIZE
            out[:, start : start + HEAD_SIZE] = (x / total[:, g : g + 1]).astype(BF16)


def waiting_specs(count, waits):
    whole = pl.BlockSpec(memory_space=pltpu.MemorySpace.VMEM)
    return [whole] * count + [pl.BlockSpec(memory_space=pl.ANY)] * waits


def merge_pieces(pieces, after):
    heads, plane = len(pieces), len(pieces[0])
    blocks, rows, cols = pieces[0][0].shape
    return pl.pallas_call(
        functools.partial(merge_kernel, heads=heads, plane=plane, waits=len(after)),
        in_specs=waiting_specs(heads * plane, len(after)),
        out_shape=[jax.ShapeDtypeStruct((rows, heads * cols), BF16)] * blocks,
        compiler_params=pltpu.CompilerParams(vmem_limit_bytes=SHORT_VMEM),
        cost_estimate=SHORT,
        name="merge",
    )(*[p for own in pieces for p in own], *after)


def normalize_pieces(pieces, after):
    rows, cols = pieces[0].shape
    heads = cols // (GROUP_QUERIES * HEAD_SIZE + LANES)
    return pl.pallas_call(
        functools.partial(normalize_kernel, heads=heads, count=len(pieces)),
        in_specs=waiting_specs(len(pieces), len(after)),
        out_shape=jax.ShapeDtypeStruct((rows, cols - heads * LANES), BF16),
        compiler_params=pltpu.CompilerParams(vmem_limit_bytes=SHORT_VMEM),
        cost_estimate=SHORT,
        name="normalize",
    )(*pieces, *after)


def project_kernel(info, *refs, order, chosen, rows, width):
    ins, (w_ref, *base_ref, out) = refs[: len(chosen)], refs[len(chosen) :]
    out[...] = base_ref[0][...].astype(out.dtype) if base_ref else jnp.zeros_like(out)
    for x_ref, b in zip(ins, chosen):
        x = x_ref[...].reshape(len(order) * rows, width)
        y = jnp.dot(x, w_ref[...], preferred_element_type=F32)
        for n, a in enumerate(order):
            at = (info[3 + len(order) + a], b ^ info[1])
            part = y[n * rows : (n + 1) * rows]
            out[at] = ((base_ref[0][at] + part) if base_ref else part).astype(out.dtype)


def project(info, pieces, order, chosen, weight, group, base, dtype):
    plane = len(pieces)
    blocks, rows, width = pieces[0].shape
    out_cols = weight.shape[1]
    span = len(chosen) * blocks * rows
    whole = pl.BlockSpec((blocks, rows, width), lambda i, s: (0, 0, 0))
    out_block = pl.BlockSpec((blocks, plane, rows, out_cols), lambda i, s: (0, 0, 0, 0))
    return pl.pallas_call(
        functools.partial(project_kernel, order=order, chosen=chosen, rows=rows, width=width),
        grid_spec=pltpu.PrefetchScalarGridSpec(
            num_scalar_prefetch=1,
            grid=(1,),
            in_specs=[whole] * len(chosen)
            + [pl.BlockSpec((width, out_cols), lambda i, s: (group, 0))]
            + [out_block] * len(base),
            out_specs=out_block,
        ),
        out_shape=jax.ShapeDtypeStruct((blocks, plane, rows, out_cols), dtype),
        compiler_params=pltpu.CompilerParams(vmem_limit_bytes=SHORT_VMEM),
        cost_estimate=pl.CostEstimate(
            flops=2 * span * width * out_cols,
            bytes_accessed=2 * (width * out_cols + span * width),
            transcendentals=0,
        ),
        name="project",
    )(info, *[pieces[b] for b in chosen], weight, *base)


def exchange(x, axis, distance):
    count = lax.axis_size(axis)
    return lax.ppermute(x, axis, [(i, i ^ distance) for i in range(count)])


def local(queries, span_keys, span_values, context_keys, context_values, selected, out_weight):
    ctx_count, me = lax.axis_size("ctx"), lax.axis_index("ctx")
    head_count, my_head = lax.axis_size("head"), lax.axis_index("head")
    blocks = selected.shape[0]
    plane = ctx_count // blocks
    rows = queries.shape[0]
    heads = context_keys.shape[1] // HEAD_SIZE
    width = GROUP_QUERIES * HEAD_SIZE

    slot_block = lax.div(me, plane) ^ jnp.arange(blocks, dtype=jnp.int32)
    wanted = jnp.any(selected == me, axis=1)[slot_block]
    order = jnp.argsort(jnp.logical_not(wanted), stable=True).astype(jnp.int32)
    info = jnp.concatenate(
        [
            jnp.stack([me, lax.rem(me, plane), jnp.sum(wanted)]).astype(jnp.int32),
            order,
            slot_block.astype(jnp.int32),
        ]
    )

    def doubled(column):
        stack, order, distance = column
        if not distance:
            return column
        stack = jnp.concatenate([stack, exchange(stack, "ctx", distance * plane)])
        return stack, order + [a ^ distance for a in order], distance // 2

    def stack_blocks(x):
        return jnp.stack([x] + [exchange(x, "ctx", a * plane) for a in range(1, blocks)])

    def gather_plane(stack):
        return [stack] + [exchange(stack, "ctx", b) for b in range(1, plane)]

    first = stack_blocks(queries[:, :width])
    sources, stacks = [(gather_plane(first), 0)], []
    if heads > 1:
        held, _ = lax.optimization_barrier((queries[:, width:], first))
        early = [exchange(held, "ctx", a * plane) for a in range(1, blocks)]
        keys_t = transpose_keys(context_keys, early[:1])
        held, _ = lax.optimization_barrier((held, keys_t))
        stacks = [jnp.stack([held] + early)]
        pieces = gather_plane(stacks[0])
        sources += [(pieces, i) for i in range(heads - 1)]
    else:
        keys_t = transpose_keys(context_keys, [])

    size = 2 if heads % 2 == 0 else 1
    attended, merged, rows_of = [], [], []

    received = {}

    def receive(h):
        if h not in received:
            received[h] = [exchange(x, "ctx", b) for b, x in zip(range(1, plane), attended[h][1 - plane :])]
        return received[h]

    def merge(after):
        group = range(len(merged) * size, (len(merged) + 1) * size)
        parts = [[attended[h][0]] + receive(h) for h in group]
        merged.append(merge_pieces(parts, after))
        return [merged[-1][0]]

    def normalize(after):
        own = merged[len(rows_of)]
        parts = [own[0]] + [exchange(own[a], "ctx", a * plane) for a in range(1, blocks)]
        rows_of.append(normalize_pieces(parts, after))
        return [rows_of[-1]]

    def attend(h, chosen, after):
        pieces, q_head = sources[h]
        return attend_head(
            info, pieces, chosen, q_head, keys_t, context_values, span_keys, span_values, h, after
        )

    latest = stacks
    for h in range(heads):
        start = 1 if h == heads - 1 else 0
        attended.append(attend(h, range(start, plane), latest))
        latest = [attended[h][0]]
        if len(rows_of) < len(merged):
            latest = normalize(latest)
        if start:
            before = receive(h - 1) if h else []
            attended[h] = attend(h, [0], latest + before) + attended[h]
            latest = [attended[h][0]]
        if h >= (len(merged) + 1) * size:
            latest = merge(latest)
    columns = []

    def gather_round():
        columns.extend((x[None], [0], blocks // 2) for x in rows_of[len(columns) :])
        if len(merged) == heads // size and columns:
            held, *_ = lax.optimization_barrier(
                ([column[0] for column in columns], attended[-1][0], receive(heads - 1))
            )
            columns[:] = [(x, *column[1:]) for x, column in zip(held, columns)]
        columns[:] = [doubled(column) for column in columns]
        return [column[0] for column in columns]

    while len(merged) < heads // size:
        latest = merge(latest + gather_round())
    gathered = []
    while len(rows_of) < heads // size:
        after = gather_round()
        if columns and not columns[0][2]:
            gathered = [gather_plane(after[0])]
            after = [gathered[0][b] for b in (1, 2) if b < plane]
        latest = normalize(latest + after)
    while any(distance for _, _, distance in columns) or len(columns) < len(rows_of):
        gather_round()

    total = []
    for g, (stack, order, _) in enumerate(columns):
        if g:
            stack, _ = lax.optimization_barrier((stack, pieces))
        pieces = gathered.pop() if gathered else gather_plane(stack)
        if g < len(rows_of) - 1:
            total = [project(info, pieces, order, range(plane), out_weight, g, total, F32)]
        else:
            total = [project(info, pieces, order, range(plane // 2), out_weight, g, total, F32)]
            total = [project(info, pieces, order, range(plane // 2, plane), out_weight, g, total, BF16)]
    partial_out = total[0].reshape(ctx_count * rows, -1)
    share = partial_out.shape[0] // head_count
    total = lax.dynamic_slice_in_dim(partial_out, my_head * share, share, 0).astype(F32)
    for d in range(1, head_count):
        other = lax.dynamic_slice_in_dim(partial_out, (my_head ^ d) * share, share, 0)
        total = total + exchange(other, "head", d).astype(F32)
    return total.astype(BF16)


def solution(mesh):
    return jax.shard_map(
        local,
        mesh=mesh,
        in_specs=(
            P("ctx", "head"),
            P("ctx", "head"),
            P("ctx", "head"),
            P("ctx", "head"),
            P("ctx", "head"),
            P(),
            P("head", "ctx"),
        ),
        out_specs=P("head", "ctx"),
        check_vma=False,
    )
```

```python
import functools
import math

import jax
import jax.numpy as jnp
import numpy as np
from jax import lax
from jax.experimental import pallas as pl
from jax.experimental.pallas import tpu as pltpu
from jax.sharding import PartitionSpec as P

HEAD_SIZE = 128
GROUP_QUERIES = 8
LANES = 128
LOG2_SCALE = float(HEAD_SIZE**-0.5 * np.log2(np.e))
MASKED = -1e30
LOWEST = -1e20
ATTEND_VMEM = 28 * 1024 * 1024
SHORT_VMEM = 16 * 1024 * 1024

BF16, F32 = jnp.bfloat16, jnp.float32
SHORT = pl.CostEstimate(flops=0, bytes_accessed=0, transcendentals=0)


def fold_lanes(op, x):
    parts = [x[:, i : i + LANES] for i in range(0, x.shape[1], LANES)]
    while len(parts) > 1:
        parts = [op(*parts[i : i + 2]) if i + 1 < len(parts) else parts[i] for i in range(0, len(parts), 2)]
    return parts[0]


def attend_kernel(info, *refs, chosen, blocks, plane, rows, group_step, key_chunk, waits):
    count = len(chosen)
    q_refs, refs = refs[:count], refs[count:]
    kt_ref, v_ref, ks_ref, vs_ref = refs[:4]
    refs = refs[4 + waits :]
    o_refs, refs = refs[:count], refs[count:]
    weight_refs, refs = refs[:2], refs[2:]
    score_ref, shift_ref, aux_ref, pos_ref, ks_pad, vs_pad = refs
    me, my_plane, wanted = info[0], info[1], info[2]
    keys = v_ref.shape[0]
    block_rows = count * rows
    tile_rows = group_step * block_rows
    steps = GROUP_QUERIES // group_step
    chunks = keys // key_chunk
    strip = math.gcd(tile_rows, 64)

    ks_pad[...] = jnp.zeros_like(ks_pad)
    vs_pad[...] = jnp.zeros_like(vs_pad)
    ks_pad[0:rows, :] = ks_ref[...]
    vs_pad[0:rows, :] = vs_ref[...]
    row = lax.broadcasted_iota(jnp.int32, (rows, LANES), 0)
    col = lax.broadcasted_iota(jnp.int32, (rows, LANES), 1)
    for i in range(group_step):
        for n, b in enumerate(chosen):
            start = (i * count + n) * rows
            base = ((b ^ my_plane) - me) * rows
            pos_ref[start : start + rows] = jnp.where(col < rows, row - col + base, -(1 << 30))
    lane = lax.broadcasted_iota(jnp.int32, (block_rows, LANES), 1)

    def place(tile):
        return info[3 + lax.div(tile, steps)], lax.rem(tile, steps) * group_step

    def load_queries(tile):
        slot, group = place(tile)
        parts = []
        for i in range(group_step):
            cols = pl.ds(pl.multiple_of((group + i) * HEAD_SIZE, HEAD_SIZE), HEAD_SIZE)
            parts += [q[slot, :, cols] for q in q_refs]
        return jnp.concatenate(parts, axis=0)

    def span_scores(q, tile):
        slot, _ = place(tile)
        start = info[3 + blocks + slot] * (plane * rows)
        scores = lax.dot_general(q, ks_pad[...], (((1,), (1,)), ((), ())), preferred_element_type=F32)
        return jnp.where(pos_ref[...] + start >= 0, scores, MASKED)

    def shift_of(peak):
        top = jnp.max(peak, axis=1, keepdims=True) * LOG2_SCALE
        return jnp.broadcast_to(jnp.maximum(top, LOWEST).astype(BF16).astype(F32), (tile_rows, LANES))

    def finish(tile, shift, total, acc):
        slot, group = place(tile)
        total = jnp.sum(total, axis=1, keepdims=True)
        high = total.astype(BF16).astype(F32)
        low = total - high
        aux = jnp.where(group == 0, 0.0, aux_ref[...])
        for i in range(group_step):
            cols = pl.ds(pl.multiple_of((group + i) * HEAD_SIZE, HEAD_SIZE), HEAD_SIZE)
            part = slice(i * block_rows, (i + 1) * block_rows)
            aux = jnp.where(lane == group + i, shift[part], aux)
            aux = jnp.where(lane == group + i + GROUP_QUERIES, high[part], aux)
            aux = jnp.where(lane == group + i + 2 * GROUP_QUERIES, low[part], aux)
            for b, o in enumerate(o_refs):
                start = i * block_rows + b * rows
                o[slot, :, cols] = acc[start : start + rows].astype(BF16)
        aux_ref[...] = aux
        for b, o in enumerate(o_refs):
            o[slot, :, GROUP_QUERIES * HEAD_SIZE :] = aux[b * rows : (b + 1) * rows].astype(BF16)

    def score_chunk(q, peak, j):
        part = slice(j * key_chunk, (j + 1) * key_chunk)
        scores = jnp.dot(q, kt_ref[:, part], preferred_element_type=F32)
        score_ref[:, part] = scores
        return jnp.maximum(peak, fold_lanes(jnp.maximum, scores))

    def weigh_chunk(totals, j):
        weight_ref = weight_refs[j % 2]
        for n, r in enumerate(range(0, tile_rows, strip)):
            part = slice(r, r + strip)
            shift = shift_ref[part]
            for c in range(0, key_chunk, LANES):
                start = j * key_chunk + c
                weights = jnp.exp2(score_ref[part, start : start + LANES] * LOG2_SCALE - shift)
                totals[n] = totals[n] + weights
                weight_ref[part, c : c + LANES] = weights.astype(BF16)

    def apply_chunk(acc, j):
        values = v_ref[j * key_chunk : (j + 1) * key_chunk]
        return acc + jnp.dot(weight_refs[j % 2][...], values, preferred_element_type=F32)

    def step(now, later):
        weights = jnp.exp2(score_ref[:, keys:] * LOG2_SCALE - shift_ref[...])
        acc = jnp.dot(weights.astype(BF16), vs_pad[...], preferred_element_type=F32)
        totals = [weights[r : r + strip] for r in range(0, tile_rows, strip)]
        q = load_queries(later)
        peak = span_scores(q, later)
        score_ref[:, keys:] = peak
        for j in range(chunks):
            weigh_chunk(totals, j)
            peak = score_chunk(q, peak, j)
            if j > 0:
                acc = apply_chunk(acc, j - 1)
        acc = apply_chunk(acc, chunks - 1)
        finish(now, shift_ref[...], jnp.concatenate(totals, axis=0), acc)
        shift_ref[...] = shift_of(peak)

    tiles = wanted * steps

    @pl.when(tiles > 0)
    def _():
        q = load_queries(jnp.int32(0))
        peak = span_scores(q, jnp.int32(0))
        score_ref[:, keys:] = peak
        for j in range(chunks):
            peak = score_chunk(q, peak, j)
        shift_ref[...] = shift_of(peak)

        def body(t, _):
            step(t, jnp.minimum(t + 1, tiles - 1))
            return 0

        lax.fori_loop(0, tiles, body, 0)

    def span_only(t, _):
        scores = span_scores(load_queries(t), t)
        shift = shift_of(scores)
        weights = jnp.exp2(scores * LOG2_SCALE - shift)
        acc = jnp.dot(weights.astype(BF16), vs_pad[...], preferred_element_type=F32)
        finish(t, shift, weights, acc)
        return 0

    lax.fori_loop(tiles, blocks * steps, span_only, 0)


def attend_head(info, q_pieces, chosen, q_head, keys_t, values, span_keys, span_values, head, after):
    blocks, rows, _ = q_pieces[0].shape
    plane, count = len(q_pieces), len(chosen)
    cols = GROUP_QUERIES * HEAD_SIZE
    key_count = values.shape[0]
    group_step = min(GROUP_QUERIES, 2 * (plane // count))
    tile_rows = group_step * count * rows
    key_chunk = min(key_count, 256 if tile_rows % 256 == 0 else 512)
    vmem = pltpu.MemorySpace.VMEM
    span_block = pl.BlockSpec((rows, HEAD_SIZE), lambda i, s: (0, head))
    scored = blocks * count * rows * GROUP_QUERIES * key_count
    return pl.pallas_call(
        functools.partial(
            attend_kernel,
            chosen=chosen,
            blocks=blocks,
            plane=plane,
            rows=rows,
            group_step=group_step,
            key_chunk=key_chunk,
            waits=len(after),
        ),
        grid_spec=pltpu.PrefetchScalarGridSpec(
            num_scalar_prefetch=1,
            grid=(1,),
            in_specs=[pl.BlockSpec((blocks, rows, cols), lambda i, s: (0, 0, q_head))] * count
            + [
                pl.BlockSpec((HEAD_SIZE, key_count), lambda i, s: (head, 0)),
                pl.BlockSpec((key_count, HEAD_SIZE), lambda i, s: (0, head)),
                span_block,
                span_block,
            ]
            + [pl.BlockSpec(memory_space=pl.ANY)] * len(after),
            out_specs=[pl.BlockSpec((blocks, rows, cols + LANES), lambda i, s: (0, 0, 0))] * count,
            scratch_shapes=[vmem((tile_rows, key_chunk), BF16)] * 2
            + [
                vmem((tile_rows, key_count + LANES), F32),
                vmem((tile_rows, LANES), F32),
                vmem((count * rows, LANES), F32),
                vmem((tile_rows, LANES), jnp.int32),
                vmem((LANES, HEAD_SIZE), BF16),
                vmem((LANES, HEAD_SIZE), BF16),
            ],
        ),
        out_shape=[jax.ShapeDtypeStruct((blocks, rows, cols + LANES), BF16)] * count,
        compiler_params=pltpu.CompilerParams(vmem_limit_bytes=ATTEND_VMEM),
        cost_estimate=pl.CostEstimate(
            flops=8 * scored * HEAD_SIZE,
            bytes_accessed=4 * key_count * HEAD_SIZE + 4 * blocks * count * rows * cols,
            transcendentals=scored,
        ),
        name="attend",
    )(info, *[q_pieces[b] for b in chosen], keys_t, values, span_keys, span_values, *after)


def transpose_kernel(x_ref, *refs):
    refs[-1][...] = x_ref[...].T


def transpose_keys(keys, after):
    count, cols = keys.shape
    chunk = min(count, 1024)
    return pl.pallas_call(
        transpose_kernel,
        grid=(count // chunk,),
        in_specs=[pl.BlockSpec((chunk, cols), lambda i: (i, 0))] + [pl.BlockSpec(memory_space=pl.ANY)] * len(after),
        out_specs=pl.BlockSpec((cols, chunk), lambda i: (0, i)),
        out_shape=jax.ShapeDtypeStruct((cols, count), keys.dtype),
        compiler_params=pltpu.CompilerParams(vmem_limit_bytes=SHORT_VMEM),
        cost_estimate=pl.CostEstimate(flops=0, bytes_accessed=4 * keys.size, transcendentals=0),
        name="transpose",
    )(keys, *after)


def combine(parts):
    width = GROUP_QUERIES * HEAD_SIZE
    aux = [p[:, width:].astype(F32) for p in parts]
    top = functools.reduce(jnp.maximum, aux)
    factors = [jnp.exp2(jnp.minimum(a - top, 0.0)) for a in aux]
    sums = [
        pltpu.roll(a, LANES - GROUP_QUERIES, 1) + pltpu.roll(a, LANES - 2 * GROUP_QUERIES, 1) for a in aux
    ]
    total = sum(f * s for f, s in zip(factors, sums))
    heads = []
    for g in range(GROUP_QUERIES):
        cols = slice(g * HEAD_SIZE, (g + 1) * HEAD_SIZE)
        heads.append(sum(f[:, g : g + 1] * p[:, cols].astype(F32) for f, p in zip(factors, parts)))
    return heads, top, total


def merge_kernel(*refs, heads, plane, waits):
    ins, outs = refs[: heads * plane], refs[heads * plane + waits :]
    width = GROUP_QUERIES * HEAD_SIZE
    for h in range(heads):
        first = h * (width + LANES)
        for a, out in enumerate(outs):
            parts, top, total = combine([p[a] for p in ins[h * plane : (h + 1) * plane]])
            for g, x in enumerate(parts):
                out[:, first + g * HEAD_SIZE : first + (g + 1) * HEAD_SIZE] = x.astype(BF16)
            lane = lax.broadcasted_iota(jnp.int32, top.shape, 1)
            high = total.astype(BF16).astype(F32)
            aux = jnp.where(
                lane < GROUP_QUERIES,
                top,
                jnp.where(
                    lane < 2 * GROUP_QUERIES,
                    pltpu.roll(high, GROUP_QUERIES, 1),
                    pltpu.roll(total - high, 2 * GROUP_QUERIES, 1),
                ),
            )
            aux = jnp.where(lane < 3 * GROUP_QUERIES, aux, 0.0)
            out[:, first + width : first + width + LANES] = aux.astype(BF16)


def normalize_kernel(*refs, heads, count):
    ins, out = refs[:count], refs[-1]
    width = GROUP_QUERIES * HEAD_SIZE
    for h in range(heads):
        first = h * (width + LANES)
        parts, _, total = combine([p[:, first : first + width + LANES] for p in ins])
        for g, x in enumerate(parts):
            start = h * width + g * HEAD_SIZE
            out[:, start : start + HEAD_SIZE] = (x / total[:, g : g + 1]).astype(BF16)


def waiting_specs(count, waits):
    whole = pl.BlockSpec(memory_space=pltpu.MemorySpace.VMEM)
    return [whole] * count + [pl.BlockSpec(memory_space=pl.ANY)] * waits


def merge_pieces(pieces, after):
    heads, plane = len(pieces), len(pieces[0])
    blocks, rows, cols = pieces[0][0].shape
    return pl.pallas_call(
        functools.partial(merge_kernel, heads=heads, plane=plane, waits=len(after)),
        in_specs=waiting_specs(heads * plane, len(after)),
        out_shape=[jax.ShapeDtypeStruct((rows, heads * cols), BF16)] * blocks,
        compiler_params=pltpu.CompilerParams(vmem_limit_bytes=SHORT_VMEM),
        cost_estimate=SHORT,
        name="merge",
    )(*[p for own in pieces for p in own], *after)


def normalize_pieces(pieces, after):
    rows, cols = pieces[0].shape
    heads = cols // (GROUP_QUERIES * HEAD_SIZE + LANES)
    return pl.pallas_call(
        functools.partial(normalize_kernel, heads=heads, count=len(pieces)),
        in_specs=waiting_specs(len(pieces), len(after)),
        out_shape=jax.ShapeDtypeStruct((rows, cols - heads * LANES), BF16),
        compiler_params=pltpu.CompilerParams(vmem_limit_bytes=SHORT_VMEM),
        cost_estimate=SHORT,
        name="normalize",
    )(*pieces, *after)


def project_kernel(info, *refs, order, chosen, rows, width):
    ins, (w_ref, *base_ref, out) = refs[: len(chosen)], refs[len(chosen) :]
    out[...] = base_ref[0][...].astype(out.dtype) if base_ref else jnp.zeros_like(out)
    for x_ref, b in zip(ins, chosen):
        x = x_ref[...].reshape(len(order) * rows, width)
        y = jnp.dot(x, w_ref[...], preferred_element_type=F32)
        for n, a in enumerate(order):
            at = (info[3 + len(order) + a], b ^ info[1])
            part = y[n * rows : (n + 1) * rows]
            out[at] = ((base_ref[0][at] + part) if base_ref else part).astype(out.dtype)


def project(info, pieces, order, chosen, weight, group, base, dtype):
    plane = len(pieces)
    blocks, rows, width = pieces[0].shape
    out_cols = weight.shape[1]
    span = len(chosen) * blocks * rows
    whole = pl.BlockSpec((blocks, rows, width), lambda i, s: (0, 0, 0))
    out_block = pl.BlockSpec((blocks, plane, rows, out_cols), lambda i, s: (0, 0, 0, 0))
    return pl.pallas_call(
        functools.partial(project_kernel, order=order, chosen=chosen, rows=rows, width=width),
        grid_spec=pltpu.PrefetchScalarGridSpec(
            num_scalar_prefetch=1,
            grid=(1,),
            in_specs=[whole] * len(chosen)
            + [pl.BlockSpec((width, out_cols), lambda i, s: (group, 0))]
            + [out_block] * len(base),
            out_specs=out_block,
        ),
        out_shape=jax.ShapeDtypeStruct((blocks, plane, rows, out_cols), dtype),
        compiler_params=pltpu.CompilerParams(vmem_limit_bytes=SHORT_VMEM),
        cost_estimate=pl.CostEstimate(
            flops=2 * span * width * out_cols,
            bytes_accessed=2 * (width * out_cols + span * width),
            transcendentals=0,
        ),
        name="project",
    )(info, *[pieces[b] for b in chosen], weight, *base)


def exchange(x, axis, distance):
    count = lax.axis_size(axis)
    return lax.ppermute(x, axis, [(i, i ^ distance) for i in range(count)])


def local(queries, span_keys, span_values, context_keys, context_values, selected, out_weight):
    ctx_count, me = lax.axis_size("ctx"), lax.axis_index("ctx")
    head_count, my_head = lax.axis_size("head"), lax.axis_index("head")
    blocks = selected.shape[0]
    plane = ctx_count // blocks
    rows = queries.shape[0]
    heads = context_keys.shape[1] // HEAD_SIZE
    width = GROUP_QUERIES * HEAD_SIZE

    def doubled(column):
        stack, order, distance = column
        if not distance:
            return column
        stack = jnp.concatenate([stack, exchange(stack, "ctx", distance * plane)])
        return stack, order + [a ^ distance for a in order], distance // 2

    def gather_plane(stack):
        return [stack] + [exchange(stack, "ctx", b) for b in range(1, plane)]

    own = queries[:, :width]
    near = [exchange(own, "ctx", a * plane) for a in range(1, blocks)]
    first = jnp.stack([own] + near)
    sources, stacks = [(gather_plane(first), 0)], []
    if heads > 1:
        held, _ = lax.optimization_barrier((queries[:, width:], near[0]))
        early = [exchange(held, "ctx", a * plane) for a in range(1, blocks)]
        keys_t = transpose_keys(context_keys, early[:1])
        selected, _ = lax.optimization_barrier((selected, early[0]))
    else:
        keys_t = transpose_keys(context_keys, [])

    slot_block = lax.div(me, plane) ^ jnp.arange(blocks, dtype=jnp.int32)
    wanted = jnp.any(selected == me, axis=1)[slot_block]
    order = jnp.argsort(jnp.logical_not(wanted), stable=True).astype(jnp.int32)
    info = jnp.concatenate(
        [
            jnp.stack([me, lax.rem(me, plane), jnp.sum(wanted)]).astype(jnp.int32),
            order,
            slot_block.astype(jnp.int32),
        ]
    )

    if heads > 1:
        held, *_ = lax.optimization_barrier((held, keys_t, info))
        stacks = [jnp.stack([held] + early)]
        pieces = gather_plane(stacks[0])
        sources += [(pieces, i) for i in range(heads - 1)]

    size = 2 if heads % 2 == 0 else 1
    attended, merged, rows_of = [], [], []

    received = {}

    def receive(h):
        if h not in received:
            received[h] = [exchange(x, "ctx", b) for b, x in zip(range(1, plane), attended[h][1 - plane :])]
        return received[h]

    def merge(after):
        group = range(len(merged) * size, (len(merged) + 1) * size)
        parts = [[attended[h][0]] + receive(h) for h in group]
        merged.append(merge_pieces(parts, after))
        return [merged[-1][0]]

    def normalize(after):
        own = merged[len(rows_of)]
        parts = [own[0]] + [exchange(own[a], "ctx", a * plane) for a in range(1, blocks)]
        rows_of.append(normalize_pieces(parts, after))
        return [rows_of[-1]]

    def attend(h, chosen, after):
        pieces, q_head = sources[h]
        return attend_head(
            info, pieces, chosen, q_head, keys_t, context_values, span_keys, span_values, h, after
        )

    latest = stacks
    for h in range(heads):
        start = 1 if h == heads - 1 else 0
        attended.append(attend(h, range(start, plane), latest))
        latest = [attended[h][0]]
        if len(rows_of) < len(merged):
            latest = normalize(latest)
        if start:
            before = receive(h - 1) if h else []
            attended[h] = attend(h, [0], latest + before) + attended[h]
            latest = [attended[h][0]]
        if h >= (len(merged) + 1) * size:
            latest = merge(latest)
    columns = []

    def gather_round():
        columns.extend((x[None], [0], blocks // 2) for x in rows_of[len(columns) :])
        if len(merged) == heads // size and columns:
            held, *_ = lax.optimization_barrier(
                ([column[0] for column in columns], attended[-1][0], receive(heads - 1))
            )
            columns[:] = [(x, *column[1:]) for x, column in zip(held, columns)]
        columns[:] = [doubled(column) for column in columns]
        return [column[0] for column in columns]

    while len(merged) < heads // size:
        latest = merge(latest + gather_round())
    gathered = []
    while len(rows_of) < heads // size:
        after = gather_round()
        if columns and not columns[0][2]:
            gathered = [gather_plane(after[0])]
            after = [gathered[0][b] for b in (1, 2) if b < plane]
        latest = normalize(latest + after)
    while any(distance for _, _, distance in columns) or len(columns) < len(rows_of):
        gather_round()

    total = []
    for g, (stack, order, _) in enumerate(columns):
        if g:
            stack, _ = lax.optimization_barrier((stack, pieces))
        pieces = gathered.pop() if gathered else gather_plane(stack)
        if g < len(rows_of) - 1:
            total = [project(info, pieces, order, range(plane), out_weight, g, total, F32)]
        else:
            total = [project(info, pieces, order, range(plane // 2), out_weight, g, total, F32)]
            total = [project(info, pieces, order, range(plane // 2, plane), out_weight, g, total, BF16)]
    partial_out = total[0].reshape(ctx_count * rows, -1)
    share = partial_out.shape[0] // head_count
    total = lax.dynamic_slice_in_dim(partial_out, my_head * share, share, 0).astype(F32)
    for d in range(1, head_count):
        other = lax.dynamic_slice_in_dim(partial_out, (my_head ^ d) * share, share, 0)
        total = total + exchange(other, "head", d).astype(F32)
    return total.astype(BF16)


def solution(mesh):
    return jax.shard_map(
        local,
        mesh=mesh,
        in_specs=(
            P("ctx", "head"),
            P("ctx", "head"),
            P("ctx", "head"),
            P("ctx", "head"),
            P("ctx", "head"),
            P(),
            P("head", "ctx"),
        ),
        out_specs=P("head", "ctx"),
        check_vma=False,
    )
```

```python
import functools
import math

import jax
import jax.numpy as jnp
import numpy as np
from jax import lax
from jax.experimental import pallas as pl
from jax.experimental.pallas import tpu as pltpu
from jax.sharding import PartitionSpec as P

HEAD_SIZE = 128
GROUP_QUERIES = 8
LANES = 128
LOG2_SCALE = float(HEAD_SIZE**-0.5 * np.log2(np.e))
MASKED = -1e30
LOWEST = -1e20
ATTEND_VMEM = 28 * 1024 * 1024
SHORT_VMEM = 16 * 1024 * 1024

BF16, F32 = jnp.bfloat16, jnp.float32
SHORT = pl.CostEstimate(flops=0, bytes_accessed=0, transcendentals=0)


def fold_lanes(op, x):
    parts = [x[:, i : i + LANES] for i in range(0, x.shape[1], LANES)]
    while len(parts) > 1:
        parts = [op(*parts[i : i + 2]) if i + 1 < len(parts) else parts[i] for i in range(0, len(parts), 2)]
    return parts[0]


def attend_kernel(info, *refs, chosen, blocks, plane, rows, group_step, key_chunk, waits):
    count = len(chosen)
    q_refs, refs = refs[:count], refs[count:]
    kt_ref, v_ref, ks_ref, vs_ref = refs[:4]
    refs = refs[4 + waits :]
    o_refs, refs = refs[:count], refs[count:]
    weight_refs, refs = refs[:2], refs[2:]
    score_ref, shift_ref, aux_ref, pos_ref, ks_pad, vs_pad = refs
    me, my_plane, wanted = info[0], info[1], info[2]
    keys = v_ref.shape[0]
    block_rows = count * rows
    tile_rows = group_step * block_rows
    steps = GROUP_QUERIES // group_step
    chunks = keys // key_chunk
    strip = math.gcd(tile_rows, 64)

    ks_pad[...] = jnp.zeros_like(ks_pad)
    vs_pad[...] = jnp.zeros_like(vs_pad)
    ks_pad[0:rows, :] = ks_ref[...]
    vs_pad[0:rows, :] = vs_ref[...]
    row = lax.broadcasted_iota(jnp.int32, (rows, LANES), 0)
    col = lax.broadcasted_iota(jnp.int32, (rows, LANES), 1)
    for i in range(group_step):
        for n, b in enumerate(chosen):
            start = (i * count + n) * rows
            base = ((b ^ my_plane) - me) * rows
            pos_ref[start : start + rows] = jnp.where(col < rows, row - col + base, -(1 << 30))
    lane = lax.broadcasted_iota(jnp.int32, (block_rows, LANES), 1)

    def place(tile):
        return info[3 + lax.div(tile, steps)], lax.rem(tile, steps) * group_step

    def load_queries(tile):
        slot, group = place(tile)
        parts = []
        for i in range(group_step):
            cols = pl.ds(pl.multiple_of((group + i) * HEAD_SIZE, HEAD_SIZE), HEAD_SIZE)
            parts += [q[slot, :, cols] for q in q_refs]
        return jnp.concatenate(parts, axis=0)

    def span_scores(q, tile):
        slot, _ = place(tile)
        start = info[3 + blocks + slot] * (plane * rows)
        scores = lax.dot_general(q, ks_pad[...], (((1,), (1,)), ((), ())), preferred_element_type=F32)
        return jnp.where(pos_ref[...] + start >= 0, scores, MASKED)

    def shift_of(peak):
        top = jnp.max(peak, axis=1, keepdims=True) * LOG2_SCALE
        return jnp.broadcast_to(jnp.maximum(top, LOWEST).astype(BF16).astype(F32), (tile_rows, LANES))

    def finish(tile, shift, total, acc):
        slot, group = place(tile)
        total = jnp.sum(total, axis=1, keepdims=True)
        high = total.astype(BF16).astype(F32)
        low = total - high
        aux = jnp.where(group == 0, 0.0, aux_ref[...])
        for i in range(group_step):
            cols = pl.ds(pl.multiple_of((group + i) * HEAD_SIZE, HEAD_SIZE), HEAD_SIZE)
            part = slice(i * block_rows, (i + 1) * block_rows)
            aux = jnp.where(lane == group + i, shift[part], aux)
            aux = jnp.where(lane == group + i + GROUP_QUERIES, high[part], aux)
            aux = jnp.where(lane == group + i + 2 * GROUP_QUERIES, low[part], aux)
            for b, o in enumerate(o_refs):
                start = i * block_rows + b * rows
                o[slot, :, cols] = acc[start : start + rows].astype(BF16)
        aux_ref[...] = aux
        for b, o in enumerate(o_refs):
            o[slot, :, GROUP_QUERIES * HEAD_SIZE :] = aux[b * rows : (b + 1) * rows].astype(BF16)

    def score_chunk(q, peak, j):
        part = slice(j * key_chunk, (j + 1) * key_chunk)
        scores = jnp.dot(q, kt_ref[:, part], preferred_element_type=F32)
        score_ref[:, part] = scores
        return jnp.maximum(peak, fold_lanes(jnp.maximum, scores))

    def weigh_chunk(totals, j):
        weight_ref = weight_refs[j % 2]
        for n, r in enumerate(range(0, tile_rows, strip)):
            part = slice(r, r + strip)
            shift = shift_ref[part]
            for c in range(0, key_chunk, LANES):
                start = j * key_chunk + c
                weights = jnp.exp2(score_ref[part, start : start + LANES] * LOG2_SCALE - shift)
                totals[n] = totals[n] + weights
                weight_ref[part, c : c + LANES] = weights.astype(BF16)

    def apply_chunk(acc, j):
        values = v_ref[j * key_chunk : (j + 1) * key_chunk]
        return acc + jnp.dot(weight_refs[j % 2][...], values, preferred_element_type=F32)

    def step(now, later):
        weights = jnp.exp2(score_ref[:, keys:] * LOG2_SCALE - shift_ref[...])
        acc = jnp.dot(weights.astype(BF16), vs_pad[...], preferred_element_type=F32)
        totals = [weights[r : r + strip] for r in range(0, tile_rows, strip)]
        q = load_queries(later)
        peak = span_scores(q, later)
        score_ref[:, keys:] = peak
        for j in range(chunks):
            weigh_chunk(totals, j)
            peak = score_chunk(q, peak, j)
            if j > 0:
                acc = apply_chunk(acc, j - 1)
        acc = apply_chunk(acc, chunks - 1)
        finish(now, shift_ref[...], jnp.concatenate(totals, axis=0), acc)
        shift_ref[...] = shift_of(peak)

    tiles = wanted * steps

    @pl.when(tiles > 0)
    def _():
        q = load_queries(jnp.int32(0))
        peak = span_scores(q, jnp.int32(0))
        score_ref[:, keys:] = peak
        for j in range(chunks):
            peak = score_chunk(q, peak, j)
        shift_ref[...] = shift_of(peak)

        def body(t, _):
            step(t, jnp.minimum(t + 1, tiles - 1))
            return 0

        lax.fori_loop(0, tiles, body, 0)

    def span_only(t, _):
        scores = span_scores(load_queries(t), t)
        shift = shift_of(scores)
        weights = jnp.exp2(scores * LOG2_SCALE - shift)
        acc = jnp.dot(weights.astype(BF16), vs_pad[...], preferred_element_type=F32)
        finish(t, shift, weights, acc)
        return 0

    lax.fori_loop(tiles, blocks * steps, span_only, 0)


def attend_head(info, q_pieces, chosen, q_head, keys_t, values, span_keys, span_values, head, after):
    blocks, rows, _ = q_pieces[0].shape
    plane, count = len(q_pieces), len(chosen)
    cols = GROUP_QUERIES * HEAD_SIZE
    key_count = values.shape[0]
    group_step = min(GROUP_QUERIES, 2 * (plane // count))
    tile_rows = group_step * count * rows
    key_chunk = min(key_count, 256 if tile_rows % 256 == 0 else 512)
    vmem = pltpu.MemorySpace.VMEM
    span_block = pl.BlockSpec((rows, HEAD_SIZE), lambda i, s: (0, head))
    scored = blocks * count * rows * GROUP_QUERIES * key_count
    return pl.pallas_call(
        functools.partial(
            attend_kernel,
            chosen=chosen,
            blocks=blocks,
            plane=plane,
            rows=rows,
            group_step=group_step,
            key_chunk=key_chunk,
            waits=len(after),
        ),
        grid_spec=pltpu.PrefetchScalarGridSpec(
            num_scalar_prefetch=1,
            grid=(1,),
            in_specs=[pl.BlockSpec((blocks, rows, cols), lambda i, s: (0, 0, q_head))] * count
            + [
                pl.BlockSpec((HEAD_SIZE, key_count), lambda i, s: (head, 0)),
                pl.BlockSpec((key_count, HEAD_SIZE), lambda i, s: (0, head)),
                span_block,
                span_block,
            ]
            + [pl.BlockSpec(memory_space=pl.ANY)] * len(after),
            out_specs=[pl.BlockSpec((blocks, rows, cols + LANES), lambda i, s: (0, 0, 0))] * count,
            scratch_shapes=[vmem((tile_rows, key_chunk), BF16)] * 2
            + [
                vmem((tile_rows, key_count + LANES), F32),
                vmem((tile_rows, LANES), F32),
                vmem((count * rows, LANES), F32),
                vmem((tile_rows, LANES), jnp.int32),
                vmem((LANES, HEAD_SIZE), BF16),
                vmem((LANES, HEAD_SIZE), BF16),
            ],
        ),
        out_shape=[jax.ShapeDtypeStruct((blocks, rows, cols + LANES), BF16)] * count,
        compiler_params=pltpu.CompilerParams(vmem_limit_bytes=ATTEND_VMEM),
        cost_estimate=pl.CostEstimate(
            flops=8 * scored * HEAD_SIZE,
            bytes_accessed=4 * key_count * HEAD_SIZE + 4 * blocks * count * rows * cols,
            transcendentals=scored,
        ),
        name="attend",
    )(info, *[q_pieces[b] for b in chosen], keys_t, values, span_keys, span_values, *after)


def transpose_kernel(x_ref, *refs):
    refs[-1][...] = x_ref[...].T


def transpose_keys(keys, after):
    count, cols = keys.shape
    chunk = min(count, 1024)
    return pl.pallas_call(
        transpose_kernel,
        grid=(count // chunk,),
        in_specs=[pl.BlockSpec((chunk, cols), lambda i: (i, 0))] + [pl.BlockSpec(memory_space=pl.ANY)] * len(after),
        out_specs=pl.BlockSpec((cols, chunk), lambda i: (0, i)),
        out_shape=jax.ShapeDtypeStruct((cols, count), keys.dtype),
        compiler_params=pltpu.CompilerParams(vmem_limit_bytes=SHORT_VMEM),
        cost_estimate=pl.CostEstimate(flops=0, bytes_accessed=4 * keys.size, transcendentals=0),
        name="transpose",
    )(keys, *after)


def combine(parts):
    width = GROUP_QUERIES * HEAD_SIZE
    aux = [p[:, width:].astype(F32) for p in parts]
    top = functools.reduce(jnp.maximum, aux)
    factors = [jnp.exp2(jnp.minimum(a - top, 0.0)) for a in aux]
    sums = [
        pltpu.roll(a, LANES - GROUP_QUERIES, 1) + pltpu.roll(a, LANES - 2 * GROUP_QUERIES, 1) for a in aux
    ]
    total = sum(f * s for f, s in zip(factors, sums))
    heads = []
    for g in range(GROUP_QUERIES):
        cols = slice(g * HEAD_SIZE, (g + 1) * HEAD_SIZE)
        heads.append(sum(f[:, g : g + 1] * p[:, cols].astype(F32) for f, p in zip(factors, parts)))
    return heads, top, total


def merge_kernel(*refs, heads, plane, waits):
    ins, outs = refs[: heads * plane], refs[heads * plane + waits :]
    width = GROUP_QUERIES * HEAD_SIZE
    for h in range(heads):
        first = h * (width + LANES)
        for a, out in enumerate(outs):
            parts, top, total = combine([p[a] for p in ins[h * plane : (h + 1) * plane]])
            for g, x in enumerate(parts):
                out[:, first + g * HEAD_SIZE : first + (g + 1) * HEAD_SIZE] = x.astype(BF16)
            lane = lax.broadcasted_iota(jnp.int32, top.shape, 1)
            high = total.astype(BF16).astype(F32)
            aux = jnp.where(
                lane < GROUP_QUERIES,
                top,
                jnp.where(
                    lane < 2 * GROUP_QUERIES,
                    pltpu.roll(high, GROUP_QUERIES, 1),
                    pltpu.roll(total - high, 2 * GROUP_QUERIES, 1),
                ),
            )
            aux = jnp.where(lane < 3 * GROUP_QUERIES, aux, 0.0)
            out[:, first + width : first + width + LANES] = aux.astype(BF16)


def normalize_kernel(*refs, heads, count):
    ins, out = refs[:count], refs[-1]
    width = GROUP_QUERIES * HEAD_SIZE
    for h in range(heads):
        first = h * (width + LANES)
        parts, _, total = combine([p[:, first : first + width + LANES] for p in ins])
        for g, x in enumerate(parts):
            start = h * width + g * HEAD_SIZE
            out[:, start : start + HEAD_SIZE] = (x / total[:, g : g + 1]).astype(BF16)


def waiting_specs(count, waits):
    whole = pl.BlockSpec(memory_space=pltpu.MemorySpace.VMEM)
    return [whole] * count + [pl.BlockSpec(memory_space=pl.ANY)] * waits


def merge_pieces(pieces, after):
    heads, plane = len(pieces), len(pieces[0])
    blocks, rows, cols = pieces[0][0].shape
    return pl.pallas_call(
        functools.partial(merge_kernel, heads=heads, plane=plane, waits=len(after)),
        in_specs=waiting_specs(heads * plane, len(after)),
        out_shape=[jax.ShapeDtypeStruct((rows, heads * cols), BF16)] * blocks,
        compiler_params=pltpu.CompilerParams(vmem_limit_bytes=SHORT_VMEM),
        cost_estimate=SHORT,
        name="merge",
    )(*[p for own in pieces for p in own], *after)


def normalize_pieces(pieces, after):
    rows, cols = pieces[0].shape
    heads = cols // (GROUP_QUERIES * HEAD_SIZE + LANES)
    return pl.pallas_call(
        functools.partial(normalize_kernel, heads=heads, count=len(pieces)),
        in_specs=waiting_specs(len(pieces), len(after)),
        out_shape=jax.ShapeDtypeStruct((rows, cols - heads * LANES), BF16),
        compiler_params=pltpu.CompilerParams(vmem_limit_bytes=SHORT_VMEM),
        cost_estimate=SHORT,
        name="normalize",
    )(*pieces, *after)


def project_kernel(info, *refs, order, chosen, rows, width):
    ins, (w_ref, *base_ref, out) = refs[: len(chosen)], refs[len(chosen) :]
    out[...] = base_ref[0][...].astype(out.dtype) if base_ref else jnp.zeros_like(out)
    for x_ref, b in zip(ins, chosen):
        x = x_ref[...].reshape(len(order) * rows, width)
        y = jnp.dot(x, w_ref[...], preferred_element_type=F32)
        for n, a in enumerate(order):
            at = (info[3 + len(order) + a], b ^ info[1])
            part = y[n * rows : (n + 1) * rows]
            out[at] = ((base_ref[0][at] + part) if base_ref else part).astype(out.dtype)


def project(info, pieces, order, chosen, weight, group, base, dtype):
    plane = len(pieces)
    blocks, rows, width = pieces[0].shape
    out_cols = weight.shape[1]
    span = len(chosen) * blocks * rows
    whole = pl.BlockSpec((blocks, rows, width), lambda i, s: (0, 0, 0))
    out_block = pl.BlockSpec((blocks, plane, rows, out_cols), lambda i, s: (0, 0, 0, 0))
    return pl.pallas_call(
        functools.partial(project_kernel, order=order, chosen=chosen, rows=rows, width=width),
        grid_spec=pltpu.PrefetchScalarGridSpec(
            num_scalar_prefetch=1,
            grid=(1,),
            in_specs=[whole] * len(chosen)
            + [pl.BlockSpec((width, out_cols), lambda i, s: (group, 0))]
            + [out_block] * len(base),
            out_specs=out_block,
        ),
        out_shape=jax.ShapeDtypeStruct((blocks, plane, rows, out_cols), dtype),
        compiler_params=pltpu.CompilerParams(vmem_limit_bytes=SHORT_VMEM),
        cost_estimate=pl.CostEstimate(
            flops=2 * span * width * out_cols,
            bytes_accessed=2 * (width * out_cols + span * width),
            transcendentals=0,
        ),
        name="project",
    )(info, *[pieces[b] for b in chosen], weight, *base)


def exchange(x, axis, distance):
    count = lax.axis_size(axis)
    return lax.ppermute(x, axis, [(i, i ^ distance) for i in range(count)])


def local(queries, span_keys, span_values, context_keys, context_values, selected, out_weight):
    ctx_count, me = lax.axis_size("ctx"), lax.axis_index("ctx")
    head_count, my_head = lax.axis_size("head"), lax.axis_index("head")
    blocks = selected.shape[0]
    plane = ctx_count // blocks
    rows = queries.shape[0]
    heads = context_keys.shape[1] // HEAD_SIZE
    width = GROUP_QUERIES * HEAD_SIZE

    def doubled(column):
        stack, order, distance = column
        if not distance:
            return column
        stack = jnp.concatenate([stack, exchange(stack, "ctx", distance * plane)])
        return stack, order + [a ^ distance for a in order], distance // 2

    def gather_plane(stack):
        return [stack] + [exchange(stack, "ctx", b) for b in range(1, plane)]

    own = queries[:, :width]
    near = [exchange(own, "ctx", a * plane) for a in range(1, blocks)]
    first = jnp.stack([own] + near)
    sources, stacks = [(gather_plane(first), 0)], []
    if heads > 1:
        held, _ = lax.optimization_barrier((queries[:, width:], near[0]))
        early = [exchange(held, "ctx", a * plane) for a in range(1, blocks)]
        keys_t = transpose_keys(context_keys, early[:1])
        selected, _ = lax.optimization_barrier((selected, early[0]))
    else:
        keys_t = transpose_keys(context_keys, [])

    slot_block = lax.div(me, plane) ^ jnp.arange(blocks, dtype=jnp.int32)
    wanted = jnp.any(selected == me, axis=1)[slot_block]
    order = jnp.argsort(jnp.logical_not(wanted), stable=True).astype(jnp.int32)
    info = jnp.concatenate(
        [
            jnp.stack([me, lax.rem(me, plane), jnp.sum(wanted)]).astype(jnp.int32),
            order,
            slot_block.astype(jnp.int32),
        ]
    )

    if heads > 1:
        held, *_ = lax.optimization_barrier((held, keys_t, info))
        stacks = [jnp.stack([held] + early)]
        sources.append((gather_plane(stacks[0][..., :width]), 0))
        if heads > 2:
            pieces = gather_plane(stacks[0][..., width:])
            sources += [(pieces, i) for i in range(heads - 2)]

    size = 2 if heads % 2 == 0 else 1
    attended, merged, rows_of = [], [], []

    received = {}

    def receive(h):
        if h not in received:
            received[h] = [exchange(x, "ctx", b) for b, x in zip(range(1, plane), attended[h][1 - plane :])]
        return received[h]

    def merge(after):
        group = range(len(merged) * size, (len(merged) + 1) * size)
        parts = [[attended[h][0]] + receive(h) for h in group]
        merged.append(merge_pieces(parts, after))
        return [merged[-1][0]]

    def normalize(after):
        own = merged[len(rows_of)]
        parts = [own[0]] + [exchange(own[a], "ctx", a * plane) for a in range(1, blocks)]
        rows_of.append(normalize_pieces(parts, after))
        return [rows_of[-1]]

    def attend(h, chosen, after):
        pieces, q_head = sources[h]
        return attend_head(
            info, pieces, chosen, q_head, keys_t, context_values, span_keys, span_values, h, after
        )

    latest = stacks
    for h in range(heads):
        start = 1 if h == heads - 1 else 0
        attended.append(attend(h, range(start, plane), latest))
        latest = [attended[h][0]]
        if len(rows_of) < len(merged):
            latest = normalize(latest)
        if start:
            before = receive(h - 1) if h else []
            attended[h] = attend(h, [0], latest + before) + attended[h]
            latest = [attended[h][0]]
        if h >= (len(merged) + 1) * size:
            latest = merge(latest)
    columns = []

    def gather_round():
        columns.extend((x[None], [0], blocks // 2) for x in rows_of[len(columns) :])
        if len(merged) == heads // size and columns:
            held, *_ = lax.optimization_barrier(
                ([column[0] for column in columns], attended[-1][0], receive(heads - 1))
            )
            columns[:] = [(x, *column[1:]) for x, column in zip(held, columns)]
        columns[:] = [doubled(column) for column in columns]
        return [column[0] for column in columns]

    while len(merged) < heads // size:
        latest = merge(latest + gather_round())
    gathered = []
    while len(rows_of) < heads // size:
        after = gather_round()
        if columns and not columns[0][2]:
            gathered = [gather_plane(after[0])]
            after = [gathered[0][b] for b in (1, 2) if b < plane]
        latest = normalize(latest + after)
    while any(distance for _, _, distance in columns) or len(columns) < len(rows_of):
        gather_round()

    total = []
    for g, (stack, order, _) in enumerate(columns):
        if g:
            stack, _ = lax.optimization_barrier((stack, pieces))
        pieces = gathered.pop() if gathered else gather_plane(stack)
        if g < len(rows_of) - 1:
            total = [project(info, pieces, order, range(plane), out_weight, g, total, F32)]
        else:
            total = [project(info, pieces, order, range(plane // 2), out_weight, g, total, F32)]
            total = [project(info, pieces, order, range(plane // 2, plane), out_weight, g, total, BF16)]
    partial_out = total[0].reshape(ctx_count * rows, -1)
    share = partial_out.shape[0] // head_count
    total = lax.dynamic_slice_in_dim(partial_out, my_head * share, share, 0).astype(F32)
    for d in range(1, head_count):
        other = lax.dynamic_slice_in_dim(partial_out, (my_head ^ d) * share, share, 0)
        total = total + exchange(other, "head", d).astype(F32)
    return total.astype(BF16)


def solution(mesh):
    return jax.shard_map(
        local,
        mesh=mesh,
        in_specs=(
            P("ctx", "head"),
            P("ctx", "head"),
            P("ctx", "head"),
            P("ctx", "head"),
            P("ctx", "head"),
            P(),
            P("head", "ctx"),
        ),
        out_specs=P("head", "ctx"),
        check_vma=False,
    )
```
